32 devices in a mesh: batch: 8 (over z, y), seq: 4 (over x, core).
Axes of the slice: x: 2, y: 2, z: 4, core: 2. Of those that a mesh axis runs over, the one named last changes fastest.
Arguments:
- tokens: bfloat16 [8, 512, 1280], P('batch', 'seq'), may hold values from -26 to 26
- query_key_value_weight: bfloat16 [1280, 3840], P(('batch', 'seq')), may hold values from -0.15625 to 0.15625
- attention_output_weight: bfloat16 [1280, 1280], P(('batch', 'seq')), may hold values from -1 to 1
- up_projection_weight: bfloat16 [1280, 1280], P(('batch', 'seq')), may hold values from -0.15625 to 0.15625
- down_projection_weight: bfloat16 [1280, 1280], P(('batch', 'seq')), may hold values from -0.15625 to 0.15625
- gain_attn: bfloat16 [1280], P(('batch', 'seq')), may hold values from 0.25 to 1.75
- gain_ffn: bfloat16 [1280], P(('batch', 'seq')), may hold values from 0.25 to 1.75
- up_projection_bias: bfloat16 [1280], P(('batch', 'seq')), may hold values from -3 to 3
- down_projection_bias: bfloat16 [1280], P(('batch', 'seq')), may hold values from -2 to 2
- scale_param: bfloat16 [80], replicated, may hold values from -0.5 to 1.5
- cotangent: bfloat16 [8, 512, 1280], P('batch', 'seq'), may hold values from -6 to 6
Outputs:
- mixed: bfloat16 [8, 512, 1280], P('batch', 'seq')
- grad_tokens: float32 [8, 512, 1280], P('batch', 'seq')
- grad_qkv: float32 [1280, 3840], P(('batch', 'seq'))
- grad_out: float32 [1280, 1280], P(('batch', 'seq'))
- grad_up: float32 [1280, 1280], P(('batch', 'seq'))
- grad_down: float32 [1280, 1280], P(('batch', 'seq'))
- grad_gain_attn: float32 [1280], P(('batch', 'seq'))
- grad_gain_ffn: float32 [1280], P(('batch', 'seq'))
- grad_bias_up: float32 [1280], P(('batch', 'seq'))
- grad_bias_down: float32 [1280], P(('batch', 'seq'))
- grad_scale: float32 [80], replicated
The draws below stay inside these ranges and needn't reach their ends.
All inputs are finite; a program needn't handle non-finite values.
Results may differ from the reference program's by a relative error of at most 0.025.
Values may be sent and summed in bfloat16 or wider, within the bound.
A program may use at most 192 MiB of HBM per device.

```python
import math
import jax
import jax.numpy as jnp
from jax import lax

D = 1280
H = 16
HD = 80
FF = 1280
LEN = 512
SEQS = 8


def draw_tokens(key, part):
    key = jax.random.fold_in(key, 11)
    row_key, col_key, base_key = jax.random.split(key, 3)
    row_scale = jnp.exp(jax.random.uniform(row_key, (SEQS, LEN, 1), jnp.float32, -1.15, 1.15))
    col_scale = jnp.exp(jax.random.uniform(col_key, (1, 1, D), jnp.float32, -0.7, 0.7))
    base_draw = jax.random.normal(base_key, (SEQS, LEN, D), jnp.float32)
    base_draw = jnp.clip(base_draw, -4.0, 4.0)
    return (base_draw * row_scale * col_scale).astype(jnp.bfloat16)


def levels(key, dims, cuts, least, top_value):
    factor_of = 1.0
    for position, parts in cuts:
        draws = jax.random.uniform(jax.random.fold_in(jax.random.fold_in(key, 6), position), (parts,), jnp.float32, least / len(cuts), top_value / len(cuts))
        factor_of = factor_of * jnp.repeat(jnp.exp(draws), dims[position] // parts).reshape((-1,) + (1,) * (len(dims) - 1 - position))
    return factor_of


def centred(key, shape, deviation, limit, shards=(), kind=jnp.bfloat16):
    level = levels(key, shape, shards, -0.22, 0.18) if shards else 1.0
    entries = jax.random.normal(key, shape, jnp.float32) * deviation * level
    return jnp.minimum(jnp.maximum(entries, -limit), limit).astype(kind)


def setup_inputs(seed: int = 0) -> dict:
    arg_keys = jax.random.split(jax.random.key(seed), 12)
    return {
        "tokens": draw_tokens(jax.random.fold_in(arg_keys[11], 71), 0),
        "query_key_value_weight": centred(arg_keys[1], (D, 3 * D), D ** -0.5, 0.15625, ((0, 32),)),
        "attention_output_weight": centred(arg_keys[2], (D, D), (D // 32) ** -0.5, 1.0, ((0, 32),)),
        "up_projection_weight": centred(arg_keys[3], (D, FF), D ** -0.5, 0.15625, ((0, 32),)),
        "down_projection_weight": centred(arg_keys[4], (FF, D), FF ** -0.5, 0.15625, ((0, 32),)),
        "gain_attn": jnp.clip(1.0 + 0.15 * jax.random.normal(arg_keys[5], (D,), jnp.float32), 0.25, 1.75).astype(jnp.bfloat16),
        "gain_ffn": jnp.clip(1.0 + 0.15 * jax.random.normal(arg_keys[6], (D,), jnp.float32), 0.25, 1.75).astype(jnp.bfloat16),
        "up_projection_bias": centred(arg_keys[7], (FF,), 0.5, 3.0, ((0, 32),)),
        "down_projection_bias": centred(arg_keys[8], (D,), 0.3, 2.0, ((0, 32),)),
        "scale_param": jnp.clip(jax.random.uniform(arg_keys[9], (HD,), jnp.float32, -0.5, 1.5), -0.5, 1.5).astype(jnp.bfloat16),
        "cotangent": centred(arg_keys[10], (SEQS, LEN, D), 1.0, 6.0, ((0, 8), (1, 4))),
    }


@jax.custom_vjp
def low(v):
    return lax.optimization_barrier(v.astype(jnp.bfloat16)).astype(jnp.float32)

@jax.custom_vjp
def low_back(v):
    return v

def low_keep(v):
    return (low(v), None)

def low_pass(kept, grad):
    return (grad,)

def back_keep(v):
    return (v, None)

def back_low(kept, grad):
    return (low(grad),)
low.defvjp(low_keep, low_pass)
low_back.defvjp(back_keep, back_low)
epsilon = 1e-06
soft_unit = 1.442695041
neg_large = -1e+30
highest_precision = lax.Precision.HIGHEST

def rms_norm(values, gain):
    inverse = lax.rsqrt(lax.optimization_barrier(jnp.mean(values * values, axis=-1, keepdims=True)) + epsilon)
    return values * inverse * gain

def attend_block(query_blk, keys, values, first):
    scores = low_back(jnp.einsum('qhd,khd->hqk', query_blk, keys, precision=highest_precision))
    query_pos = first + jnp.arange(query_blk.shape[0], dtype=jnp.int32)
    key_pos = jnp.arange(keys.shape[0], dtype=jnp.int32)
    allowed = key_pos[None, :] <= query_pos[:, None]
    scores = jnp.where(allowed[None], scores, neg_large)
    top = lax.optimization_barrier(jnp.max(scores, axis=-1, keepdims=True))
    weights = jnp.exp(scores - top)
    probs = low(weights / lax.optimization_barrier(jnp.sum(weights, axis=-1, keepdims=True)))
    return jnp.einsum('hqk,khd->qhd', probs, values, precision=highest_precision)

def attend_sequence(queries, keys, values):
    length = queries.shape[0]
    block = min(512, length)
    blocks = queries.reshape(length // block, block, H, HD)
    starts = jnp.arange(length // block, dtype=jnp.int32) * block
    checked = jax.checkpoint(attend_block)
    result = lax.map(lambda pair: checked(pair[0], keys, values, pair[1]), (blocks, starts))
    return result.reshape(length, H, HD)

def layer(tokens, query_key_value_weight, attention_output_weight, up_projection_weight, down_projection_weight, gain_attn, gain_ffn, up_projection_bias, down_projection_bias, scale_param):
    seq_total, length, width = tokens.shape
    attention_normed_input = low(rms_norm(tokens, gain_attn))
    query_key_value = low_back(jnp.einsum('wgv,vk->wgk', attention_normed_input, query_key_value_weight, precision=highest_precision))
    q_raw = query_key_value[..., :width].reshape(seq_total, length, H, HD)
    keys = low(query_key_value[..., width:2 * width]).reshape(seq_total, length, H, HD)
    values = low(query_key_value[..., 2 * width:]).reshape(seq_total, length, H, HD)
    factor = soft_unit / math.sqrt(HD) * jax.nn.softplus(scale_param)
    queries = low(q_raw * factor)
    attention_output = lax.map(lambda trio: attend_sequence(trio[0], trio[1], trio[2]), (queries, keys, values))
    attention_output = low(low_back(attention_output.reshape(seq_total, length, width)))
    residual_middle_state = tokens + low_back(jnp.einsum('wgv,vk->wgk', attention_output, attention_output_weight, precision=highest_precision))
    feedforward_normed_input = low(rms_norm(residual_middle_state, gain_ffn))
    up_projected_value = low_back(jnp.einsum('gnj,jb->gnb', feedforward_normed_input, up_projection_weight, precision=highest_precision) + up_projection_bias)
    activation_output = low(jax.nn.silu(up_projected_value))
    return residual_middle_state + jnp.einsum('vhj,jm->vhm', activation_output, down_projection_weight, precision=highest_precision) + down_projection_bias

def reference(tokens, query_key_value_weight, attention_output_weight, up_projection_weight, down_projection_weight, gain_attn, gain_ffn, up_projection_bias, down_projection_bias, scale_param, cotangent):
    floats = [a.astype(jnp.float32) for a in (tokens, query_key_value_weight, attention_output_weight, up_projection_weight, down_projection_weight, gain_attn, gain_ffn, up_projection_bias, down_projection_bias, scale_param)]
    result, pull = jax.vjp(layer, *floats)
    grads = pull(cotangent.astype(jnp.float32))
    return (result.astype(jnp.bfloat16), grads[0], grads[1], grads[2], grads[3], grads[4], grads[5], grads[6], grads[7], grads[8], grads[9])
```

```python
import functools
import math
import types

import jax
import jax.numpy as jnp
from jax import lax
from jax.experimental import pallas as pl
from jax.experimental.pallas import tpu as pltpu
from jax.sharding import PartitionSpec as P

H = 16
HD = 80


epsilon = 1e-06
soft_unit = 1.442695041
neg_large = -1e30


def norm_forward(values, gain):
    inverse = lax.rsqrt(jnp.mean(values * values, axis=1, keepdims=True) + epsilon)
    return (inverse, (values * inverse * gain.astype(jnp.float32)).astype(jnp.bfloat16))


def norm_back(grad_out, values, inverse, gain):
    normed = values * inverse
    scaled = grad_out * gain.astype(jnp.float32)
    grad_gain = jnp.sum(grad_out * normed, axis=0)
    grad_in = inverse * (scaled - normed * jnp.mean(scaled * normed, axis=1, keepdims=True))
    return (grad_in, grad_gain)


def generic_layer(
    tokens,
    query_key_value_weight,
    attention_output_weight,
    up_projection_weight,
    down_projection_weight,
    gain_attn,
    gain_ffn,
    up_projection_bias,
    down_projection_bias,
    scale_param,
    cotangent,
):
    seq_local, tok_seq, width = tokens.shape
    row_count = seq_local * tok_seq
    shards = (
        query_key_value_weight,
        attention_output_weight,
        up_projection_weight,
        down_projection_weight,
        gain_attn,
        gain_ffn,
        up_projection_bias,
        down_projection_bias,
    )
    fwd_weights = (
        lax.all_gather(shards[0], ("batch", "seq"), axis=0, tiled=True),
        lax.all_gather(shards[1], ("batch", "seq"), axis=0, tiled=True),
        lax.all_gather(shards[2], ("batch", "seq"), axis=0, tiled=True),
        lax.all_gather(shards[3], ("batch", "seq"), axis=0, tiled=True),
        lax.all_gather(shards[4], ("batch", "seq"), axis=0, tiled=True),
        lax.all_gather(shards[5], ("batch", "seq"), axis=0, tiled=True),
        lax.all_gather(shards[6], ("batch", "seq"), axis=0, tiled=True),
        lax.all_gather(shards[7], ("batch", "seq"), axis=0, tiled=True),
    )
    wqkv_full, wout_full, wup_full, wdown_full, gattn_full, gffn_full, bup_full, bdown_full = (
        fwd_weights
    )
    inputs = tokens.astype(jnp.float32).reshape(row_count, width)
    inv_attn, attention_normed_input = norm_forward(inputs, gattn_full)
    query_key_value = jnp.dot(attention_normed_input, wqkv_full, preferred_element_type=jnp.float32)
    q_raw = query_key_value[:, :width]
    scale_float = scale_param.astype(jnp.float32)
    factor = soft_unit / math.sqrt(HD) * jax.nn.softplus(scale_float)
    factor_row = jnp.tile(factor, H)
    queries = (q_raw * factor_row).astype(jnp.bfloat16)
    keys_own = (
        query_key_value[:, width : 2 * width]
        .astype(jnp.bfloat16)
        .reshape(seq_local, tok_seq, width)
    )
    values_own = (
        query_key_value[:, 2 * width :].astype(jnp.bfloat16).reshape(seq_local, tok_seq, width)
    )
    keys_all, values_all = (
        lax.all_gather(keys_own, "seq", axis=1, tiled=True),
        lax.all_gather(values_own, "seq", axis=1, tiled=True),
    )
    position = lax.axis_index("seq")
    block_total = lax.axis_size("seq")
    query_pos = position * tok_seq + jnp.arange(tok_seq, dtype=jnp.int32)
    key_offsets = jnp.arange(tok_seq, dtype=jnp.int32)
    queries_h = queries.reshape(seq_local, tok_seq, H, HD)

    def key_block(source, block):
        piece = lax.dynamic_slice_in_dim(source, block * tok_seq, tok_seq, 1)
        return piece.reshape(seq_local, tok_seq, H, HD)

    def block_scores(block):
        scores = jnp.einsum(
            "sqhd,skhd->shqk",
            queries_h,
            key_block(keys_all, block),
            preferred_element_type=jnp.float32,
        )
        allowed = (block * tok_seq + key_offsets)[None, :] <= query_pos[:, None]
        return jnp.where(allowed, scores, neg_large)

    def max_step(block, carry):
        top, total = carry
        scores = block_scores(block)
        new_top = jnp.maximum(top, jnp.max(scores, axis=3, keepdims=True))
        total = total * jnp.exp(top - new_top) + jnp.sum(
            jnp.exp(scores - new_top), axis=3, keepdims=True
        )
        return (new_top, total)

    start_top = jnp.full((seq_local, H, tok_seq, 1), neg_large, jnp.float32)
    top, total = lax.fori_loop(0, block_total, max_step, (start_top, jnp.zeros_like(start_top)))
    log_sum = top + jnp.log(total)

    def value_step(block, accum):
        probs = jnp.exp(block_scores(block) - log_sum).astype(jnp.bfloat16)
        return accum + jnp.einsum(
            "shqk,skhd->sqhd",
            probs,
            key_block(values_all, block),
            preferred_element_type=jnp.float32,
        )

    attention_output = lax.fori_loop(
        0, block_total, value_step, jnp.zeros((seq_local, tok_seq, H, HD), jnp.float32)
    )
    attention_output = attention_output.reshape(row_count, width)
    att_low = attention_output.astype(jnp.bfloat16)
    middle = inputs + jnp.dot(att_low, wout_full, preferred_element_type=jnp.float32)
    inv_ffn, feedforward_normed_input = norm_forward(middle, gffn_full)
    up_projected_value = jnp.dot(
        feedforward_normed_input, wup_full, preferred_element_type=jnp.float32
    ) + bup_full.astype(jnp.float32)
    act_low = jax.nn.silu(up_projected_value).astype(jnp.bfloat16)
    result = (
        middle
        + jnp.dot(act_low, wdown_full, preferred_element_type=jnp.float32)
        + bdown_full.astype(jnp.float32)
    )
    mixed = result.astype(jnp.bfloat16).reshape(seq_local, tok_seq, width)
    back_weights = (
        lax.all_gather(shards[0], ("batch", "seq"), axis=0, tiled=True),
        lax.all_gather(shards[1], ("batch", "seq"), axis=0, tiled=True),
        lax.all_gather(shards[2], ("batch", "seq"), axis=0, tiled=True),
        lax.all_gather(shards[3], ("batch", "seq"), axis=0, tiled=True),
        lax.all_gather(shards[4], ("batch", "seq"), axis=0, tiled=True),
        lax.all_gather(shards[5], ("batch", "seq"), axis=0, tiled=True),
        lax.all_gather(shards[6], ("batch", "seq"), axis=0, tiled=True),
        lax.all_gather(shards[7], ("batch", "seq"), axis=0, tiled=True),
    )
    wqkv_back, wout_back, wup_back, wdown_back, gattn_back, gffn_back, bup_back, bdown_back = (
        back_weights
    )
    grad_low = cotangent.reshape(row_count, width)
    grad_float = grad_low.astype(jnp.float32)
    grad_down = jnp.einsum("rf,rd->fd", act_low, grad_low, preferred_element_type=jnp.float32)
    grad_bias_down = jnp.sum(grad_float, axis=0)
    grad_act = jnp.einsum("rd,fd->rf", grad_low, wdown_back, preferred_element_type=jnp.float32)
    sigma = jax.nn.sigmoid(up_projected_value)
    grad_upv = (grad_act * sigma * (1.0 + up_projected_value * (1.0 - sigma))).astype(jnp.bfloat16)
    grad_up = jnp.einsum(
        "rd,rf->df", feedforward_normed_input, grad_upv, preferred_element_type=jnp.float32
    )
    grad_bias_up = jnp.sum(grad_upv.astype(jnp.float32), axis=0)
    grad_hn_ffn = jnp.einsum("rf,df->rd", grad_upv, wup_back, preferred_element_type=jnp.float32)
    grad_norm_ffn, grad_gain_ffn = norm_back(grad_hn_ffn, middle, inv_ffn, gffn_back)
    grad_middle = grad_float + grad_norm_ffn
    grad_attn = grad_middle.astype(jnp.bfloat16)
    grad_out = jnp.einsum("rd,re->de", att_low, grad_attn, preferred_element_type=jnp.float32)
    block_summed = (
        lax.psum_scatter(grad_out, ("batch", "seq"), scatter_dimension=0, tiled=True),
        lax.psum_scatter(grad_up, ("batch", "seq"), scatter_dimension=0, tiled=True),
        lax.psum_scatter(grad_down, ("batch", "seq"), scatter_dimension=0, tiled=True),
        lax.psum_scatter(grad_gain_ffn, ("batch", "seq"), scatter_dimension=0, tiled=True),
        lax.psum_scatter(grad_bias_up, ("batch", "seq"), scatter_dimension=0, tiled=True),
        lax.psum_scatter(grad_bias_down, ("batch", "seq"), scatter_dimension=0, tiled=True),
    )
    grad_att_low = jnp.einsum(
        "re,de->rd", grad_attn, wout_back, preferred_element_type=jnp.float32
    ).astype(jnp.bfloat16)
    grad_heads = grad_att_low.reshape(seq_local, tok_seq, H, HD)
    delta = jnp.sum(
        (grad_att_low.astype(jnp.float32) * attention_output).reshape(seq_local, tok_seq, H, HD),
        axis=3,
    )
    delta = jnp.transpose(delta, (0, 2, 1))[..., None]
    query_init = jnp.zeros((seq_local, tok_seq, H, HD), jnp.float32)

    def grad_step(block, carry):
        grad_query, term = carry
        scores = block_scores(block)
        probs = jnp.exp(scores - log_sum)
        keys_blk = key_block(keys_all, block)
        values_blk = key_block(values_all, block)
        grad_probs = jnp.einsum(
            "sqhd,skhd->shqk", grad_heads, values_blk, preferred_element_type=jnp.float32
        )
        grad_scores = (probs * (grad_probs - delta)).astype(jnp.bfloat16)
        grad_values = jnp.einsum(
            "shqk,sqhd->skhd",
            probs.astype(jnp.bfloat16),
            grad_heads,
            preferred_element_type=jnp.float32,
        )
        grad_keys = jnp.einsum(
            "shqk,sqhd->skhd", grad_scores, queries_h, preferred_element_type=jnp.float32
        )
        grad_query = grad_query + jnp.einsum(
            "shqk,skhd->sqhd", grad_scores, keys_blk, preferred_element_type=jnp.float32
        )
        piece = jnp.concatenate(
            [
                grad_keys.reshape(seq_local, tok_seq, width),
                grad_values.reshape(seq_local, tok_seq, width),
            ],
            axis=2,
        )
        term = lax.dynamic_update_slice_in_dim(term, piece, block * tok_seq, 1)
        return (grad_query, term)

    term_init = jnp.zeros((seq_local, tok_seq * block_total, 2 * width), jnp.float32)
    grad_query, term = lax.fori_loop(0, block_total, grad_step, (query_init, term_init))
    kv_grads = lax.psum_scatter(
        term.astype(jnp.bfloat16), "seq", scatter_dimension=1, tiled=True
    ).astype(jnp.float32)
    grad_scaled = grad_query.reshape(row_count, width)
    scale_local = jnp.sum((grad_scaled * q_raw).reshape(row_count, H, HD), axis=(0, 1))
    scale_total = lax.psum(scale_local, ("batch", "seq"))
    grad_scale = scale_total * (soft_unit / math.sqrt(HD)) * jax.nn.sigmoid(scale_float)
    grad_qkv_low = jnp.concatenate(
        [grad_scaled * factor_row, kv_grads.reshape(row_count, 2 * width)], axis=1
    ).astype(jnp.bfloat16)
    grad_qkv = jnp.einsum(
        "rd,re->de", attention_normed_input, grad_qkv_low, preferred_element_type=jnp.float32
    )
    grad_hn_attn = jnp.einsum(
        "re,de->rd", grad_qkv_low, wqkv_back, preferred_element_type=jnp.float32
    )
    grad_norm_attn, grad_gain_attn = norm_back(grad_hn_attn, inputs, inv_attn, gattn_back)
    grad_tokens = (grad_middle + grad_norm_attn).reshape(seq_local, tok_seq, width)
    qkv_summed = (
        lax.psum_scatter(grad_qkv, ("batch", "seq"), scatter_dimension=0, tiled=True),
        lax.psum_scatter(grad_gain_attn, ("batch", "seq"), scatter_dimension=0, tiled=True),
    )
    return (
        mixed,
        grad_tokens,
        qkv_summed[0],
        block_summed[0],
        block_summed[1],
        block_summed[2],
        qkv_summed[1],
        block_summed[3],
        block_summed[4],
        block_summed[5],
        grad_scale,
    )


MESH = pl.DeviceIdType.MESH
F32 = jnp.float32
BF16 = jnp.bfloat16


def fits_fused(nb, ns, tokens, wqkv, wup):
    rows, width = wup.shape[0], wup.shape[1]
    return (
        ns == 4
        and nb % 2 == 0
        and tokens.shape == (1, 128, H * HD)
        and width == H * HD
        and 2 * rows == HD
        and nb * ns * rows == width
        and wqkv.shape == (rows, 3 * width)
    )


def nt(a, b):
    return lax.dot_general(a, b, (((1,), (1,)), ((), ())), preferred_element_type=F32)


def nn(a, b):
    return lax.dot_general(a, b, (((1,), (0,)), ((), ())), preferred_element_type=F32)


def tn(a, b):
    return lax.dot_general(a, b, (((0,), (0,)), ((), ())), preferred_element_type=F32)


def layer_kernel(nz, scratch_names, tok, cot, w1p, w2p, smalls, scl, *refs):
    mixed_o, gtok_o, o1, o2, sg_o = refs[:5]
    r = types.SimpleNamespace(**dict(zip(scratch_names, refs[5:])))
    D = tok.shape[1]
    T = tok.shape[0]
    L = 4 * T
    HP = 2 * T
    NH = 4
    HW = NH * HD
    CB = HD
    RW = HD // 2
    LO = 256
    b = lax.axis_index("batch")
    s = lax.axis_index("seq")
    z, y = b // 2, b % 2
    x, c = s // 2, s % 2
    sib = (b, 2 * x + (1 - c))
    xp = (b, 2 * (1 - x) + c)
    yp = (2 * z + (1 - y), s)
    zup = (lax.rem(2 * (z + 1), 2 * nz) + y, s)
    zdn = (lax.rem(2 * (z + nz - 1), 2 * nz) + y, s)
    drains = []

    def when(cond, fn):
        if cond is None:
            fn()
        else:
            pl.when(cond)(fn)

    def both(p, q):
        if p is None:
            return q
        if q is None:
            return p
        return jnp.logical_and(p, q)

    def copy(src, dst, ssem, rsem, dev):
        return pltpu.make_async_remote_copy(
            src_ref=src, dst_ref=dst, send_sem=ssem, recv_sem=rsem, device_id=dev, device_id_type=MESH
        )

    def send(make, cond=None):
        when(cond, lambda: make().start())
        drains.append((make, cond))

    def arrive(make, cond=None):
        when(cond, lambda: make().wait_recv())

    bar = pltpu.get_barrier_semaphore()
    peers = [sib, xp, yp]
    for k in range(1, nz):
        peers.append((2 * lax.rem(z + k, nz) + y, s))
    for dev in peers:
        pl.semaphore_signal(bar, inc=1, device_id=dev, device_id_type=MESH)
    pl.semaphore_wait(bar, len(peers))

    m_sib1 = lambda: copy(w1p.at[1 - c], r.SIB1, r.s_one.at[0], r.r_one.at[0], sib)
    m_ssib = lambda: copy(smalls, r.S.at[b, s], r.s_one.at[1], r.r_one.at[1], sib)
    m_sib2 = lambda: copy(w2p, r.SIB2, r.s_one.at[2], r.r_one.at[2], sib)
    send(m_sib1)
    send(m_ssib)
    send(m_sib2)
    r.S[b, s] = smalls[...]
    r.X[s] = tok[...]
    r.DY[s] = cot[...]

    def chip_rows(own, other):
        own, other = own[:RW].astype(F32), other[:RW].astype(F32)
        lo = jnp.where(c == 0, own, other)
        hi = jnp.where(c == 0, other, own)
        return jnp.concatenate([lo, hi], axis=0).astype(BF16)

    arrive(m_sib1)
    r.CB1[...] = chip_rows(w1p[c, 1 - x], r.SIB1[1 - x])
    m_x1 = lambda: copy(r.CB1, r.W1.at[b, x], r.s_one.at[3], r.r_one.at[3], xp)
    send(m_x1)
    r.W1[b, x] = chip_rows(w1p[c, x], r.SIB1[x])
    m_ssib_r = lambda: copy(smalls, r.S.at[b, 2 * x + (1 - c)], r.s_one.at[1], r.r_one.at[1], sib)
    arrive(m_ssib_r)
    m_xs = lambda: copy(
        r.S.at[b, pl.ds(2 * x, 2)], r.S.at[b, pl.ds(2 * x, 2)], r.s_one.at[4], r.r_one.at[4], xp
    )
    send(m_xs)
    m_xt = lambda: copy(tok, r.X.at[s], r.s_one.at[5], r.r_one.at[5], xp)
    m_st = lambda: copy(tok, r.X.at[s], r.s_one.at[6], r.r_one.at[6], sib)
    m_xc = lambda: copy(cot, r.DY.at[s], r.s_one.at[7], r.r_one.at[7], xp)
    m_sc = lambda: copy(cot, r.DY.at[s], r.s_one.at[8], r.r_one.at[8], sib)
    send(m_xt)
    send(m_st)
    send(m_xc)
    send(m_sc)
    arrive(m_sib2)

    def fill_w2():
        r.W2[z] = chip_rows(w2p[...], r.SIB2[...])

    mine = c == y
    when(mine, fill_w2)

    def gather_item(idx, block, zcond):
        up = lambda zz: copy(block(zz, y), block(zz, y), r.s_up.at[idx, zz], r.r_up.at[idx, zz], zup)
        dn = lambda zz: copy(block(zz, y), block(zz, y), r.s_dn.at[idx, zz], r.r_dn.at[idx, zz], zdn)
        yy = lambda zz: copy(block(zz, y), block(zz, y), r.s_y.at[idx, zz], r.r_y.at[idx, zz], yp)

        def start():
            send(lambda: up(z), both(zcond, z < nz - 1))
            send(lambda: dn(z), both(zcond, z > 0))
            send(lambda: yy(z), zcond)

        def step(d):
            lo, hi = z - d, z + d
            below, above = both(zcond, lo >= 0), both(zcond, hi < nz)
            arrive(lambda: up(lo), below)
            send(lambda: up(lo), both(below, z < nz - 1))
            arrive(lambda: dn(hi), above)
            send(lambda: dn(hi), both(above, z > 0))
            send(lambda: yy(lo), below)
            send(lambda: yy(hi), above)

        def finish():
            for k in range(nz):
                when(
                    None if zcond is None else jnp.logical_not(zcond),
                    lambda k=k: copy(
                        block(k, 1 - y), block(k, 1 - y), r.s_y.at[idx, k], r.r_y.at[idx, k], yp
                    ).wait_recv(),
                )

        return start, step, finish

    g_s = gather_item(0, lambda zz, q: r.S.at[2 * zz + q], None)
    g_qkv = gather_item(1, lambda zz, q: r.W1.at[2 * zz + q, :, :, pl.ds(LO, D - LO)], None)
    g_out = gather_item(2, lambda zz, q: r.W2.at[zz, :, pl.ds(0, D)], mine)
    g_up = gather_item(3, lambda zz, q: r.W1.at[2 * zz + q, :, :, pl.ds(0, LO)], None)
    g_dn = gather_item(4, lambda zz, q: r.W2.at[zz, :, pl.ds(D, D)], mine)

    m_x1_r = lambda: copy(r.CB1, r.W1.at[b, 1 - x], r.s_one.at[3], r.r_one.at[3], xp)
    m_xs_r = lambda: copy(
        r.S.at[b, pl.ds(2 - 2 * x, 2)],
        r.S.at[b, pl.ds(2 - 2 * x, 2)],
        r.s_one.at[4],
        r.r_one.at[4],
        xp,
    )
    arrive(m_xs_r)
    arrive(m_x1_r)
    g_s[0]()
    g_qkv[0]()
    sx = 2 * (1 - x) + c
    so = 2 * (1 - x) + (1 - c)
    ss = 2 * x + (1 - c)
    fwd = lambda name, k, src_i: copy(
        name.at[src_i], name.at[src_i], r.s_one.at[k], r.r_one.at[k], sib
    )
    arrive(lambda: copy(tok, r.X.at[sx], r.s_one.at[5], r.r_one.at[5], xp))
    send(lambda: fwd(r.X, 9, sx))
    g_s[1](1)
    g_qkv[1](1)
    arrive(lambda: copy(cot, r.DY.at[sx], r.s_one.at[7], r.r_one.at[7], xp))
    send(lambda: fwd(r.DY, 10, sx))
    arrive(lambda: copy(tok, r.X.at[ss], r.s_one.at[6], r.r_one.at[6], sib))
    arrive(lambda: fwd(r.X, 9, so))
    arrive(lambda: copy(cot, r.DY.at[ss], r.s_one.at[8], r.r_one.at[8], sib))
    arrive(lambda: fwd(r.DY, 10, so))
    for d in range(2, nz):
        g_s[1](d)
        g_qkv[1](d)
    g_out[0]()
    g_up[0]()
    g_dn[0]()
    g_s[2]()

    jf = lax.broadcasted_iota(jnp.int32, (1, D), 1).astype(F32)
    jk = jnp.floor((jf + 0.5) / RW)
    jl = jf - RW * jk
    pick = (lax.broadcasted_iota(jnp.int32, (128, D), 0).astype(F32) == jl).astype(BF16)
    sm_rows = 2 * nz * 4
    spread = nn(r.S[...].reshape(sm_rows * 8, 128).astype(BF16), pick)
    spread = spread.reshape(sm_rows, 8, D)
    owner = lax.broadcasted_iota(jnp.int32, (sm_rows, 8, D), 0).astype(F32)
    r.ROWS[...] = jnp.sum(jnp.where(owner == jk[None], spread, 0.0), axis=0)
    uf = jf[:, :HW]
    uj = jnp.floor((uf + 0.5) / HD)
    uh = jnp.floor((uf - HD * uj + 0.5) / RW)
    base = (2 * c + x).astype(F32)
    uk = 2.0 * (4.0 * uj + base) + uh
    r.BUP[...] = jnp.sum(
        jnp.where(owner[:, :, :HW] == uk[None], spread[:, :, :HW], 0.0), axis=0
    )
    gain_attn = r.ROWS[0:1]
    gain_ffn = r.ROWS[1:2]
    bias_down = r.ROWS[3:4]
    bias_up = r.BUP[2:3]
    scale = scl[0:1, :]
    factor = soft_unit / math.sqrt(HD) * (
        jnp.maximum(scale, 0.0) + jnp.log(1.0 + jnp.exp(-jnp.abs(scale)))
    )

    for k in range(4):
        xv = r.X[k].astype(F32)
        inv = lax.rsqrt(jnp.mean(xv * xv, axis=1, keepdims=True) + epsilon)
        hn = xv * inv * gain_attn
        r.HN1[pl.ds(k * T, T)] = hn.astype(BF16)
        r.HN1T[:, :, pl.ds(k * T, T)] = hn.T.astype(BF16).reshape(2 * nz, 2 * CB, T)
    g_out[1](1)
    g_qkv[2]()
    g_up[1](1)

    W1 = r.W1
    W2 = r.W2
    for h in range(2):
        wq = W1[:, :, :, pl.ds(LO + 512 * h, 512)].reshape(D, 512)
        r.QKV[:, pl.ds(512 * h, 512)] = nn(r.HN1[...], wq)
    g_out[1](2)
    g_up[1](2)
    g_dn[1](1)
    off = HW - LO
    for j in range(NH):
        q = r.QKV[:, off + HD * j : off + HD * (j + 1)]
        k = r.QKV[:, off + HW + HD * j : off + HW + HD * (j + 1)]
        v = r.QKV[:, off + 2 * HW + HD * j : off + 2 * HW + HD * (j + 1)]
        r.QRAW[j] = q
        r.QH[j] = (q * factor[:, :HD]).astype(BF16)
        r.KH[j] = k.astype(BF16)
        r.VH[j] = v.astype(BF16)
        r.KT[j] = k.T.astype(BF16)
        r.VT[j] = v.T.astype(BF16)
    for d in range(3, nz):
        g_out[1](d)
        g_up[1](d)
    if nz > 2:
        g_dn[1](2)

    tri_k = lax.broadcasted_iota(jnp.int32, (HP, HP), 0)
    tri_q = lax.broadcasted_iota(jnp.int32, (HP, HP), 1)
    seen = tri_k <= tri_q

    def rows_of(p):
        return pl.ds(p * HP, HP)

    def attend(p, j):
        q = r.QH[j, rows_of(p)]
        diag = jnp.where(seen, nt(r.KH[j, rows_of(p)], q), neg_large)
        top = jnp.max(diag, axis=0, keepdims=True)
        if p:
            full = nt(r.KH[j, pl.ds(0, HP)], q)
            top = jnp.maximum(top, jnp.max(full, axis=0, keepdims=True))
            full = jnp.exp(full - top)
        diag = jnp.exp(diag - top)
        total = jnp.sum(diag, axis=0, keepdims=True)
        if p:
            total = total + jnp.sum(full, axis=0, keepdims=True)
        inv = 1.0 / total
        diag = (diag * inv).astype(BF16)
        if p:
            r.PT1[j, pl.ds(0, HP)] = (full * inv).astype(BF16)
            r.PT1[j, pl.ds(HP, HP)] = diag
            ot = nn(r.VT[j], r.PT1[j])
        else:
            r.PT0[j] = diag
            ot = nn(r.VT[j, :, pl.ds(0, HP)], diag)
        r.OT[j, :, rows_of(p)] = ot
        r.OB[rows_of(p), HD * j : HD * (j + 1)] = ot.T.astype(BF16)

    def to_sibling(st, p, value):
        r.PF[p] = value.reshape(2, T, D)
        r.ES[st, p] = r.PF[p, 1 - c].astype(BF16)
        send(lambda: copy(r.ES.at[st, p], r.ER.at[st, p], r.s_e.at[st, p], r.r_e.at[st, p], sib))

    def chip_sum(st, p):
        arrive(lambda: copy(r.ES.at[st, p], r.ER.at[st, p], r.s_e.at[st, p], r.r_e.at[st, p], sib))
        return r.PF[p, c] + r.ER[st, p].astype(F32)

    def xslot(st, p):
        return 2 * st + p if st < 2 else st + 2

    def xcopy(st, p):
        i = xslot(st, p)
        return copy(r.XS.at[i], r.XR.at[i], r.s_x.at[i], r.r_x.at[i], xp)

    def to_x(st, p):
        r.XS[xslot(st, p)] = chip_sum(st, p).astype(BF16)
        send(lambda: xcopy(st, p))

    def pair_sum(st, p):
        arrive(lambda: xcopy(st, p))
        return r.XS[xslot(st, p)].astype(F32) + r.XR[xslot(st, p)].astype(F32)

    def share(name, st, p):
        mk = lambda i: copy(name.at[i], name.at[i], r.s_h.at[st, p], r.r_h.at[st, p], sib)
        send(lambda: mk(2 * p + c))
        return lambda: arrive(lambda: mk(2 * p + (1 - c)))

    def out_proj(p):
        to_sibling(0, p, nn(r.OB[rows_of(p)], W2[:, :, pl.ds(0, D)].reshape(HW, D)))

    for j in range(NH):
        attend(0, j)
    g_out[2]()
    out_proj(0)
    for d in range(3, nz):
        g_dn[1](d)
    attend(1, 0)
    attend(1, 1)
    to_x(0, 0)
    attend(1, 2)
    attend(1, 3)
    out_proj(1)

    r.SGA[...] = jnp.zeros_like(r.SGA)

    def middle(p):
        mid = r.X[2 * p + c].astype(F32) + pair_sum(0, p)
        r.MID[p] = mid
        inv = lax.rsqrt(jnp.mean(mid * mid, axis=1, keepdims=True) + epsilon)
        r.HN2[2 * p + c] = (mid * inv * gain_ffn).astype(BF16)
        return share(r.HN2, 0, p)

    def w_up():
        return W1[:, :, :, pl.ds(0, HW)].reshape(D, HW)

    def feed(p):
        hn = r.HN2[pl.ds(2 * p, 2)].reshape(HP, D)
        u = nn(hn, w_up()) + bias_up
        sig = 1.0 / (1.0 + jnp.exp(-u))
        r.ACT[rows_of(p)] = (u * sig).astype(BF16)
        dy = r.DY[pl.ds(2 * p, 2)].reshape(HP, D)
        dact = nt(dy, W2[:, :, pl.ds(D, D)].reshape(HW, D))
        dup = (dact * sig * (1.0 + u * (1.0 - sig))).astype(BF16)
        r.DUP[rows_of(p), 0:HW] = dup
        to_sibling(1, p, nt(dup, w_up()))
        row = pl.ds(4 + s, 1)
        r.SGA[row, 0:HW] = r.SGA[row, 0:HW] + jnp.sum(dup.astype(F32), axis=0, keepdims=True)

    def transpose_hn2(p):
        for k in range(2):
            t = r.HN2[2 * p + k].astype(F32).T.astype(BF16)
            r.HN2T[:, :, pl.ds((2 * p + k) * T, T)] = t.reshape(2 * nz, 2 * CB, T)

    r.DUP[:, 256:384] = jnp.zeros((L, 128), BF16)
    r.DQ[:, 0:128] = jnp.zeros((L, 128), BF16)
    wait_hn = middle(0)
    to_x(0, 1)
    g_up[2]()
    g_dn[2]()
    wait_hn()
    feed(0)
    transpose_hn2(0)
    wait_hn = middle(1)
    to_x(1, 0)
    wait_hn()
    feed(1)
    transpose_hn2(1)
    to_x(1, 1)

    def scatter_item(idx, part, yr, zu, zd, zcond):
        yc = lambda zz: copy(part(zz, 1 - y), yr(zz), r.s_ry.at[idx, zz], r.r_ry.at[idx, zz], yp)
        up = lambda zz: copy(part(zz, y), zu(zz), r.s_ru.at[idx, zz], r.r_ru.at[idx, zz], zup)
        dn = lambda zz: copy(part(zz, y), zd(zz), r.s_rd.at[idx, zz], r.r_rd.at[idx, zz], zdn)

        def add(zz, other):
            part(zz, y)[...] = (part(zz, y)[...].astype(F32) + other(zz)[...].astype(F32)).astype(BF16)

        def order(visit):
            for d in range(nz - 1, 0, -1):
                visit(z + d, z + d < nz)
                visit(z - d, z - d >= 0)
            visit(z, None)

        ycond = None if zcond is None else jnp.logical_not(zcond)

        def start():
            order(lambda zz, ok: send(lambda: yc(zz), both(ok, ycond)))

        def step(d):
            if d:
                ok = both(zcond, z + d < nz)
                from_below = both(ok, z > 0)
                arrive(lambda: yc(z + d), ok)
                when(ok, lambda: add(z + d, yr))
                arrive(lambda: up(z + d), from_below)
                when(from_below, lambda: add(z + d, zu))
                send(lambda: up(z + d), ok)
                ok2 = both(zcond, z - d >= 0)
                from_above = both(ok2, z < nz - 1)
                arrive(lambda: yc(z - d), ok2)
                when(ok2, lambda: add(z - d, yr))
                arrive(lambda: dn(z - d), from_above)
                when(from_above, lambda: add(z - d, zd))
                send(lambda: dn(z - d), ok2)
            else:
                arrive(lambda: yc(z), zcond)
                when(zcond, lambda: add(z, yr))
                below, above = both(zcond, z > 0), both(zcond, z < nz - 1)
                arrive(lambda: up(z), below)
                when(below, lambda: add(z, zu))
                arrive(lambda: dn(z), above)
                when(above, lambda: add(z, zd))

        return start, step

    def w1_item(idx, lo, width):
        cut = pl.ds(lo, width)
        return scatter_item(
            idx,
            lambda zz, q: r.G1.at[2 * zz + q, :, :, cut],
            lambda zz: r.YR1.at[zz, :, :, cut],
            lambda zz: r.ZU1.at[zz - 1, :, :, cut],
            lambda zz: r.ZD1.at[zz, :, :, cut],
            None,
        )

    def w2_item(idx, lo, width):
        cut = pl.ds(lo, width)
        return scatter_item(
            idx,
            lambda zz, q: r.G2.at[zz, :, cut],
            lambda zz: r.YR2.at[zz, :, cut],
            lambda zz: r.ZU2.at[zz - 1, :, cut],
            lambda zz: r.ZD2.at[zz, :, cut],
            mine,
        )

    s_up = w1_item(0, 0, LO)
    s_dn = w2_item(1, D, D)
    s_out = w2_item(2, 0, D)
    s_qkv = w1_item(3, LO, D - LO)

    gu = nn(r.HN2T[...].reshape(D, L), r.DUP[...])
    r.G1[:, :, :, 0:384] = gu.astype(BF16).reshape(2 * nz, 2, CB, 384)
    s_up[0]()
    dy_all = r.DY[...].reshape(L, D)
    r.G2[:, :, pl.ds(D, D)] = tn(r.ACT[...], dy_all).astype(BF16).reshape(nz, CB, D)
    s_dn[0]()

    def back_middle(p):
        dh = pair_sum(1, p)
        mid = r.MID[p]
        inv = lax.rsqrt(jnp.mean(mid * mid, axis=1, keepdims=True) + epsilon)
        n = mid * inv
        dn = dh * gain_ffn
        dmid = r.DY[2 * p + c].astype(F32) + inv * (
            dn - n * jnp.mean(dn * n, axis=1, keepdims=True)
        )
        r.DMID[p] = dmid
        r.DA[2 * p + c] = dmid.astype(BF16)
        own = jnp.where(x == p, jnp.sum(dh * n, axis=0, keepdims=True), 0.0)
        r.SGA[1:2] = r.SGA[1:2] + own
        return share(r.DA, 1, p)

    def back_out(p):
        da = r.DA[pl.ds(2 * p, 2)].reshape(HP, D)
        r.QKV[0:HP, 0:HW] = nt(da, W2[:, :, pl.ds(0, D)].reshape(HW, D))

    def back_attend(p, j):
        do = r.QKV[0:HP, HD * j : HD * (j + 1)].astype(BF16)
        dof = do.astype(F32)
        delta = jnp.sum(dof.T * r.OT[j, :, rows_of(p)], axis=0, keepdims=True)
        span = HP * (p + 1)
        pt = r.PT1[j] if p else r.PT0[j]
        dpt = nt(r.VH[j, pl.ds(0, span)], do)
        dst = (pt.astype(F32) * (dpt - delta)).astype(BF16)
        dv = nn(pt, do)
        dk = nn(dst, r.QH[j, rows_of(p)])
        dq = nn(r.KT[j, :, pl.ds(0, span)], dst).T
        raw = r.QRAW[j, rows_of(p)]
        r.SGA[3:4, 0:HD] = r.SGA[3:4, 0:HD] + jnp.sum(dq * raw, axis=0, keepdims=True)
        r.DQ[rows_of(p), off + HD * j : off + HD * (j + 1)] = (dq * factor[:, :HD]).astype(BF16)
        ko, vo = off + HW + HD * j, off + 2 * HW + HD * j
        if p == 0:
            r.DKA[j] = dk
            r.DVA[j] = dv
        else:
            r.DQ[0:HP, ko : ko + HD] = (dk[:HP] + r.DKA[j]).astype(BF16)
            r.DQ[HP:L, ko : ko + HD] = dk[HP:].astype(BF16)
            r.DQ[0:HP, vo : vo + HD] = (dv[:HP] + r.DVA[j]).astype(BF16)
            r.DQ[HP:L, vo : vo + HD] = dv[HP:].astype(BF16)

    def down_proj(p):
        to_sibling(2, p, nn(r.ACT[rows_of(p)], W2[:, :, pl.ds(D, D)].reshape(HW, D)))

    wait_da = back_middle(0)
    down_proj(0)
    down_proj(1)
    for d in range(nz - 1, 0, -1):
        s_up[1](d)
    wait_da()
    back_out(0)
    for j in range(NH):
        back_attend(0, j)
    for d in range(nz - 1, 0, -1):
        s_dn[1](d)
    wait_da = back_middle(1)
    r.XS[4] = chip_sum(2, 1 - x).astype(BF16)
    send(lambda: xcopy(2, 0))
    r.PF2[...] = chip_sum(2, x)
    wait_da()
    back_out(1)
    da_all = r.DA[...].reshape(L, D)
    r.G2[:, :, pl.ds(0, D)] = tn(r.OB[...], da_all).astype(BF16).reshape(nz, CB, D)
    s_out[0]()
    for j in range(NH):
        back_attend(1, j)
    s_up[1](0)
    s_dn[1](0)

    def qkv_block(bb):
        t = nn(r.HN1T[bb], r.DQ[...]).reshape(2, CB, D - LO)
        head = t[:, :, 0:128] + r.G1[bb, :, :, pl.ds(LO, 128)].astype(F32)
        r.G1[bb, :, :, pl.ds(LO, 128)] = head.astype(BF16)
        r.G1[bb, :, :, pl.ds(384, D - 384)] = t[:, :, 128:].astype(BF16)

    for k in range(nz):
        qkv_block(2 * k + (1 - y))
    s_qkv[0]()
    for k in range(nz):
        qkv_block(2 * k + y)
    for d in range(nz - 1, 0, -1):
        s_out[1](d)

    arrive(lambda: xcopy(2, 0))
    own_out = r.PF2[...] + r.XR[4].astype(F32)
    mixed_o[...] = (r.MID[x] + own_out + bias_down).astype(BF16)

    for p in range(2):
        w = W1[:, :, :, pl.ds(LO, D - LO)].reshape(D, D - LO)
        to_sibling(3, p, nt(r.DQ[rows_of(p)], w))
    r.XS[5] = chip_sum(3, 1 - x).astype(BF16)
    send(lambda: xcopy(3, 0))
    r.PF2[...] = chip_sum(3, x)

    s_qkv[1](nz - 1)
    s_out[1](0)

    arrive(lambda: xcopy(3, 0))
    dh = r.PF2[...] + r.XR[5].astype(F32)
    xv = r.X[s].astype(F32)
    inv = lax.rsqrt(jnp.mean(xv * xv, axis=1, keepdims=True) + epsilon)
    n = xv * inv
    dn = dh * gain_attn
    gtok_o[...] = r.DMID[x] + inv * (dn - n * jnp.mean(dn * n, axis=1, keepdims=True))
    r.SGA[0:1] = jnp.sum(dh * n, axis=0, keepdims=True)
    r.SGA[2:3] = jnp.sum(r.DY[s].astype(F32), axis=0, keepdims=True)

    def small_copy(k, slot, dev):
        return lambda: copy(r.SGA if k == 0 else r.SGS.at[k - 1], r.SGR.at[slot], r.s_sg.at[slot], r.r_sg.at[slot], dev)

    total = r.SGA[...]
    for k, dev in enumerate((sib, xp, yp)):
        mk = small_copy(k, k, dev)
        send(mk)
        if k == 1:
            for d in range(nz - 2, 0, -1):
                s_qkv[1](d)
        arrive(mk)
        total = total + r.SGR[k]
        r.SGS[k] = total
    mks = []
    for k in range(1, nz):
        mk = small_copy(3, 2 + k, (2 * lax.rem(z + k, nz) + y, s))
        send(mk)
        mks.append(mk)
    s_qkv[1](0)

    m_fx = lambda: copy(r.G1.at[b, 1 - x], r.FX, r.s_one.at[11], r.r_one.at[11], xp)
    send(m_fx)
    done2 = r.G2[z].astype(F32)
    r.GF2[0] = done2[:RW]
    r.GF2[1] = done2[RW:]
    m_g2 = lambda: copy(r.GF2.at[1 - c], r.GR2, r.s_one.at[12], r.r_one.at[12], sib)
    send(m_g2, mine)
    own = r.G1[b, x].astype(F32)
    r.GF[0, x] = own[:RW]
    r.GF[1, x] = own[RW:]
    for k, mk in enumerate(mks):
        arrive(mk)
        total = total + r.SGR[3 + k]
    sg_o[...] = total
    not_mine = jnp.logical_not(mine)
    arrive(m_g2, not_mine)

    def out2_own():
        o2[...] = r.GF2[c]

    def out2_sib():
        o2[...] = r.GR2[...]

    when(mine, out2_own)
    when(not_mine, out2_sib)
    arrive(m_fx)
    other = r.FX[...].astype(F32)
    r.GF[0, 1 - x] = other[:RW]
    r.GF[1, 1 - x] = other[RW:]
    m_gf = lambda: copy(r.GF.at[1 - c], r.GRV, r.s_one.at[13], r.r_one.at[13], sib)
    send(m_gf)
    o1[:, c] = r.GF[c]
    arrive(m_gf)
    o1[:, 1 - c] = r.GRV[...]

    for make, cond in drains:
        when(cond, lambda make=make: make().wait_send())


def fused_layer(nb, ns, tokens, wqkv, wout, wup, wdown, gattn, gffn, bup, bdown, scale_param, cot):
    nz = nb // 2
    rows, D = wout.shape
    T = tokens.shape[1]
    L = ns * T
    cols = jnp.concatenate([wup.reshape(rows, 1, 4, 2, 2, HD), wqkv.reshape(rows, 3, 4, 2, 2, HD)], axis=1)
    w1p = jnp.transpose(cols, (3, 4, 0, 1, 2, 5)).reshape(2, 2, rows, D)
    w1p = jnp.pad(w1p, ((0, 0), (0, 0), (0, 8), (0, 0)))
    w2p = jnp.pad(jnp.concatenate([wout, wdown], axis=1), ((0, 8), (0, 0)))
    smalls = jnp.stack([gattn, gffn, bup, bdown]).astype(F32)
    smalls = jnp.pad(smalls, ((0, 4), (0, 128 - rows)))
    scale = jnp.broadcast_to(jnp.tile(scale_param.astype(F32), 4)[None], (8, 4 * HD))
    V = pltpu.VMEM
    scratch = dict(
        SIB1=V((2, 48, D), BF16),
        SIB2=V((48, 2 * D), BF16),
        CB1=V((HD, D), BF16),
        W1=V((nb, 2, HD, D), BF16),
        W2=V((nz, HD, 2 * D), BF16),
        S=V((nb, 4, 8, 128), F32),
        X=V((4, T, D), BF16),
        DY=V((4, T, D), BF16),
        ROWS=V((8, D), F32),
        BUP=V((8, 4 * HD), F32),
        HN1=V((L, D), BF16),
        HN1T=V((nb, 2 * HD, L), BF16),
        HN2T=V((nb, 2 * HD, L), BF16),
        QKV=V((L, D - 256), F32),
        QRAW=V((4, L, HD), F32),
        QH=V((4, L, HD), BF16),
        KH=V((4, L, HD), BF16),
        VH=V((4, L, HD), BF16),
        KT=V((4, HD, L), BF16),
        VT=V((4, HD, L), BF16),
        PT0=V((4, L // 2, L // 2), BF16),
        PT1=V((4, L, L // 2), BF16),
        OT=V((4, HD, L), F32),
        OB=V((L, 4 * HD), BF16),
        PF=V((2, 2, T, D), F32),
        PF2=V((T, D), F32),
        ES=V((4, 2, T, D), BF16),
        ER=V((4, 2, T, D), BF16),
        XS=V((6, T, D), BF16),
        XR=V((6, T, D), BF16),
        MID=V((2, T, D), F32),
        HN2=V((4, T, D), BF16),
        ACT=V((L, 4 * HD), BF16),
        DUP=V((L, 384), BF16),
        DA=V((4, T, D), BF16),
        DMID=V((2, T, D), F32),
        DQ=V((L, D - 256), BF16),
        DKA=V((4, L // 2, HD), F32),
        DVA=V((4, L // 2, HD), F32),
        G1=V((nb, 2, HD, D), BF16),
        G2=V((nz, HD, 2 * D), BF16),
        YR1=V((nz, 2, HD, D), BF16),
        ZU1=V((nz - 1, 2, HD, D), BF16),
        ZD1=V((nz - 1, 2, HD, D), BF16),
        YR2=V((nz, HD, 2 * D), BF16),
        ZU2=V((nz - 1, HD, 2 * D), BF16),
        ZD2=V((nz - 1, HD, 2 * D), BF16),
        FX=V((HD, D), BF16),
        GF=V((2, 2, rows, D), F32),
        GRV=V((2, rows, D), F32),
        GF2=V((2, rows, 2 * D), F32),
        GR2=V((rows, 2 * D), F32),
        SGA=V((8, D), F32),
        SGS=V((3, 8, D), F32),
        SGR=V((2 + nz, 8, D), F32),
    )
    dma = pltpu.SemaphoreType.DMA
    scratch.update(
        s_one=dma((14,)), r_one=dma((14,)),
        s_up=dma((5, nz)), r_up=dma((5, nz)),
        s_dn=dma((5, nz)), r_dn=dma((5, nz)),
        s_y=dma((5, nz)), r_y=dma((5, nz)),
        s_e=dma((4, 2)), r_e=dma((4, 2)),
        s_x=dma((6,)), r_x=dma((6,)),
        s_h=dma((2, 2)), r_h=dma((2, 2)),
        s_ry=dma((4, nz)), r_ry=dma((4, nz)),
        s_ru=dma((4, nz)), r_ru=dma((4, nz)),
        s_rd=dma((4, nz)), r_rd=dma((4, nz)),
        s_sg=dma((2 + nz,)), r_sg=dma((2 + nz,)),
    )
    vmem = pl.BlockSpec(memory_space=pltpu.VMEM)
    mixed, gtok, o1, o2, sg = pl.pallas_call(
        functools.partial(layer_kernel, nz, tuple(scratch)),
        out_shape=(
            jax.ShapeDtypeStruct((T, D), BF16),
            jax.ShapeDtypeStruct((T, D), F32),
            jax.ShapeDtypeStruct((2, 2, rows, D), F32),
            jax.ShapeDtypeStruct((rows, 2 * D), F32),
            jax.ShapeDtypeStruct((8, D), F32),
        ),
        in_specs=[vmem] * 6,
        out_specs=(vmem,) * 5,
        scratch_shapes=list(scratch.values()),
        compiler_params=pltpu.CompilerParams(
            collective_id=0, has_side_effects=True, vmem_limit_bytes=63 << 20
        ),
        name="decoder_layer",
    )(tokens[0], cot[0], w1p, w2p, smalls, scale)
    grads = jnp.transpose(o1.reshape(2, 2, rows, 4, 4, HD), (2, 3, 4, 1, 0, 5)).reshape(rows, 4 * D)
    b, s = lax.axis_index("batch"), lax.axis_index("seq")
    at = (b * ns + s) * rows
    own = lambda v: lax.dynamic_slice(v, (at,), (rows,))
    bias_up = jnp.transpose(sg[4:8, : 4 * HD].reshape(2, 2, 4, HD), (2, 1, 0, 3)).reshape(D)
    scale_float = scale_param.astype(F32)
    grad_scale = sg[3, :HD] * (soft_unit / math.sqrt(HD)) * jax.nn.sigmoid(scale_float)
    return (
        mixed[None],
        gtok[None],
        grads[:, D:],
        o2[:, :D],
        grads[:, :D],
        o2[:, D:],
        own(sg[0]),
        own(sg[1]),
        own(bias_up),
        own(sg[2]),
        grad_scale,
    )


def layer_step(nb, ns, *args):
    if fits_fused(nb, ns, args[0], args[1], args[3]):
        return fused_layer(nb, ns, *args)
    return generic_layer(*args)


def solution(mesh):
    return jax.shard_map(
        functools.partial(layer_step, mesh.shape["batch"], mesh.shape["seq"]),
        mesh=mesh,
        in_specs=(
            P("batch", "seq", None),
            P(("batch", "seq"), None),
            P(("batch", "seq"), None),
            P(("batch", "seq"), None),
            P(("batch", "seq"), None),
            P(("batch", "seq")),
            P(("batch", "seq")),
            P(("batch", "seq")),
            P(("batch", "seq")),
            P(),
            P("batch", "seq", None),
        ),
        out_specs=(
            P("batch", "seq", None),
            P("batch", "seq", None),
            P(("batch", "seq"), None),
            P(("batch", "seq"), None),
            P(("batch", "seq"), None),
            P(("batch", "seq"), None),
            P(("batch", "seq")),
            P(("batch", "seq")),
            P(("batch", "seq")),
            P(("batch", "seq")),
            P(),
        ),
        check_vma=False,
    )
```

```python
import functools
import math
import types

import jax
import jax.numpy as jnp
from jax import lax
from jax.experimental import pallas as pl
from jax.experimental.pallas import tpu as pltpu
from jax.sharding import PartitionSpec as P

H = 16
HD = 80


epsilon = 1e-06
soft_unit = 1.442695041
neg_large = -1e30


def norm_forward(values, gain):
    inverse = lax.rsqrt(jnp.mean(values * values, axis=1, keepdims=True) + epsilon)
    return (inverse, (values * inverse * gain.astype(jnp.float32)).astype(jnp.bfloat16))


def norm_back(grad_out, values, inverse, gain):
    normed = values * inverse
    scaled = grad_out * gain.astype(jnp.float32)
    grad_gain = jnp.sum(grad_out * normed, axis=0)
    grad_in = inverse * (scaled - normed * jnp.mean(scaled * normed, axis=1, keepdims=True))
    return (grad_in, grad_gain)


def generic_layer(
    tokens,
    query_key_value_weight,
    attention_output_weight,
    up_projection_weight,
    down_projection_weight,
    gain_attn,
    gain_ffn,
    up_projection_bias,
    down_projection_bias,
    scale_param,
    cotangent,
):
    seq_local, tok_seq, width = tokens.shape
    row_count = seq_local * tok_seq
    shards = (
        query_key_value_weight,
        attention_output_weight,
        up_projection_weight,
        down_projection_weight,
        gain_attn,
        gain_ffn,
        up_projection_bias,
        down_projection_bias,
    )
    fwd_weights = (
        lax.all_gather(shards[0], ("batch", "seq"), axis=0, tiled=True),
        lax.all_gather(shards[1], ("batch", "seq"), axis=0, tiled=True),
        lax.all_gather(shards[2], ("batch", "seq"), axis=0, tiled=True),
        lax.all_gather(shards[3], ("batch", "seq"), axis=0, tiled=True),
        lax.all_gather(shards[4], ("batch", "seq"), axis=0, tiled=True),
        lax.all_gather(shards[5], ("batch", "seq"), axis=0, tiled=True),
        lax.all_gather(shards[6], ("batch", "seq"), axis=0, tiled=True),
        lax.all_gather(shards[7], ("batch", "seq"), axis=0, tiled=True),
    )
    wqkv_full, wout_full, wup_full, wdown_full, gattn_full, gffn_full, bup_full, bdown_full = (
        fwd_weights
    )
    inputs = tokens.astype(jnp.float32).reshape(row_count, width)
    inv_attn, attention_normed_input = norm_forward(inputs, gattn_full)
    query_key_value = jnp.dot(attention_normed_input, wqkv_full, preferred_element_type=jnp.float32)
    q_raw = query_key_value[:, :width]
    scale_float = scale_param.astype(jnp.float32)
    factor = soft_unit / math.sqrt(HD) * jax.nn.softplus(scale_float)
    factor_row = jnp.tile(factor, H)
    queries = (q_raw * factor_row).astype(jnp.bfloat16)
    keys_own = (
        query_key_value[:, width : 2 * width]
        .astype(jnp.bfloat16)
        .reshape(seq_local, tok_seq, width)
    )
    values_own = (
        query_key_value[:, 2 * width :].astype(jnp.bfloat16).reshape(seq_local, tok_seq, width)
    )
    keys_all, values_all = (
        lax.all_gather(keys_own, "seq", axis=1, tiled=True),
        lax.all_gather(values_own, "seq", axis=1, tiled=True),
    )
    position = lax.axis_index("seq")
    block_total = lax.axis_size("seq")
    query_pos = position * tok_seq + jnp.arange(tok_seq, dtype=jnp.int32)
    key_offsets = jnp.arange(tok_seq, dtype=jnp.int32)
    queries_h = queries.reshape(seq_local, tok_seq, H, HD)

    def key_block(source, block):
        piece = lax.dynamic_slice_in_dim(source, block * tok_seq, tok_seq, 1)
        return piece.reshape(seq_local, tok_seq, H, HD)

    def block_scores(block):
        scores = jnp.einsum(
            "sqhd,skhd->shqk",
            queries_h,
            key_block(keys_all, block),
            preferred_element_type=jnp.float32,
        )
        allowed = (block * tok_seq + key_offsets)[None, :] <= query_pos[:, None]
        return jnp.where(allowed, scores, neg_large)

    def max_step(block, carry):
        top, total = carry
        scores = block_scores(block)
        new_top = jnp.maximum(top, jnp.max(scores, axis=3, keepdims=True))
        total = total * jnp.exp(top - new_top) + jnp.sum(
            jnp.exp(scores - new_top), axis=3, keepdims=True
        )
        return (new_top, total)

    start_top = jnp.full((seq_local, H, tok_seq, 1), neg_large, jnp.float32)
    top, total = lax.fori_loop(0, block_total, max_step, (start_top, jnp.zeros_like(start_top)))
    log_sum = top + jnp.log(total)

    def value_step(block, accum):
        probs = jnp.exp(block_scores(block) - log_sum).astype(jnp.bfloat16)
        return accum + jnp.einsum(
            "shqk,skhd->sqhd",
            probs,
            key_block(values_all, block),
            preferred_element_type=jnp.float32,
        )

    attention_output = lax.fori_loop(
        0, block_total, value_step, jnp.zeros((seq_local, tok_seq, H, HD), jnp.float32)
    )
    attention_output = attention_output.reshape(row_count, width)
    att_low = attention_output.astype(jnp.bfloat16)
    middle = inputs + jnp.dot(att_low, wout_full, preferred_element_type=jnp.float32)
    inv_ffn, feedforward_normed_input = norm_forward(middle, gffn_full)
    up_projected_value = jnp.dot(
        feedforward_normed_input, wup_full, preferred_element_type=jnp.float32
    ) + bup_full.astype(jnp.float32)
    act_low = jax.nn.silu(up_projected_value).astype(jnp.bfloat16)
    result = (
        middle
        + jnp.dot(act_low, wdown_full, preferred_element_type=jnp.float32)
        + bdown_full.astype(jnp.float32)
    )
    mixed = result.astype(jnp.bfloat16).reshape(seq_local, tok_seq, width)
    back_weights = (
        lax.all_gather(shards[0], ("batch", "seq"), axis=0, tiled=True),
        lax.all_gather(shards[1], ("batch", "seq"), axis=0, tiled=True),
        lax.all_gather(shards[2], ("batch", "seq"), axis=0, tiled=True),
        lax.all_gather(shards[3], ("batch", "seq"), axis=0, tiled=True),
        lax.all_gather(shards[4], ("batch", "seq"), axis=0, tiled=True),
        lax.all_gather(shards[5], ("batch", "seq"), axis=0, tiled=True),
        lax.all_gather(shards[6], ("batch", "seq"), axis=0, tiled=True),
        lax.all_gather(shards[7], ("batch", "seq"), axis=0, tiled=True),
    )
    wqkv_back, wout_back, wup_back, wdown_back, gattn_back, gffn_back, bup_back, bdown_back = (
        back_weights
    )
    grad_low = cotangent.reshape(row_count, width)
    grad_float = grad_low.astype(jnp.float32)
    grad_down = jnp.einsum("rf,rd->fd", act_low, grad_low, preferred_element_type=jnp.float32)
    grad_bias_down = jnp.sum(grad_float, axis=0)
    grad_act = jnp.einsum("rd,fd->rf", grad_low, wdown_back, preferred_element_type=jnp.float32)
    sigma = jax.nn.sigmoid(up_projected_value)
    grad_upv = (grad_act * sigma * (1.0 + up_projected_value * (1.0 - sigma))).astype(jnp.bfloat16)
    grad_up = jnp.einsum(
        "rd,rf->df", feedforward_normed_input, grad_upv, preferred_element_type=jnp.float32
    )
    grad_bias_up = jnp.sum(grad_upv.astype(jnp.float32), axis=0)
    grad_hn_ffn = jnp.einsum("rf,df->rd", grad_upv, wup_back, preferred_element_type=jnp.float32)
    grad_norm_ffn, grad_gain_ffn = norm_back(grad_hn_ffn, middle, inv_ffn, gffn_back)
    grad_middle = grad_float + grad_norm_ffn
    grad_attn = grad_middle.astype(jnp.bfloat16)
    grad_out = jnp.einsum("rd,re->de", att_low, grad_attn, preferred_element_type=jnp.float32)
    block_summed = (
        lax.psum_scatter(grad_out, ("batch", "seq"), scatter_dimension=0, tiled=True),
        lax.psum_scatter(grad_up, ("batch", "seq"), scatter_dimension=0, tiled=True),
        lax.psum_scatter(grad_down, ("batch", "seq"), scatter_dimension=0, tiled=True),
        lax.psum_scatter(grad_gain_ffn, ("batch", "seq"), scatter_dimension=0, tiled=True),
        lax.psum_scatter(grad_bias_up, ("batch", "seq"), scatter_dimension=0, tiled=True),
        lax.psum_scatter(grad_bias_down, ("batch", "seq"), scatter_dimension=0, tiled=True),
    )
    grad_att_low = jnp.einsum(
        "re,de->rd", grad_attn, wout_back, preferred_element_type=jnp.float32
    ).astype(jnp.bfloat16)
    grad_heads = grad_att_low.reshape(seq_local, tok_seq, H, HD)
    delta = jnp.sum(
        (grad_att_low.astype(jnp.float32) * attention_output).reshape(seq_local, tok_seq, H, HD),
        axis=3,
    )
    delta = jnp.transpose(delta, (0, 2, 1))[..., None]
    query_init = jnp.zeros((seq_local, tok_seq, H, HD), jnp.float32)

    def grad_step(block, carry):
        grad_query, term = carry
        scores = block_scores(block)
        probs = jnp.exp(scores - log_sum)
        keys_blk = key_block(keys_all, block)
        values_blk = key_block(values_all, block)
        grad_probs = jnp.einsum(
            "sqhd,skhd->shqk", grad_heads, values_blk, preferred_element_type=jnp.float32
        )
        grad_scores = (probs * (grad_probs - delta)).astype(jnp.bfloat16)
        grad_values = jnp.einsum(
            "shqk,sqhd->skhd",
            probs.astype(jnp.bfloat16),
            grad_heads,
            preferred_element_type=jnp.float32,
        )
        grad_keys = jnp.einsum(
            "shqk,sqhd->skhd", grad_scores, queries_h, preferred_element_type=jnp.float32
        )
        grad_query = grad_query + jnp.einsum(
            "shqk,skhd->sqhd", grad_scores, keys_blk, preferred_element_type=jnp.float32
        )
        piece = jnp.concatenate(
            [
                grad_keys.reshape(seq_local, tok_seq, width),
                grad_values.reshape(seq_local, tok_seq, width),
            ],
            axis=2,
        )
        term = lax.dynamic_update_slice_in_dim(term, piece, block * tok_seq, 1)
        return (grad_query, term)

    term_init = jnp.zeros((seq_local, tok_seq * block_total, 2 * width), jnp.float32)
    grad_query, term = lax.fori_loop(0, block_total, grad_step, (query_init, term_init))
    kv_grads = lax.psum_scatter(
        term.astype(jnp.bfloat16), "seq", scatter_dimension=1, tiled=True
    ).astype(jnp.float32)
    grad_scaled = grad_query.reshape(row_count, width)
    scale_local = jnp.sum((grad_scaled * q_raw).reshape(row_count, H, HD), axis=(0, 1))
    scale_total = lax.psum(scale_local, ("batch", "seq"))
    grad_scale = scale_total * (soft_unit / math.sqrt(HD)) * jax.nn.sigmoid(scale_float)
    grad_qkv_low = jnp.concatenate(
        [grad_scaled * factor_row, kv_grads.reshape(row_count, 2 * width)], axis=1
    ).astype(jnp.bfloat16)
    grad_qkv = jnp.einsum(
        "rd,re->de", attention_normed_input, grad_qkv_low, preferred_element_type=jnp.float32
    )
    grad_hn_attn = jnp.einsum(
        "re,de->rd", grad_qkv_low, wqkv_back, preferred_element_type=jnp.float32
    )
    grad_norm_attn, grad_gain_attn = norm_back(grad_hn_attn, inputs, inv_attn, gattn_back)
    grad_tokens = (grad_middle + grad_norm_attn).reshape(seq_local, tok_seq, width)
    qkv_summed = (
        lax.psum_scatter(grad_qkv, ("batch", "seq"), scatter_dimension=0, tiled=True),
        lax.psum_scatter(grad_gain_attn, ("batch", "seq"), scatter_dimension=0, tiled=True),
    )
    return (
        mixed,
        grad_tokens,
        qkv_summed[0],
        block_summed[0],
        block_summed[1],
        block_summed[2],
        qkv_summed[1],
        block_summed[3],
        block_summed[4],
        block_summed[5],
        grad_scale,
    )


MESH = pl.DeviceIdType.MESH
F32 = jnp.float32
BF16 = jnp.bfloat16


def fits_fused(nb, ns, tokens, wqkv, wup):
    rows, width = wup.shape[0], wup.shape[1]
    return (
        ns == 4
        and nb % 2 == 0
        and tokens.shape == (1, 128, H * HD)
        and width == H * HD
        and 2 * rows == HD
        and nb * ns * rows == width
        and wqkv.shape == (rows, 3 * width)
    )


def nt(a, b):
    return lax.dot_general(a, b, (((1,), (1,)), ((), ())), preferred_element_type=F32)


def nn(a, b):
    return lax.dot_general(a, b, (((1,), (0,)), ((), ())), preferred_element_type=F32)


def tn(a, b):
    return lax.dot_general(a, b, (((0,), (0,)), ((), ())), preferred_element_type=F32)


def layer_kernel(nz, scratch_names, tok, cot, wqkv, wout, wup, wdown, ga, gf, bu, bd, scl, *refs):
    mixed_o, gtok_o, o1, o2, sg_o = refs[:5]
    r = types.SimpleNamespace(**dict(zip(scratch_names, refs[5:])))
    D = tok.shape[1]
    T = tok.shape[0]
    L = 4 * T
    HP = 2 * T
    NH = 4
    HW = NH * HD
    CB = HD
    RW = HD // 2
    LO = 256
    b = lax.axis_index("batch")
    s = lax.axis_index("seq")
    z, y = b // 2, b % 2
    x, c = s // 2, s % 2
    sib = (b, 2 * x + (1 - c))
    xp = (b, 2 * (1 - x) + c)
    yp = (2 * z + (1 - y), s)
    zup = (lax.rem(2 * (z + 1), 2 * nz) + y, s)
    zdn = (lax.rem(2 * (z + nz - 1), 2 * nz) + y, s)
    drains = []

    def when(cond, fn):
        if cond is None:
            fn()
        else:
            pl.when(cond)(fn)

    def both(p, q):
        if p is None:
            return q
        if q is None:
            return p
        return jnp.logical_and(p, q)

    def copy(src, dst, ssem, rsem, dev):
        return pltpu.make_async_remote_copy(
            src_ref=src, dst_ref=dst, send_sem=ssem, recv_sem=rsem, device_id=dev, device_id_type=MESH
        )

    def send(make, cond=None):
        when(cond, lambda: make().start())
        drains.append((make, cond))

    def arrive(make, cond=None):
        when(cond, lambda: make().wait_recv())

    bar = pltpu.get_barrier_semaphore()
    peers = [sib, xp, yp]
    for k in range(1, nz):
        peers.append((2 * lax.rem(z + k, nz) + y, s))
    for dev in peers:
        pl.semaphore_signal(bar, inc=1, device_id=dev, device_id_type=MESH)
    fetches = [
        pltpu.make_async_copy(src, dst, r.s_in.at[k])
        for k, (src, dst) in enumerate(
            (
                (wqkv, r.WQ),
                (wup, r.WU),
                (wout, r.WO),
                (wdown, r.WD),
                (tok, r.X.at[s]),
                (cot, r.DY.at[s]),
            )
        )
    ]
    for f in fetches:
        f.start()
    small_rows = [v[...].astype(F32).reshape(1, RW) for v in (ga, gf, bu, bd)]
    r.SM[...] = jnp.zeros_like(r.SM)
    for k, row in enumerate(small_rows):
        r.SM[k : k + 1, 0:RW] = row
    fetches[0].wait()
    fetches[1].wait()

    def pieces(cc):
        for xx in range(2):
            for t in range(4):
                for j in range(NH):
                    src = HD * (4 * j + 2 * cc + xx)
                    v = r.WU[:, src : src + HD] if t == 0 else r.WQ[:, D * (t - 1) + src : D * (t - 1) + src + HD]
                    r.W1P[cc, xx, 0:RW, HW * t + HD * j : HW * t + HD * (j + 1)] = v

    pieces(0)
    pieces(1)
    pl.semaphore_wait(bar, len(peers))

    m_sib1 = lambda: copy(r.W1P.at[1 - c], r.SIB1, r.s_one.at[0], r.r_one.at[0], sib)
    m_ssib = lambda: copy(r.SM, r.S.at[b, s], r.s_one.at[1], r.r_one.at[1], sib)
    m_sib2 = lambda: copy(r.W2P, r.SIB2, r.s_one.at[2], r.r_one.at[2], sib)
    send(m_sib1)
    send(m_ssib)
    fetches[2].wait()
    fetches[3].wait()
    r.W2P[0:RW, 0:D] = r.WO[...]
    r.W2P[0:RW, D : 2 * D] = r.WD[...]
    send(m_sib2)
    r.S[b, s] = r.SM[...]

    def chip_rows(own, other):
        own, other = own[:RW].astype(F32), other[:RW].astype(F32)
        lo = jnp.where(c == 0, own, other)
        hi = jnp.where(c == 0, other, own)
        return jnp.concatenate([lo, hi], axis=0).astype(BF16)

    arrive(m_sib1)
    r.CB1[...] = chip_rows(r.W1P[c, 1 - x], r.SIB1[1 - x])
    m_x1 = lambda: copy(r.CB1, r.W1.at[b, x], r.s_one.at[3], r.r_one.at[3], xp)
    send(m_x1)
    r.W1[b, x] = chip_rows(r.W1P[c, x], r.SIB1[x])
    def gather_item(idx, block, zcond, passes_y=True):
        up = lambda zz: copy(block(zz, y), block(zz, y), r.s_up.at[idx, zz], r.r_up.at[idx, zz], zup)
        dn = lambda zz: copy(block(zz, y), block(zz, y), r.s_dn.at[idx, zz], r.r_dn.at[idx, zz], zdn)
        yy = lambda zz: copy(block(zz, y), block(zz, y), r.s_y.at[idx, zz], r.r_y.at[idx, zz], yp)

        def start():
            send(lambda: up(z), both(zcond, z < nz - 1))
            send(lambda: dn(z), both(zcond, z > 0))
            if passes_y:
                send(lambda: yy(z), zcond)

        def step(d):
            lo, hi = z - d, z + d
            below, above = both(zcond, lo >= 0), both(zcond, hi < nz)
            arrive(lambda: up(lo), below)
            send(lambda: up(lo), both(below, z < nz - 1))
            arrive(lambda: dn(hi), above)
            send(lambda: dn(hi), both(above, z > 0))
            if passes_y:
                send(lambda: yy(lo), below)
                send(lambda: yy(hi), above)

        def finish():
            if passes_y:
                for k in range(nz):
                    when(
                        None if zcond is None else jnp.logical_not(zcond),
                        lambda k=k: copy(
                            block(k, 1 - y), block(k, 1 - y), r.s_y.at[idx, k], r.r_y.at[idx, k], yp
                        ).wait_recv(),
                    )

        return start, step, finish

    mine = c == y
    not_mine = c != y
    g_s = gather_item(0, lambda zz, q: r.S.at[2 * zz + q], None)
    g_own = gather_item(1, lambda zz, q: r.W1.at[2 * zz + q, x, :, pl.ds(LO, D - LO)], None)
    g_oth = gather_item(2, lambda zz, q: r.W1.at[2 * zz + q, 1 - x, :, pl.ds(LO, D - LO)], None)
    g_out = gather_item(3, lambda zz, q: r.W2.at[zz, :, pl.ds(0, D)], None, False)
    g_up = gather_item(4, lambda zz, q: r.W1.at[2 * zz + q, :, :, pl.ds(0, LO)], None)
    g_dn = gather_item(5, lambda zz, q: r.W2.at[zz, :, pl.ds(D, D)], mine)

    g_own[0]()
    m_ssib_r = lambda: copy(r.SM, r.S.at[b, 2 * x + (1 - c)], r.s_one.at[1], r.r_one.at[1], sib)
    arrive(m_ssib_r)
    m_xs = lambda: copy(
        r.S.at[b, pl.ds(2 * x, 2)], r.S.at[b, pl.ds(2 * x, 2)], r.s_one.at[4], r.r_one.at[4], xp
    )
    send(m_xs)
    fetches[4].wait()
    fetches[5].wait()
    own_tok, own_cot = r.X.at[s], r.DY.at[s]
    m_xt = lambda: copy(own_tok, own_tok, r.s_one.at[5], r.r_one.at[5], xp)
    m_st = lambda: copy(own_tok, own_tok, r.s_one.at[6], r.r_one.at[6], sib)
    m_xc = lambda: copy(own_cot, own_cot, r.s_one.at[7], r.r_one.at[7], xp)
    m_sc = lambda: copy(own_cot, own_cot, r.s_one.at[8], r.r_one.at[8], sib)
    send(m_xt)
    send(m_st)
    send(m_xc)
    send(m_sc)
    arrive(m_sib2)

    def fill_w2():
        r.W2[z] = chip_rows(r.W2P[...], r.SIB2[...])

    when(mine, fill_w2)
    m_y2 = lambda: copy(
        r.W2.at[z, :, pl.ds(0, D)], r.W2.at[z, :, pl.ds(0, D)], r.s_one.at[14], r.r_one.at[14], yp
    )

    m_x1_r = lambda: copy(r.CB1, r.W1.at[b, 1 - x], r.s_one.at[3], r.r_one.at[3], xp)
    m_xs_r = lambda: copy(
        r.S.at[b, pl.ds(2 - 2 * x, 2)],
        r.S.at[b, pl.ds(2 - 2 * x, 2)],
        r.s_one.at[4],
        r.r_one.at[4],
        xp,
    )
    sx = 2 * (1 - x) + c
    so = 2 * (1 - x) + (1 - c)
    ss = 2 * x + (1 - c)
    fwd = lambda name, k, src_i: copy(
        name.at[src_i], name.at[src_i], r.s_one.at[k], r.r_one.at[k], sib
    )
    arrive(m_x1_r)
    g_oth[0]()
    arrive(m_xs_r)
    g_s[0]()
    send(m_y2, mine)
    g_own[1](1)
    arrive(lambda: copy(own_tok, r.X.at[sx], r.s_one.at[5], r.r_one.at[5], xp))
    send(lambda: fwd(r.X, 9, sx))
    g_oth[1](1)
    g_s[1](1)
    arrive(m_y2, not_mine)
    g_out[0]()
    g_own[1](2)
    arrive(lambda: copy(own_tok, r.X.at[ss], r.s_one.at[6], r.r_one.at[6], sib))
    arrive(lambda: fwd(r.X, 9, so))
    g_oth[1](2)
    g_s[1](2)
    arrive(lambda: copy(own_cot, r.DY.at[sx], r.s_one.at[7], r.r_one.at[7], xp))
    send(lambda: fwd(r.DY, 10, sx))
    arrive(lambda: copy(own_cot, r.DY.at[ss], r.s_one.at[8], r.r_one.at[8], sib))
    for d in range(3, nz):
        g_own[1](d)
        g_oth[1](d)
        g_s[1](d)
    g_up[0]()
    g_dn[0]()
    g_out[1](1)
    g_s[2]()
    arrive(lambda: fwd(r.DY, 10, so))

    jf = lax.broadcasted_iota(jnp.int32, (1, D), 1).astype(F32)
    jk = jnp.floor((jf + 0.5) / RW)
    jl = jf - RW * jk
    pick = (lax.broadcasted_iota(jnp.int32, (128, D), 0).astype(F32) == jl).astype(BF16)
    sm_rows = 2 * nz * 4
    spread = nn(r.S[...].reshape(sm_rows * 8, 128).astype(BF16), pick)
    spread = spread.reshape(sm_rows, 8, D)
    owner = lax.broadcasted_iota(jnp.int32, (sm_rows, 8, D), 0).astype(F32)
    r.ROWS[...] = jnp.sum(jnp.where(owner == jk[None], spread, 0.0), axis=0)
    uf = jf[:, :HW]
    uj = jnp.floor((uf + 0.5) / HD)
    uh = jnp.floor((uf - HD * uj + 0.5) / RW)
    base = (2 * c + x).astype(F32)
    uk = 2.0 * (4.0 * uj + base) + uh
    r.BUP[...] = jnp.sum(
        jnp.where(owner[:, :, :HW] == uk[None], spread[:, :, :HW], 0.0), axis=0
    )
    gain_attn = r.ROWS[0:1]
    gain_ffn = r.ROWS[1:2]
    bias_down = r.ROWS[3:4]
    bias_up = r.BUP[2:3]
    scale = scl[...].astype(F32).reshape(1, HD)
    factor = soft_unit / math.sqrt(HD) * (
        jnp.maximum(scale, 0.0) + jnp.log(1.0 + jnp.exp(-jnp.abs(scale)))
    )

    for k in range(4):
        xv = r.X[k].astype(F32)
        inv = lax.rsqrt(jnp.mean(xv * xv, axis=1, keepdims=True) + epsilon)
        hn = xv * inv * gain_attn
        r.HN1[pl.ds(k * T, T)] = hn.astype(BF16)
        r.HN1T[:, :, pl.ds(k * T, T)] = hn.T.astype(BF16).reshape(2 * nz, 2 * CB, T)
    g_out[1](2)
    g_own[2]()
    g_oth[2]()
    for d in range(3, nz):
        g_out[1](d)

    W1 = r.W1
    W2 = r.W2
    for h in range(2):
        wq = W1[:, :, :, pl.ds(LO + 512 * h, 512)].reshape(D, 512)
        r.QKV[:, pl.ds(512 * h, 512)] = nn(r.HN1[...], wq)
    off = HW - LO
    for j in range(NH):
        q = r.QKV[:, off + HD * j : off + HD * (j + 1)]
        k = r.QKV[:, off + HW + HD * j : off + HW + HD * (j + 1)]
        v = r.QKV[:, off + 2 * HW + HD * j : off + 2 * HW + HD * (j + 1)]
        r.QRAW[j] = q
        r.QH[j] = (q * factor).astype(BF16)
        r.KH[j] = k.astype(BF16)
        r.VH[j] = v.astype(BF16)
        r.KT[j] = k.T.astype(BF16)
        r.VT[j] = v.T.astype(BF16)
    tri_k = lax.broadcasted_iota(jnp.int32, (HP, HP), 0)
    tri_q = lax.broadcasted_iota(jnp.int32, (HP, HP), 1)
    seen = tri_k <= tri_q

    def rows_of(p):
        return pl.ds(p * HP, HP)

    def attend(p, j):
        q = r.QH[j, rows_of(p)]
        diag = jnp.where(seen, nt(r.KH[j, rows_of(p)], q), neg_large)
        top = jnp.max(diag, axis=0, keepdims=True)
        if p:
            full = nt(r.KH[j, pl.ds(0, HP)], q)
            top = jnp.maximum(top, jnp.max(full, axis=0, keepdims=True))
            full = jnp.exp(full - top)
        diag = jnp.exp(diag - top)
        total = jnp.sum(diag, axis=0, keepdims=True)
        if p:
            total = total + jnp.sum(full, axis=0, keepdims=True)
        inv = 1.0 / total
        diag = (diag * inv).astype(BF16)
        if p:
            r.PT1[j, pl.ds(0, HP)] = (full * inv).astype(BF16)
            r.PT1[j, pl.ds(HP, HP)] = diag
            ot = nn(r.VT[j], r.PT1[j])
        else:
            r.PT0[j] = diag
            ot = nn(r.VT[j, :, pl.ds(0, HP)], diag)
        r.OT[j, :, rows_of(p)] = ot
        r.OB[rows_of(p), HD * j : HD * (j + 1)] = ot.T.astype(BF16)

    def to_sibling(st, p, value):
        r.PF[p] = value.reshape(2, T, D)
        r.ES[st, p] = r.PF[p, 1 - c].astype(BF16)
        send(lambda: copy(r.ES.at[st, p], r.ER.at[st, p], r.s_e.at[st, p], r.r_e.at[st, p], sib))

    def chip_sum(st, p):
        arrive(lambda: copy(r.ES.at[st, p], r.ER.at[st, p], r.s_e.at[st, p], r.r_e.at[st, p], sib))
        return r.PF[p, c] + r.ER[st, p].astype(F32)

    def xslot(st, p):
        return 2 * st + p if st < 2 else st + 2

    def xcopy(st, p):
        i = xslot(st, p)
        return copy(r.XS.at[i], r.XR.at[i], r.s_x.at[i], r.r_x.at[i], xp)

    def to_x(st, p):
        r.XS[xslot(st, p)] = chip_sum(st, p).astype(BF16)
        send(lambda: xcopy(st, p))

    def pair_sum(st, p):
        arrive(lambda: xcopy(st, p))
        return r.XS[xslot(st, p)].astype(F32) + r.XR[xslot(st, p)].astype(F32)

    def share(name, st, p):
        mk = lambda i: copy(name.at[i], name.at[i], r.s_h.at[st, p], r.r_h.at[st, p], sib)
        send(lambda: mk(2 * p + c))
        return lambda: arrive(lambda: mk(2 * p + (1 - c)))

    def out_proj(p):
        to_sibling(0, p, nn(r.OB[rows_of(p)], W2[:, :, pl.ds(0, D)].reshape(HW, D)))

    for j in range(NH):
        attend(0, j)
    out_proj(0)
    g_up[1](1)
    attend(1, 0)
    attend(1, 1)
    to_x(0, 0)
    g_dn[1](1)
    attend(1, 2)
    attend(1, 3)
    out_proj(1)
    for d in range(2, nz):
        g_up[1](d)
        g_dn[1](d)
    to_x(0, 1)

    r.SGA[...] = jnp.zeros_like(r.SGA)

    def middle(p):
        mid = r.X[2 * p + c].astype(F32) + pair_sum(0, p)
        r.MID[p] = mid
        inv = lax.rsqrt(jnp.mean(mid * mid, axis=1, keepdims=True) + epsilon)
        r.HN2[2 * p + c] = (mid * inv * gain_ffn).astype(BF16)
        return share(r.HN2, 0, p)

    def w_up():
        return W1[:, :, :, pl.ds(0, HW)].reshape(D, HW)

    def feed(p):
        hn = r.HN2[pl.ds(2 * p, 2)].reshape(HP, D)
        u = nn(hn, w_up()) + bias_up
        sig = 1.0 / (1.0 + jnp.exp(-u))
        r.ACT[rows_of(p)] = (u * sig).astype(BF16)
        dy = r.DY[pl.ds(2 * p, 2)].reshape(HP, D)
        dact = nt(dy, W2[:, :, pl.ds(D, D)].reshape(HW, D))
        dup = (dact * sig * (1.0 + u * (1.0 - sig))).astype(BF16)
        r.DUP[rows_of(p), 0:HW] = dup
        to_sibling(1, p, nt(dup, w_up()))
        row = pl.ds(4 + s, 1)
        r.SGA[row, 0:HW] = r.SGA[row, 0:HW] + jnp.sum(dup.astype(F32), axis=0, keepdims=True)

    def transpose_hn2(p):
        for k in range(2):
            t = r.HN2[2 * p + k].astype(F32).T.astype(BF16)
            r.HN2T[:, :, pl.ds((2 * p + k) * T, T)] = t.reshape(2 * nz, 2 * CB, T)

    r.DUP[:, 256:384] = jnp.zeros((L, 128), BF16)
    r.DQ[:, 0:128] = jnp.zeros((L, 128), BF16)
    wait_hn = middle(0)
    g_up[2]()
    g_dn[2]()
    wait_hn()
    feed(0)
    transpose_hn2(0)
    wait_hn = middle(1)
    to_x(1, 0)
    wait_hn()
    feed(1)
    transpose_hn2(1)
    to_x(1, 1)

    def scatter_item(idx, part, yr, zu, zd, zcond, y_first=True):
        yc = lambda zz: copy(part(zz, 1 - y), yr(zz), r.s_ry.at[idx, zz], r.r_ry.at[idx, zz], yp)
        up = lambda zz: copy(part(zz, y), zu(zz), r.s_ru.at[idx, zz], r.r_ru.at[idx, zz], zup)
        dn = lambda zz: copy(part(zz, y), zd(zz), r.s_rd.at[idx, zz], r.r_rd.at[idx, zz], zdn)

        def add(zz, other):
            part(zz, y)[...] = (part(zz, y)[...].astype(F32) + other(zz)[...].astype(F32)).astype(BF16)

        ycond = None if zcond is None else jnp.logical_not(zcond)

        def start(d):
            if d:
                send(lambda: yc(z + d), both(z + d < nz, ycond))
                send(lambda: yc(z - d), both(z - d >= 0, ycond))
            else:
                send(lambda: yc(z), ycond)

        def step(d):
            if d:
                ok = both(zcond, z + d < nz)
                from_below = both(ok, z > 0)
                if y_first:
                    arrive(lambda: yc(z + d), ok)
                    when(ok, lambda: add(z + d, yr))
                arrive(lambda: up(z + d), from_below)
                when(from_below, lambda: add(z + d, zu))
                send(lambda: up(z + d), ok)
                ok2 = both(zcond, z - d >= 0)
                from_above = both(ok2, z < nz - 1)
                if y_first:
                    arrive(lambda: yc(z - d), ok2)
                    when(ok2, lambda: add(z - d, yr))
                arrive(lambda: dn(z - d), from_above)
                when(from_above, lambda: add(z - d, zd))
                send(lambda: dn(z - d), ok2)
            else:
                below, above = both(zcond, z > 0), both(zcond, z < nz - 1)
                arrive(lambda: up(z), below)
                when(below, lambda: add(z, zu))
                arrive(lambda: dn(z), above)
                when(above, lambda: add(z, zd))
                if y_first:
                    arrive(lambda: yc(z), zcond)
                    when(zcond, lambda: add(z, yr))

        return start, step

    far = range(nz - 1, 0, -1)
    cut_up, cut_qkv = pl.ds(0, LO), pl.ds(LO, D - LO)
    s_up = scatter_item(
        0,
        lambda zz, q: r.G1.at[2 * zz + q, :, :, cut_up],
        lambda zz: r.YR1.at[zz, :, :, cut_up],
        lambda zz: r.ZU1.at[zz - 1, :, :, cut_up],
        lambda zz: r.ZD1.at[zz, :, :, cut_up],
        None,
    )

    def qkv_item(idx, xx):
        return scatter_item(
            idx,
            lambda zz, q: r.G1.at[2 * zz + q, xx, :, cut_qkv],
            lambda zz: r.YR1.at[zz, xx, :, cut_qkv],
            lambda zz: r.ZU1.at[zz - 1, xx, :, cut_qkv],
            lambda zz: r.ZD1.at[zz, xx, :, cut_qkv],
            None,
        )

    def w2_item(idx, lo, zcond, y_first):
        cut = pl.ds(lo, D)
        return scatter_item(
            idx,
            lambda zz, q: r.G2.at[zz, :, cut],
            lambda zz: r.YR2.at[zz, :, cut],
            lambda zz: r.ZU2.at[zz - 1, :, cut],
            lambda zz: r.ZD2.at[zz, :, cut],
            zcond,
            y_first,
        )

    s_dn = w2_item(1, D, mine, True)
    s_out = w2_item(2, 0, None, False)
    s_far = qkv_item(3, 1 - x)
    s_own = qkv_item(4, x)

    gu = nn(r.HN2T[...].reshape(D, L), r.DUP[...])
    r.G1[:, :, :, 0:384] = gu.astype(BF16).reshape(2 * nz, 2, CB, 384)
    for d in (*far, 0):
        s_up[0](d)
    dy_all = r.DY[...].reshape(L, D)
    r.G2[:, :, pl.ds(D, D)] = tn(r.ACT[...], dy_all).astype(BF16).reshape(nz, CB, D)
    for d in (*far, 0):
        s_dn[0](d)

    def back_middle(p):
        dh = pair_sum(1, p)
        mid = r.MID[p]
        inv = lax.rsqrt(jnp.mean(mid * mid, axis=1, keepdims=True) + epsilon)
        n = mid * inv
        dn = dh * gain_ffn
        dmid = r.DY[2 * p + c].astype(F32) + inv * (
            dn - n * jnp.mean(dn * n, axis=1, keepdims=True)
        )
        r.DMID[p] = dmid
        r.DA[2 * p + c] = dmid.astype(BF16)
        own = jnp.where(x == p, jnp.sum(dh * n, axis=0, keepdims=True), 0.0)
        r.SGA[1:2] = r.SGA[1:2] + own
        return share(r.DA, 1, p)

    def back_out(p):
        da = r.DA[pl.ds(2 * p, 2)].reshape(HP, D)
        r.QKV[0:HP, 0:HW] = nt(da, W2[:, :, pl.ds(0, D)].reshape(HW, D))

    def back_attend(p, j):
        do = r.QKV[0:HP, HD * j : HD * (j + 1)].astype(BF16)
        dof = do.astype(F32)
        delta = jnp.sum(dof.T * r.OT[j, :, rows_of(p)], axis=0, keepdims=True)
        span = HP * (p + 1)
        pt = r.PT1[j] if p else r.PT0[j]
        dpt = nt(r.VH[j, pl.ds(0, span)], do)
        dst = (pt.astype(F32) * (dpt - delta)).astype(BF16)
        dv = nn(pt, do)
        dk = nn(dst, r.QH[j, rows_of(p)])
        dq = nn(r.KT[j, :, pl.ds(0, span)], dst).T
        raw = r.QRAW[j, rows_of(p)]
        r.SGA[3:4, 0:HD] = r.SGA[3:4, 0:HD] + jnp.sum(dq * raw, axis=0, keepdims=True)
        r.DQ[rows_of(p), off + HD * j : off + HD * (j + 1)] = (dq * factor).astype(BF16)
        ko, vo = off + HW + HD * j, off + 2 * HW + HD * j
        if p == 0:
            r.DKA[j] = dk
            r.DVA[j] = dv
        else:
            r.DQ[0:HP, ko : ko + HD] = (dk[:HP] + r.DKA[j]).astype(BF16)
            r.DQ[HP:L, ko : ko + HD] = dk[HP:].astype(BF16)
            r.DQ[0:HP, vo : vo + HD] = (dv[:HP] + r.DVA[j]).astype(BF16)
            r.DQ[HP:L, vo : vo + HD] = dv[HP:].astype(BF16)

    def down_proj(p):
        to_sibling(2, p, nn(r.ACT[rows_of(p)], W2[:, :, pl.ds(D, D)].reshape(HW, D)))

    wait_da = back_middle(0)
    down_proj(0)
    down_proj(1)
    if nz > 3:
        s_up[1](3)
    wait_da()
    back_out(0)
    for j in range(NH):
        back_attend(0, j)
    for d in range(min(2, nz - 1), 0, -1):
        s_up[1](d)
    wait_da = back_middle(1)
    r.XS[4] = chip_sum(2, 1 - x).astype(BF16)
    send(lambda: xcopy(2, 0))
    r.PF2[...] = chip_sum(2, x)
    if nz > 3:
        s_dn[1](3)
    wait_da()
    back_out(1)
    da_all = r.DA[...].reshape(L, D)
    r.G2[:, :, pl.ds(0, D)] = tn(r.OB[...], da_all).astype(BF16).reshape(nz, CB, D)
    if nz > 3:
        s_out[1](3)
    for j in range(NH):
        back_attend(1, j)

    def qkv_block(bb):
        t = nn(r.HN1T[bb], r.DQ[...]).reshape(2, CB, D - LO)
        head = t[:, :, 0:128] + r.G1[bb, :, :, pl.ds(LO, 128)].astype(F32)
        r.G1[bb, :, :, pl.ds(LO, 128)] = head.astype(BF16)
        r.G1[bb, :, :, pl.ds(384, D - 384)] = t[:, :, 128:].astype(BF16)

    for d in (*far, 0):
        if d:
            pl.when(z + d < nz)(lambda: qkv_block(2 * (z + d) + (1 - y)))
            pl.when(z - d >= 0)(lambda: qkv_block(2 * (z - d) + (1 - y)))
        else:
            qkv_block(2 * z + (1 - y))
        s_far[0](d)
        s_own[0](d)
    for k in range(nz):
        qkv_block(2 * k + y)

    for p in range(2):
        w = W1[:, :, :, pl.ds(LO, D - LO)].reshape(D, D - LO)
        to_sibling(3, p, nt(r.DQ[rows_of(p)], w))
    s_up[1](0)
    arrive(lambda: xcopy(2, 0))
    own_out = r.PF2[...] + r.XR[4].astype(F32)
    mixed_o[...] = (r.MID[x] + own_out + bias_down).astype(BF16)
    r.XS[5] = chip_sum(3, 1 - x).astype(BF16)
    send(lambda: xcopy(3, 0))
    r.PF2[...] = chip_sum(3, x)
    s_out[1](2)
    s_dn[1](2)
    if nz > 3:
        s_far[1](3)
        s_own[1](3)
    s_out[1](1)
    s_dn[1](1)

    arrive(lambda: xcopy(3, 0))
    dh = r.PF2[...] + r.XR[5].astype(F32)
    xv = r.X[s].astype(F32)
    inv = lax.rsqrt(jnp.mean(xv * xv, axis=1, keepdims=True) + epsilon)
    n = xv * inv
    dn = dh * gain_attn
    gtok_o[...] = r.DMID[x] + inv * (dn - n * jnp.mean(dn * n, axis=1, keepdims=True))
    r.SGA[0:1] = jnp.sum(dh * n, axis=0, keepdims=True)
    r.SGA[2:3] = jnp.sum(r.DY[s].astype(F32), axis=0, keepdims=True)
    s_out[1](0)
    m_gy = lambda: copy(
        r.G2.at[z, :, pl.ds(0, D)], r.YR2.at[z, :, pl.ds(0, D)], r.s_one.at[14 + 1], r.r_one.at[14 + 1], yp
    )
    send(m_gy, not_mine)

    def small_copy(k, slot, dev):
        return lambda: copy(r.SGA if k == 0 else r.SGS.at[k - 1], r.SGR.at[slot], r.s_sg.at[slot], r.r_sg.at[slot], dev)

    total = r.SGA[...]
    for k, dev in enumerate((sib, xp, yp)):
        mk = small_copy(k, k, dev)
        send(mk)
        if k == 1:
            s_far[1](2)
            s_own[1](2)
            s_dn[1](0)
        arrive(mk)
        total = total + r.SGR[k]
        r.SGS[k] = total
    mks = []
    for k in range(1, nz):
        mk = small_copy(3, 2 + k, (2 * lax.rem(z + k, nz) + y, s))
        send(mk)
        mks.append(mk)
    s_far[1](1)
    s_own[1](1)
    s_far[1](0)

    m_fx = lambda: copy(r.G1.at[b, 1 - x], r.FX, r.s_one.at[11], r.r_one.at[11], xp)
    send(m_fx)
    arrive(m_gy, mine)

    def out_from_y():
        cut = pl.ds(0, D)
        r.G2[z, :, cut] = (r.G2[z, :, cut].astype(F32) + r.YR2[z, :, cut].astype(F32)).astype(BF16)

    when(mine, out_from_y)
    done2 = r.G2[z].astype(F32)
    r.GF2[0] = done2[:RW]
    r.GF2[1] = done2[RW:]
    m_g2 = lambda: copy(r.GF2.at[1 - c], r.GR2, r.s_one.at[12], r.r_one.at[12], sib)
    send(m_g2, mine)
    s_own[1](0)
    own = r.G1[b, x].astype(F32)
    r.GF[0, x] = own[:RW]
    r.GF[1, x] = own[RW:]
    for k, mk in enumerate(mks):
        arrive(mk)
        total = total + r.SGR[3 + k]
    sg_o[...] = total
    arrive(m_g2, not_mine)

    def out2_own():
        o2[...] = r.GF2[c]

    def out2_sib():
        o2[...] = r.GR2[...]

    when(mine, out2_own)
    when(not_mine, out2_sib)
    arrive(m_fx)
    other = r.FX[...].astype(F32)
    r.GF[0, 1 - x] = other[:RW]
    r.GF[1, 1 - x] = other[RW:]
    m_gf = lambda: copy(r.GF.at[1 - c], r.GRV, r.s_one.at[13], r.r_one.at[13], sib)
    send(m_gf)
    o1[:, c] = r.GF[c]
    arrive(m_gf)
    o1[:, 1 - c] = r.GRV[...]

    for make, cond in drains:
        when(cond, lambda make=make: make().wait_send())


def fused_layer(nb, ns, tokens, wqkv, wout, wup, wdown, gattn, gffn, bup, bdown, scale_param, cot):
    nz = nb // 2
    rows, D = wout.shape
    T = tokens.shape[1]
    L = ns * T
    V = pltpu.VMEM
    scratch = dict(
        WQ=V((rows, 3 * D), BF16),
        WU=V((rows, D), BF16),
        WO=V((rows, D), BF16),
        WD=V((rows, D), BF16),
        SM=V((8, 128), F32),
        W1P=V((2, 2, 48, D), BF16),
        W2P=V((48, 2 * D), BF16),
        SIB1=V((2, 48, D), BF16),
        SIB2=V((48, 2 * D), BF16),
        CB1=V((HD, D), BF16),
        W1=V((nb, 2, HD, D), BF16),
        W2=V((nz, HD, 2 * D), BF16),
        S=V((nb, 4, 8, 128), F32),
        X=V((4, T, D), BF16),
        DY=V((4, T, D), BF16),
        ROWS=V((8, D), F32),
        BUP=V((8, 4 * HD), F32),
        HN1=V((L, D), BF16),
        HN1T=V((nb, 2 * HD, L), BF16),
        HN2T=V((nb, 2 * HD, L), BF16),
        QKV=V((L, D - 256), F32),
        QRAW=V((4, L, HD), F32),
        QH=V((4, L, HD), BF16),
        KH=V((4, L, HD), BF16),
        VH=V((4, L, HD), BF16),
        KT=V((4, HD, L), BF16),
        VT=V((4, HD, L), BF16),
        PT0=V((4, L // 2, L // 2), BF16),
        PT1=V((4, L, L // 2), BF16),
        OT=V((4, HD, L), F32),
        OB=V((L, 4 * HD), BF16),
        PF=V((2, 2, T, D), F32),
        PF2=V((T, D), F32),
        ES=V((4, 2, T, D), BF16),
        ER=V((4, 2, T, D), BF16),
        XS=V((6, T, D), BF16),
        XR=V((6, T, D), BF16),
        MID=V((2, T, D), F32),
        HN2=V((4, T, D), BF16),
        ACT=V((L, 4 * HD), BF16),
        DUP=V((L, 384), BF16),
        DA=V((4, T, D), BF16),
        DMID=V((2, T, D), F32),
        DQ=V((L, D - 256), BF16),
        DKA=V((4, L // 2, HD), F32),
        DVA=V((4, L // 2, HD), F32),
        G1=V((nb, 2, HD, D), BF16),
        G2=V((nz, HD, 2 * D), BF16),
        YR1=V((nz, 2, HD, D), BF16),
        ZU1=V((nz - 1, 2, HD, D), BF16),
        ZD1=V((nz - 1, 2, HD, D), BF16),
        YR2=V((nz, HD, 2 * D), BF16),
        ZU2=V((nz - 1, HD, 2 * D), BF16),
        ZD2=V((nz - 1, HD, 2 * D), BF16),
        FX=V((HD, D), BF16),
        GF=V((2, 2, rows, D), F32),
        GRV=V((2, rows, D), F32),
        GF2=V((2, rows, 2 * D), F32),
        GR2=V((rows, 2 * D), F32),
        SGA=V((8, D), F32),
        SGS=V((3, 8, D), F32),
        SGR=V((2 + nz, 8, D), F32),
    )
    dma = pltpu.SemaphoreType.DMA
    scratch.update(
        s_in=dma((6,)),
        s_one=dma((16,)), r_one=dma((16,)),
        s_up=dma((6, nz)), r_up=dma((6, nz)),
        s_dn=dma((6, nz)), r_dn=dma((6, nz)),
        s_y=dma((6, nz)), r_y=dma((6, nz)),
        s_e=dma((4, 2)), r_e=dma((4, 2)),
        s_x=dma((6,)), r_x=dma((6,)),
        s_h=dma((2, 2)), r_h=dma((2, 2)),
        s_ry=dma((5, nz)), r_ry=dma((5, nz)),
        s_ru=dma((5, nz)), r_ru=dma((5, nz)),
        s_rd=dma((5, nz)), r_rd=dma((5, nz)),
        s_sg=dma((2 + nz,)), r_sg=dma((2 + nz,)),
    )
    vmem = pl.BlockSpec(memory_space=pltpu.VMEM)
    hbm = pl.BlockSpec(memory_space=pl.ANY)
    mixed, gtok, o1, o2, sg = pl.pallas_call(
        functools.partial(layer_kernel, nz, tuple(scratch)),
        out_shape=(
            jax.ShapeDtypeStruct((T, D), BF16),
            jax.ShapeDtypeStruct((T, D), F32),
            jax.ShapeDtypeStruct((2, 2, rows, D), F32),
            jax.ShapeDtypeStruct((rows, 2 * D), F32),
            jax.ShapeDtypeStruct((8, D), F32),
        ),
        in_specs=[hbm] * 6 + [vmem] * 5,
        out_specs=(vmem,) * 5,
        scratch_shapes=list(scratch.values()),
        compiler_params=pltpu.CompilerParams(
            collective_id=0, has_side_effects=True, vmem_limit_bytes=63 << 20
        ),
        name="decoder_layer",
    )(tokens[0], cot[0], wqkv, wout, wup, wdown, gattn, gffn, bup, bdown, scale_param)
    mixed, gtok, gqkv, gout, gup, gdown, g_attn, g_ffn, g_bup, g_bdown, gscale = pl.pallas_call(
        functools.partial(outputs_kernel, ns),
        out_shape=(
            jax.ShapeDtypeStruct((T, D), BF16),
            jax.ShapeDtypeStruct((T, D), F32),
            jax.ShapeDtypeStruct((rows, 3 * D), F32),
            jax.ShapeDtypeStruct((rows, D), F32),
            jax.ShapeDtypeStruct((rows, D), F32),
            jax.ShapeDtypeStruct((rows, D), F32),
            jax.ShapeDtypeStruct((rows,), F32),
            jax.ShapeDtypeStruct((rows,), F32),
            jax.ShapeDtypeStruct((rows,), F32),
            jax.ShapeDtypeStruct((rows,), F32),
            jax.ShapeDtypeStruct((HD,), F32),
        ),
        in_specs=[vmem] * 6,
        out_specs=(vmem,) * 11,
        compiler_params=pltpu.CompilerParams(vmem_limit_bytes=63 << 20),
        name="place_outputs",
    )(mixed, gtok, o1, o2, sg, scale_param)
    return mixed[None], gtok[None], gqkv, gout, gup, gdown, g_attn, g_ffn, g_bup, g_bdown, gscale


def outputs_kernel(ns, mixed, gtok, o1, o2, sg, scl, mixed_o, gtok_o, gqkv, gout, gup, gdown, *small):
    rows, D = gup.shape
    HW = 4 * HD
    mixed_o[...] = mixed[...]
    gtok_o[...] = gtok[...]
    gout[...] = o2[:, 0:D]
    gdown[...] = o2[:, D : 2 * D]
    for xx in range(2):
        for cc in range(2):
            for t in range(4):
                for j in range(4):
                    v = o1[xx, cc, :, HW * t + HD * j : HW * t + HD * (j + 1)]
                    at = HD * (4 * j + 2 * cc + xx)
                    if t == 0:
                        gup[:, at : at + HD] = v
                    else:
                        gqkv[:, D * (t - 1) + at : D * (t - 1) + at + HD] = v
    first = (lax.axis_index("batch") * ns + lax.axis_index("seq")) * rows
    parts = []
    for h in range(H):
        j, cc, xx = h // 4, (h // 2) % 2, h % 2
        row = 4 + 2 * xx + cc
        parts.append(sg[row : row + 1, HD * j : HD * (j + 1)])
    bias_up = jnp.concatenate(parts, axis=1)
    shift = lax.rem(D - first, D)
    for ref, v in zip(small, (sg[0:1], sg[1:2], bias_up, sg[2:3])):
        v = jnp.broadcast_to(v, (8, D))
        ref[...] = pltpu.roll(v, shift, 1)[0, 0:rows]
    scale = scl[...].astype(F32).reshape(1, HD)
    small[4][...] = (sg[3:4, 0:HD] * (soft_unit / math.sqrt(HD)) / (1.0 + jnp.exp(-scale)))[0]


def layer_step(nb, ns, *args):
    if fits_fused(nb, ns, args[0], args[1], args[3]):
        return fused_layer(nb, ns, *args)
    return generic_layer(*args)


def solution(mesh):
    return jax.shard_map(
        functools.partial(layer_step, mesh.shape["batch"], mesh.shape["seq"]),
        mesh=mesh,
        in_specs=(
            P("batch", "seq", None),
            P(("batch", "seq"), None),
            P(("batch", "seq"), None),
            P(("batch", "seq"), None),
            P(("batch", "seq"), None),
            P(("batch", "seq")),
            P(("batch", "seq")),
            P(("batch", "seq")),
            P(("batch", "seq")),
            P(),
            P("batch", "seq", None),
        ),
        out_specs=(
            P("batch", "seq", None),
            P("batch", "seq", None),
            P(("batch", "seq"), None),
            P(("batch", "seq"), None),
            P(("batch", "seq"), None),
            P(("batch", "seq"), None),
            P(("batch", "seq")),
            P(("batch", "seq")),
            P(("batch", "seq")),
            P(("batch", "seq")),
            P(),
        ),
        check_vma=False,
    )
```

```python
import functools
import math
import types

import jax
import jax.numpy as jnp
from jax import lax
from jax.experimental import pallas as pl
from jax.experimental.pallas import tpu as pltpu
from jax.sharding import PartitionSpec as P

H = 16
HD = 80


epsilon = 1e-06
soft_unit = 1.442695041
neg_large = -1e30


def norm_forward(values, gain):
    inverse = lax.rsqrt(jnp.mean(values * values, axis=1, keepdims=True) + epsilon)
    return (inverse, (values * inverse * gain.astype(jnp.float32)).astype(jnp.bfloat16))


def norm_back(grad_out, values, inverse, gain):
    normed = values * inverse
    scaled = grad_out * gain.astype(jnp.float32)
    grad_gain = jnp.sum(grad_out * normed, axis=0)
    grad_in = inverse * (scaled - normed * jnp.mean(scaled * normed, axis=1, keepdims=True))
    return (grad_in, grad_gain)


def generic_layer(
    tokens,
    query_key_value_weight,
    attention_output_weight,
    up_projection_weight,
    down_projection_weight,
    gain_attn,
    gain_ffn,
    up_projection_bias,
    down_projection_bias,
    scale_param,
    cotangent,
):
    seq_local, tok_seq, width = tokens.shape
    row_count = seq_local * tok_seq
    shards = (
        query_key_value_weight,
        attention_output_weight,
        up_projection_weight,
        down_projection_weight,
        gain_attn,
        gain_ffn,
        up_projection_bias,
        down_projection_bias,
    )
    fwd_weights = (
        lax.all_gather(shards[0], ("batch", "seq"), axis=0, tiled=True),
        lax.all_gather(shards[1], ("batch", "seq"), axis=0, tiled=True),
        lax.all_gather(shards[2], ("batch", "seq"), axis=0, tiled=True),
        lax.all_gather(shards[3], ("batch", "seq"), axis=0, tiled=True),
        lax.all_gather(shards[4], ("batch", "seq"), axis=0, tiled=True),
        lax.all_gather(shards[5], ("batch", "seq"), axis=0, tiled=True),
        lax.all_gather(shards[6], ("batch", "seq"), axis=0, tiled=True),
        lax.all_gather(shards[7], ("batch", "seq"), axis=0, tiled=True),
    )
    wqkv_full, wout_full, wup_full, wdown_full, gattn_full, gffn_full, bup_full, bdown_full = (
        fwd_weights
    )
    inputs = tokens.astype(jnp.float32).reshape(row_count, width)
    inv_attn, attention_normed_input = norm_forward(inputs, gattn_full)
    query_key_value = jnp.dot(attention_normed_input, wqkv_full, preferred_element_type=jnp.float32)
    q_raw = query_key_value[:, :width]
    scale_float = scale_param.astype(jnp.float32)
    factor = soft_unit / math.sqrt(HD) * jax.nn.softplus(scale_float)
    factor_row = jnp.tile(factor, H)
    queries = (q_raw * factor_row).astype(jnp.bfloat16)
    keys_own = (
        query_key_value[:, width : 2 * width]
        .astype(jnp.bfloat16)
        .reshape(seq_local, tok_seq, width)
    )
    values_own = (
        query_key_value[:, 2 * width :].astype(jnp.bfloat16).reshape(seq_local, tok_seq, width)
    )
    keys_all, values_all = (
        lax.all_gather(keys_own, "seq", axis=1, tiled=True),
        lax.all_gather(values_own, "seq", axis=1, tiled=True),
    )
    position = lax.axis_index("seq")
    block_total = lax.axis_size("seq")
    query_pos = position * tok_seq + jnp.arange(tok_seq, dtype=jnp.int32)
    key_offsets = jnp.arange(tok_seq, dtype=jnp.int32)
    queries_h = queries.reshape(seq_local, tok_seq, H, HD)

    def key_block(source, block):
        piece = lax.dynamic_slice_in_dim(source, block * tok_seq, tok_seq, 1)
        return piece.reshape(seq_local, tok_seq, H, HD)

    def block_scores(block):
        scores = jnp.einsum(
            "sqhd,skhd->shqk",
            queries_h,
            key_block(keys_all, block),
            preferred_element_type=jnp.float32,
        )
        allowed = (block * tok_seq + key_offsets)[None, :] <= query_pos[:, None]
        return jnp.where(allowed, scores, neg_large)

    def max_step(block, carry):
        top, total = carry
        scores = block_scores(block)
        new_top = jnp.maximum(top, jnp.max(scores, axis=3, keepdims=True))
        total = total * jnp.exp(top - new_top) + jnp.sum(
            jnp.exp(scores - new_top), axis=3, keepdims=True
        )
        return (new_top, total)

    start_top = jnp.full((seq_local, H, tok_seq, 1), neg_large, jnp.float32)
    top, total = lax.fori_loop(0, block_total, max_step, (start_top, jnp.zeros_like(start_top)))
    log_sum = top + jnp.log(total)

    def value_step(block, accum):
        probs = jnp.exp(block_scores(block) - log_sum).astype(jnp.bfloat16)
        return accum + jnp.einsum(
            "shqk,skhd->sqhd",
            probs,
            key_block(values_all, block),
            preferred_element_type=jnp.float32,
        )

    attention_output = lax.fori_loop(
        0, block_total, value_step, jnp.zeros((seq_local, tok_seq, H, HD), jnp.float32)
    )
    attention_output = attention_output.reshape(row_count, width)
    att_low = attention_output.astype(jnp.bfloat16)
    middle = inputs + jnp.dot(att_low, wout_full, preferred_element_type=jnp.float32)
    inv_ffn, feedforward_normed_input = norm_forward(middle, gffn_full)
    up_projected_value = jnp.dot(
        feedforward_normed_input, wup_full, preferred_element_type=jnp.float32
    ) + bup_full.astype(jnp.float32)
    act_low = jax.nn.silu(up_projected_value).astype(jnp.bfloat16)
    result = (
        middle
        + jnp.dot(act_low, wdown_full, preferred_element_type=jnp.float32)
        + bdown_full.astype(jnp.float32)
    )
    mixed = result.astype(jnp.bfloat16).reshape(seq_local, tok_seq, width)
    back_weights = (
        lax.all_gather(shards[0], ("batch", "seq"), axis=0, tiled=True),
        lax.all_gather(shards[1], ("batch", "seq"), axis=0, tiled=True),
        lax.all_gather(shards[2], ("batch", "seq"), axis=0, tiled=True),
        lax.all_gather(shards[3], ("batch", "seq"), axis=0, tiled=True),
        lax.all_gather(shards[4], ("batch", "seq"), axis=0, tiled=True),
        lax.all_gather(shards[5], ("batch", "seq"), axis=0, tiled=True),
        lax.all_gather(shards[6], ("batch", "seq"), axis=0, tiled=True),
        lax.all_gather(shards[7], ("batch", "seq"), axis=0, tiled=True),
    )
    wqkv_back, wout_back, wup_back, wdown_back, gattn_back, gffn_back, bup_back, bdown_back = (
        back_weights
    )
    grad_low = cotangent.reshape(row_count, width)
    grad_float = grad_low.astype(jnp.float32)
    grad_down = jnp.einsum("rf,rd->fd", act_low, grad_low, preferred_element_type=jnp.float32)
    grad_bias_down = jnp.sum(grad_float, axis=0)
    grad_act = jnp.einsum("rd,fd->rf", grad_low, wdown_back, preferred_element_type=jnp.float32)
    sigma = jax.nn.sigmoid(up_projected_value)
    grad_upv = (grad_act * sigma * (1.0 + up_projected_value * (1.0 - sigma))).astype(jnp.bfloat16)
    grad_up = jnp.einsum(
        "rd,rf->df", feedforward_normed_input, grad_upv, preferred_element_type=jnp.float32
    )
    grad_bias_up = jnp.sum(grad_upv.astype(jnp.float32), axis=0)
    grad_hn_ffn = jnp.einsum("rf,df->rd", grad_upv, wup_back, preferred_element_type=jnp.float32)
    grad_norm_ffn, grad_gain_ffn = norm_back(grad_hn_ffn, middle, inv_ffn, gffn_back)
    grad_middle = grad_float + grad_norm_ffn
    grad_attn = grad_middle.astype(jnp.bfloat16)
    grad_out = jnp.einsum("rd,re->de", att_low, grad_attn, preferred_element_type=jnp.float32)
    block_summed = (
        lax.psum_scatter(grad_out, ("batch", "seq"), scatter_dimension=0, tiled=True),
        lax.psum_scatter(grad_up, ("batch", "seq"), scatter_dimension=0, tiled=True),
        lax.psum_scatter(grad_down, ("batch", "seq"), scatter_dimension=0, tiled=True),
        lax.psum_scatter(grad_gain_ffn, ("batch", "seq"), scatter_dimension=0, tiled=True),
        lax.psum_scatter(grad_bias_up, ("batch", "seq"), scatter_dimension=0, tiled=True),
        lax.psum_scatter(grad_bias_down, ("batch", "seq"), scatter_dimension=0, tiled=True),
    )
    grad_att_low = jnp.einsum(
        "re,de->rd", grad_attn, wout_back, preferred_element_type=jnp.float32
    ).astype(jnp.bfloat16)
    grad_heads = grad_att_low.reshape(seq_local, tok_seq, H, HD)
    delta = jnp.sum(
        (grad_att_low.astype(jnp.float32) * attention_output).reshape(seq_local, tok_seq, H, HD),
        axis=3,
    )
    delta = jnp.transpose(delta, (0, 2, 1))[..., None]
    query_init = jnp.zeros((seq_local, tok_seq, H, HD), jnp.float32)

    def grad_step(block, carry):
        grad_query, term = carry
        scores = block_scores(block)
        probs = jnp.exp(scores - log_sum)
        keys_blk = key_block(keys_all, block)
        values_blk = key_block(values_all, block)
        grad_probs = jnp.einsum(
            "sqhd,skhd->shqk", grad_heads, values_blk, preferred_element_type=jnp.float32
        )
        grad_scores = (probs * (grad_probs - delta)).astype(jnp.bfloat16)
        grad_values = jnp.einsum(
            "shqk,sqhd->skhd",
            probs.astype(jnp.bfloat16),
            grad_heads,
            preferred_element_type=jnp.float32,
        )
        grad_keys = jnp.einsum(
            "shqk,sqhd->skhd", grad_scores, queries_h, preferred_element_type=jnp.float32
        )
        grad_query = grad_query + jnp.einsum(
            "shqk,skhd->sqhd", grad_scores, keys_blk, preferred_element_type=jnp.float32
        )
        piece = jnp.concatenate(
            [
                grad_keys.reshape(seq_local, tok_seq, width),
                grad_values.reshape(seq_local, tok_seq, width),
            ],
            axis=2,
        )
        term = lax.dynamic_update_slice_in_dim(term, piece, block * tok_seq, 1)
        return (grad_query, term)

    term_init = jnp.zeros((seq_local, tok_seq * block_total, 2 * width), jnp.float32)
    grad_query, term = lax.fori_loop(0, block_total, grad_step, (query_init, term_init))
    kv_grads = lax.psum_scatter(
        term.astype(jnp.bfloat16), "seq", scatter_dimension=1, tiled=True
    ).astype(jnp.float32)
    grad_scaled = grad_query.reshape(row_count, width)
    scale_local = jnp.sum((grad_scaled * q_raw).reshape(row_count, H, HD), axis=(0, 1))
    scale_total = lax.psum(scale_local, ("batch", "seq"))
    grad_scale = scale_total * (soft_unit / math.sqrt(HD)) * jax.nn.sigmoid(scale_float)
    grad_qkv_low = jnp.concatenate(
        [grad_scaled * factor_row, kv_grads.reshape(row_count, 2 * width)], axis=1
    ).astype(jnp.bfloat16)
    grad_qkv = jnp.einsum(
        "rd,re->de", attention_normed_input, grad_qkv_low, preferred_element_type=jnp.float32
    )
    grad_hn_attn = jnp.einsum(
        "re,de->rd", grad_qkv_low, wqkv_back, preferred_element_type=jnp.float32
    )
    grad_norm_attn, grad_gain_attn = norm_back(grad_hn_attn, inputs, inv_attn, gattn_back)
    grad_tokens = (grad_middle + grad_norm_attn).reshape(seq_local, tok_seq, width)
    qkv_summed = (
        lax.psum_scatter(grad_qkv, ("batch", "seq"), scatter_dimension=0, tiled=True),
        lax.psum_scatter(grad_gain_attn, ("batch", "seq"), scatter_dimension=0, tiled=True),
    )
    return (
        mixed,
        grad_tokens,
        qkv_summed[0],
        block_summed[0],
        block_summed[1],
        block_summed[2],
        qkv_summed[1],
        block_summed[3],
        block_summed[4],
        block_summed[5],
        grad_scale,
    )


MESH = pl.DeviceIdType.MESH
F32 = jnp.float32
BF16 = jnp.bfloat16


def fits_fused(nb, ns, tokens, wqkv, wup):
    rows, width = wup.shape[0], wup.shape[1]
    return (
        ns == 4
        and nb % 2 == 0
        and tokens.shape == (1, 128, H * HD)
        and width == H * HD
        and 2 * rows == HD
        and nb * ns * rows == width
        and wqkv.shape == (rows, 3 * width)
    )


def nt(a, b):
    return lax.dot_general(a, b, (((1,), (1,)), ((), ())), preferred_element_type=F32)


def nn(a, b):
    return lax.dot_general(a, b, (((1,), (0,)), ((), ())), preferred_element_type=F32)


def tn(a, b):
    return lax.dot_general(a, b, (((0,), (0,)), ((), ())), preferred_element_type=F32)


def layer_kernel(nz, scratch_names, tok, cot, wqkv, wout, wup, wdown, ga, gf, bu, bd, scl, *refs):
    mixed_o, gtok_o, o1, o2, sg_o = refs[:5]
    r = types.SimpleNamespace(**dict(zip(scratch_names, refs[5:])))
    D = tok.shape[1]
    T = tok.shape[0]
    L = 4 * T
    HP = 2 * T
    NH = 4
    HW = NH * HD
    CB = HD
    RW = HD // 2
    LO = 256
    b = lax.axis_index("batch")
    s = lax.axis_index("seq")
    z, y = b // 2, b % 2
    x, c = s // 2, s % 2
    sib = (b, 2 * x + (1 - c))
    xp = (b, 2 * (1 - x) + c)
    yp = (2 * z + (1 - y), s)
    zup = (lax.rem(2 * (z + 1), 2 * nz) + y, s)
    zdn = (lax.rem(2 * (z + nz - 1), 2 * nz) + y, s)
    drains = []

    def when(cond, fn):
        if cond is None:
            fn()
        else:
            pl.when(cond)(fn)

    def both(p, q):
        if p is None:
            return q
        if q is None:
            return p
        return jnp.logical_and(p, q)

    def copy(src, dst, ssem, rsem, dev):
        return pltpu.make_async_remote_copy(
            src_ref=src, dst_ref=dst, send_sem=ssem, recv_sem=rsem, device_id=dev, device_id_type=MESH
        )

    def send(make, cond=None):
        when(cond, lambda: make().start())
        drains.append((make, cond))

    def arrive(make, cond=None):
        when(cond, lambda: make().wait_recv())

    bar = pltpu.get_barrier_semaphore()
    peers = [sib, xp, yp]
    for k in range(1, nz):
        peers.append((2 * lax.rem(z + k, nz) + y, s))
    for dev in peers:
        pl.semaphore_signal(bar, inc=1, device_id=dev, device_id_type=MESH)
    fetches = [
        pltpu.make_async_copy(src, dst, r.s_in.at[k])
        for k, (src, dst) in enumerate(
            (
                (wqkv, r.WQ),
                (wup, r.WU),
                (wout, r.WO),
                (wdown, r.WD),
                (tok, r.X.at[s]),
                (cot, r.DY.at[s]),
            )
        )
    ]
    for f in fetches:
        f.start()
    small_rows = [v[...].astype(F32).reshape(1, RW) for v in (ga, gf, bu, bd)]
    r.SM[...] = jnp.zeros_like(r.SM)
    for k, row in enumerate(small_rows):
        r.SM[k : k + 1, 0:RW] = row
    fetches[0].wait()
    fetches[1].wait()

    def pieces(cc):
        for xx in range(2):
            for t in range(4):
                for j in range(NH):
                    src = HD * (4 * j + 2 * cc + xx)
                    v = r.WU[:, src : src + HD] if t == 0 else r.WQ[:, D * (t - 1) + src : D * (t - 1) + src + HD]
                    r.W1P[cc, xx, 0:RW, HW * t + HD * j : HW * t + HD * (j + 1)] = v

    pieces(0)
    pieces(1)
    pl.semaphore_wait(bar, len(peers))

    m_sib1 = lambda: copy(r.W1P.at[1 - c], r.SIB1, r.s_one.at[0], r.r_one.at[0], sib)
    m_ssib = lambda: copy(r.SM, r.S.at[b, s], r.s_one.at[1], r.r_one.at[1], sib)
    m_sib2 = lambda: copy(r.W2P, r.SIB2, r.s_one.at[2], r.r_one.at[2], sib)
    send(m_ssib)
    send(m_sib1)
    fetches[2].wait()
    fetches[3].wait()
    r.W2P[0:RW, 0:D] = r.WO[...]
    r.W2P[0:RW, D : 2 * D] = r.WD[...]
    send(m_sib2)
    r.S[b, s] = r.SM[...]

    def chip_rows(own, other):
        own, other = own[:RW].astype(F32), other[:RW].astype(F32)
        lo = jnp.where(c == 0, own, other)
        hi = jnp.where(c == 0, other, own)
        return jnp.concatenate([lo, hi], axis=0).astype(BF16)

    m_ssib_r = lambda: copy(r.SM, r.S.at[b, 2 * x + (1 - c)], r.s_one.at[1], r.r_one.at[1], sib)
    arrive(m_ssib_r)
    m_xs = lambda: copy(
        r.S.at[b, pl.ds(2 * x, 2)], r.S.at[b, pl.ds(2 * x, 2)], r.s_one.at[4], r.r_one.at[4], xp
    )
    send(m_xs)
    arrive(m_sib1)
    r.CB1[...] = chip_rows(r.W1P[c, 1 - x], r.SIB1[1 - x])
    half = (D - LO) // 2
    cuts = (pl.ds(LO, half), pl.ds(LO + half, half), pl.ds(0, LO))

    def m_x1(k, xx):
        return copy(r.CB1.at[:, cuts[k]], r.W1.at[b, xx, :, cuts[k]], r.s_x1.at[k], r.r_x1.at[k], xp)

    for k in range(3):
        send(lambda k=k: m_x1(k, x))
    r.W1[b, x] = chip_rows(r.W1P[c, x], r.SIB1[x])

    def gather_item(idx, block, zcond, passes_y=True):
        up = lambda zz: copy(block(zz, y), block(zz, y), r.s_up.at[idx, zz], r.r_up.at[idx, zz], zup)
        dn = lambda zz: copy(block(zz, y), block(zz, y), r.s_dn.at[idx, zz], r.r_dn.at[idx, zz], zdn)
        yy = lambda zz: copy(block(zz, y), block(zz, y), r.s_y.at[idx, zz], r.r_y.at[idx, zz], yp)

        def start():
            send(lambda: up(z), both(zcond, z < nz - 1))
            send(lambda: dn(z), both(zcond, z > 0))
            if passes_y:
                send(lambda: yy(z), zcond)

        def step(d):
            lo, hi = z - d, z + d
            below, above = both(zcond, lo >= 0), both(zcond, hi < nz)
            arrive(lambda: up(lo), below)
            send(lambda: up(lo), both(below, z < nz - 1))
            arrive(lambda: dn(hi), above)
            send(lambda: dn(hi), both(above, z > 0))
            if passes_y:
                send(lambda: yy(lo), below)
                send(lambda: yy(hi), above)

        def finish():
            if passes_y:
                for k in range(nz):
                    when(
                        None if zcond is None else jnp.logical_not(zcond),
                        lambda k=k: copy(
                            block(k, 1 - y), block(k, 1 - y), r.s_y.at[idx, k], r.r_y.at[idx, k], yp
                        ).wait_recv(),
                    )

        return start, step, finish

    mine = c == y
    not_mine = c != y
    g_s = gather_item(0, lambda zz, q: r.S.at[2 * zz + q], None)
    g_own = [gather_item(1 + k, lambda zz, q, k=k: r.W1.at[2 * zz + q, x, :, cuts[k]], None) for k in range(2)]
    g_oth = [
        gather_item(3 + k, lambda zz, q, k=k: r.W1.at[2 * zz + q, 1 - x, :, cuts[k]], None) for k in range(2)
    ]
    g_out = gather_item(5, lambda zz, q: r.W2.at[zz, :, pl.ds(0, D)], None, False)
    g_up = gather_item(6, lambda zz, q: r.W1.at[2 * zz + q, :, :, pl.ds(0, LO)], None)
    g_dn = gather_item(7, lambda zz, q: r.W2.at[zz, :, pl.ds(D, D)], mine)

    g_own[0][0]()
    g_own[1][0]()
    m_xs_r = lambda: copy(
        r.S.at[b, pl.ds(2 - 2 * x, 2)],
        r.S.at[b, pl.ds(2 - 2 * x, 2)],
        r.s_one.at[4],
        r.r_one.at[4],
        xp,
    )
    arrive(m_xs_r)
    g_s[0]()
    fetches[4].wait()
    fetches[5].wait()
    own_tok, own_cot = r.X.at[s], r.DY.at[s]
    m_xt = lambda: copy(own_tok, own_tok, r.s_one.at[5], r.r_one.at[5], xp)
    m_st = lambda: copy(own_tok, own_tok, r.s_one.at[6], r.r_one.at[6], sib)
    m_xc = lambda: copy(own_cot, own_cot, r.s_one.at[7], r.r_one.at[7], xp)
    m_sc = lambda: copy(own_cot, own_cot, r.s_one.at[8], r.r_one.at[8], sib)
    send(m_xt)
    send(m_st)
    send(m_xc)
    send(m_sc)
    arrive(m_sib2)

    def fill_w2():
        r.W2[z] = chip_rows(r.W2P[...], r.SIB2[...])

    when(mine, fill_w2)
    m_y2 = lambda: copy(
        r.W2.at[z, :, pl.ds(0, D)], r.W2.at[z, :, pl.ds(0, D)], r.s_one.at[14], r.r_one.at[14], yp
    )
    sx = 2 * (1 - x) + c
    so = 2 * (1 - x) + (1 - c)
    ss = 2 * x + (1 - c)
    fwd = lambda name, k, src_i: copy(
        name.at[src_i], name.at[src_i], r.s_one.at[k], r.r_one.at[k], sib
    )
    arrive(lambda: m_x1(0, 1 - x))
    g_oth[0][0]()
    g_own[0][1](1)
    arrive(lambda: m_x1(1, 1 - x))
    g_oth[1][0]()
    send(m_y2, mine)
    g_own[1][1](1)
    g_s[1](1)
    arrive(lambda: m_x1(2, 1 - x))
    g_oth[0][1](1)
    g_oth[1][1](1)
    g_own[0][1](2)
    g_own[1][1](2)
    g_s[1](2)
    arrive(lambda: copy(own_tok, r.X.at[sx], r.s_one.at[5], r.r_one.at[5], xp))
    send(lambda: fwd(r.X, 9, sx))
    g_oth[0][1](2)
    arrive(m_y2, not_mine)
    g_out[0]()
    g_oth[1][1](2)
    for d in range(3, nz):
        g_own[0][1](d)
        g_own[1][1](d)
        g_s[1](d)
        g_oth[0][1](d)
        g_oth[1][1](d)
    arrive(lambda: copy(own_tok, r.X.at[ss], r.s_one.at[6], r.r_one.at[6], sib))
    arrive(lambda: fwd(r.X, 9, so))
    arrive(lambda: copy(own_cot, r.DY.at[sx], r.s_one.at[7], r.r_one.at[7], xp))
    send(lambda: fwd(r.DY, 10, sx))
    arrive(lambda: copy(own_cot, r.DY.at[ss], r.s_one.at[8], r.r_one.at[8], sib))
    g_out[1](1)
    g_s[2]()
    arrive(lambda: fwd(r.DY, 10, so))

    jf = lax.broadcasted_iota(jnp.int32, (1, D), 1).astype(F32)
    jk = jnp.floor((jf + 0.5) / RW)
    jl = jf - RW * jk
    pick = (lax.broadcasted_iota(jnp.int32, (128, D), 0).astype(F32) == jl).astype(BF16)
    sm_rows = 2 * nz * 4
    spread = nn(r.S[...].reshape(sm_rows * 8, 128).astype(BF16), pick)
    spread = spread.reshape(sm_rows, 8, D)
    owner = lax.broadcasted_iota(jnp.int32, (sm_rows, 8, D), 0).astype(F32)
    r.ROWS[...] = jnp.sum(jnp.where(owner == jk[None], spread, 0.0), axis=0)
    uf = jf[:, :HW]
    uj = jnp.floor((uf + 0.5) / HD)
    uh = jnp.floor((uf - HD * uj + 0.5) / RW)
    base = (2 * c + x).astype(F32)
    uk = 2.0 * (4.0 * uj + base) + uh
    r.BUP[...] = jnp.sum(
        jnp.where(owner[:, :, :HW] == uk[None], spread[:, :, :HW], 0.0), axis=0
    )
    gain_attn = r.ROWS[0:1]
    gain_ffn = r.ROWS[1:2]
    bias_down = r.ROWS[3:4]
    bias_up = r.BUP[2:3]
    scale = scl[...].astype(F32).reshape(1, HD)
    factor = soft_unit / math.sqrt(HD) * (
        jnp.maximum(scale, 0.0) + jnp.log(1.0 + jnp.exp(-jnp.abs(scale)))
    )

    for k in range(4):
        xv = r.X[k].astype(F32)
        inv = lax.rsqrt(jnp.mean(xv * xv, axis=1, keepdims=True) + epsilon)
        hn = xv * inv * gain_attn
        r.HN1[pl.ds(k * T, T)] = hn.astype(BF16)
        r.HN1T[:, :, pl.ds(k * T, T)] = hn.T.astype(BF16).reshape(2 * nz, 2 * CB, T)
    g_out[1](2)
    g_up[0]()
    g_dn[0]()
    for g in (*g_own, *g_oth):
        g[2]()

    W1 = r.W1
    W2 = r.W2
    for h in range(2):
        wq = W1[:, :, :, pl.ds(LO + 512 * h, 512)].reshape(D, 512)
        r.QKV[:, pl.ds(512 * h, 512)] = nn(r.HN1[...], wq)
    off = HW - LO
    for j in range(NH):
        q = r.QKV[:, off + HD * j : off + HD * (j + 1)]
        k = r.QKV[:, off + HW + HD * j : off + HW + HD * (j + 1)]
        v = r.QKV[:, off + 2 * HW + HD * j : off + 2 * HW + HD * (j + 1)]
        r.QRAW[j] = q
        r.QH[j] = (q * factor).astype(BF16)
        r.KH[j] = k.astype(BF16)
        r.VH[j] = v.astype(BF16)
        r.KT[j] = k.T.astype(BF16)
        r.VT[j] = v.T.astype(BF16)
    tri_k = lax.broadcasted_iota(jnp.int32, (HP, HP), 0)
    tri_q = lax.broadcasted_iota(jnp.int32, (HP, HP), 1)
    seen = tri_k <= tri_q

    def rows_of(p):
        return pl.ds(p * HP, HP)

    def attend(p, j):
        q = r.QH[j, rows_of(p)]
        diag = jnp.where(seen, nt(r.KH[j, rows_of(p)], q), neg_large)
        top = jnp.max(diag, axis=0, keepdims=True)
        if p:
            full = nt(r.KH[j, pl.ds(0, HP)], q)
            top = jnp.maximum(top, jnp.max(full, axis=0, keepdims=True))
            full = jnp.exp(full - top)
        diag = jnp.exp(diag - top)
        total = jnp.sum(diag, axis=0, keepdims=True)
        if p:
            total = total + jnp.sum(full, axis=0, keepdims=True)
        inv = 1.0 / total
        diag = (diag * inv).astype(BF16)
        if p:
            r.PT1[j, pl.ds(0, HP)] = (full * inv).astype(BF16)
            r.PT1[j, pl.ds(HP, HP)] = diag
            ot = nn(r.VT[j], r.PT1[j])
        else:
            r.PT0[j] = diag
            ot = nn(r.VT[j, :, pl.ds(0, HP)], diag)
        r.OT[j, :, rows_of(p)] = ot
        r.OB[rows_of(p), HD * j : HD * (j + 1)] = ot.T.astype(BF16)

    def to_sibling(st, p, value):
        r.PF[p] = value.reshape(2, T, D)
        r.ES[st, p] = r.PF[p, 1 - c].astype(BF16)
        send(lambda: copy(r.ES.at[st, p], r.ER.at[st, p], r.s_e.at[st, p], r.r_e.at[st, p], sib))

    def chip_sum(st, p):
        arrive(lambda: copy(r.ES.at[st, p], r.ER.at[st, p], r.s_e.at[st, p], r.r_e.at[st, p], sib))
        return r.PF[p, c] + r.ER[st, p].astype(F32)

    def xslot(st, p):
        return 2 * st + p if st < 2 else st + 2

    def xcopy(st, p):
        i = xslot(st, p)
        return copy(r.XS.at[i], r.XR.at[i], r.s_x.at[i], r.r_x.at[i], xp)

    def to_x(st, p):
        r.XS[xslot(st, p)] = chip_sum(st, p).astype(BF16)
        send(lambda: xcopy(st, p))

    def pair_sum(st, p):
        arrive(lambda: xcopy(st, p))
        return r.XS[xslot(st, p)].astype(F32) + r.XR[xslot(st, p)].astype(F32)

    def share(name, st, p):
        mk = lambda i: copy(name.at[i], name.at[i], r.s_h.at[st, p], r.r_h.at[st, p], sib)
        send(lambda: mk(2 * p + c))
        return lambda: arrive(lambda: mk(2 * p + (1 - c)))

    def out_proj(p):
        to_sibling(0, p, nn(r.OB[rows_of(p)], W2[:, :, pl.ds(0, D)].reshape(HW, D)))

    for j in range(NH):
        attend(0, j)
    for d in range(3, nz):
        g_out[1](d)
    out_proj(0)
    attend(1, 0)
    attend(1, 1)
    to_x(0, 0)
    g_up[1](1)
    g_dn[1](1)
    attend(1, 2)
    attend(1, 3)
    out_proj(1)
    to_x(0, 1)
    for d in range(2, nz):
        g_up[1](d)
        g_dn[1](d)

    r.SGA[...] = jnp.zeros_like(r.SGA)

    def middle(p):
        mid = r.X[2 * p + c].astype(F32) + pair_sum(0, p)
        r.MID[p] = mid
        inv = lax.rsqrt(jnp.mean(mid * mid, axis=1, keepdims=True) + epsilon)
        r.HN2[2 * p + c] = (mid * inv * gain_ffn).astype(BF16)
        return share(r.HN2, 0, p)

    def w_up():
        return W1[:, :, :, pl.ds(0, HW)].reshape(D, HW)

    def feed(p):
        hn = r.HN2[pl.ds(2 * p, 2)].reshape(HP, D)
        u = nn(hn, w_up()) + bias_up
        sig = 1.0 / (1.0 + jnp.exp(-u))
        r.ACT[rows_of(p)] = (u * sig).astype(BF16)
        dy = r.DY[pl.ds(2 * p, 2)].reshape(HP, D)
        dact = nt(dy, W2[:, :, pl.ds(D, D)].reshape(HW, D))
        dup = (dact * sig * (1.0 + u * (1.0 - sig))).astype(BF16)
        r.DUP[rows_of(p), 0:HW] = dup
        to_sibling(1, p, nt(dup, w_up()))
        row = pl.ds(4 + s, 1)
        r.SGA[row, 0:HW] = r.SGA[row, 0:HW] + jnp.sum(dup.astype(F32), axis=0, keepdims=True)

    def transpose_hn2(p):
        for k in range(2):
            t = r.HN2[2 * p + k].astype(F32).T.astype(BF16)
            r.HN2T[:, :, pl.ds((2 * p + k) * T, T)] = t.reshape(2 * nz, 2 * CB, T)

    r.DUP[:, 256:384] = jnp.zeros((L, 128), BF16)
    r.DQ[:, 0:128] = jnp.zeros((L, 128), BF16)
    wait_hn = middle(0)
    g_up[2]()
    g_dn[2]()
    wait_hn()
    feed(0)
    transpose_hn2(0)
    wait_hn = middle(1)
    to_x(1, 0)
    wait_hn()
    feed(1)
    transpose_hn2(1)

    def scatter_item(idx, part, yr, zu, zd, zcond, y_first=True):
        yc = lambda zz: copy(part(zz, 1 - y), yr(zz), r.s_ry.at[idx, zz], r.r_ry.at[idx, zz], yp)
        up = lambda zz: copy(part(zz, y), zu(zz), r.s_ru.at[idx, zz], r.r_ru.at[idx, zz], zup)
        dn = lambda zz: copy(part(zz, y), zd(zz), r.s_rd.at[idx, zz], r.r_rd.at[idx, zz], zdn)

        def add(zz, other):
            part(zz, y)[...] = (part(zz, y)[...].astype(F32) + other(zz)[...].astype(F32)).astype(BF16)

        ycond = None if zcond is None else jnp.logical_not(zcond)

        def start(d):
            if d:
                send(lambda: yc(z + d), both(z + d < nz, ycond))
                send(lambda: yc(z - d), both(z - d >= 0, ycond))
            else:
                send(lambda: yc(z), ycond)

        def step(d):
            if d:
                ok = both(zcond, z + d < nz)
                from_below = both(ok, z > 0)
                if y_first:
                    arrive(lambda: yc(z + d), ok)
                    when(ok, lambda: add(z + d, yr))
                arrive(lambda: up(z + d), from_below)
                when(from_below, lambda: add(z + d, zu))
                send(lambda: up(z + d), ok)
                ok2 = both(zcond, z - d >= 0)
                from_above = both(ok2, z < nz - 1)
                if y_first:
                    arrive(lambda: yc(z - d), ok2)
                    when(ok2, lambda: add(z - d, yr))
                arrive(lambda: dn(z - d), from_above)
                when(from_above, lambda: add(z - d, zd))
                send(lambda: dn(z - d), ok2)
            else:
                below, above = both(zcond, z > 0), both(zcond, z < nz - 1)
                arrive(lambda: up(z), below)
                when(below, lambda: add(z, zu))
                arrive(lambda: dn(z), above)
                when(above, lambda: add(z, zd))
                if y_first:
                    arrive(lambda: yc(z), zcond)
                    when(zcond, lambda: add(z, yr))

        return start, step

    far = range(nz - 1, 0, -1)
    cut_up, cut_qkv = pl.ds(0, LO), pl.ds(LO, D - LO)
    s_up = scatter_item(
        0,
        lambda zz, q: r.G1.at[2 * zz + q, :, :, cut_up],
        lambda zz: r.YR1.at[zz, :, :, cut_up],
        lambda zz: r.ZU1.at[zz - 1, :, :, cut_up],
        lambda zz: r.ZD1.at[zz, :, :, cut_up],
        None,
    )

    def qkv_item(idx, xx):
        return scatter_item(
            idx,
            lambda zz, q: r.G1.at[2 * zz + q, xx, :, cut_qkv],
            lambda zz: r.YR1.at[zz, xx, :, cut_qkv],
            lambda zz: r.ZU1.at[zz - 1, xx, :, cut_qkv],
            lambda zz: r.ZD1.at[zz, xx, :, cut_qkv],
            None,
        )

    def w2_item(idx, lo, width, zcond, y_first):
        cut = pl.ds(lo, width)
        return scatter_item(
            idx,
            lambda zz, q: r.G2.at[zz, :, cut],
            lambda zz: r.YR2.at[zz, :, cut],
            lambda zz: r.ZU2.at[zz - 1, :, cut],
            lambda zz: r.ZD2.at[zz, :, cut],
            zcond,
            y_first,
        )

    s_dn = w2_item(1, D, D, mine, True)
    s_out = w2_item(2, 0, D // 2, None, False)
    s_out2 = w2_item(5, D // 2, D // 2, mine, True)
    s_far = qkv_item(3, 1 - x)
    s_own = qkv_item(4, x)

    gu = nn(r.HN2T[...].reshape(D, L), r.DUP[...])
    r.G1[:, :, :, 0:384] = gu.astype(BF16).reshape(2 * nz, 2, CB, 384)
    for d in (*far, 0):
        s_up[0](d)
    to_x(1, 1)
    dy_all = r.DY[...].reshape(L, D)
    r.G2[:, :, pl.ds(D, D)] = tn(r.ACT[...], dy_all).astype(BF16).reshape(nz, CB, D)
    for d in (*far, 0):
        s_dn[0](d)

    def back_middle(p):
        dh = pair_sum(1, p)
        mid = r.MID[p]
        inv = lax.rsqrt(jnp.mean(mid * mid, axis=1, keepdims=True) + epsilon)
        n = mid * inv
        dn = dh * gain_ffn
        dmid = r.DY[2 * p + c].astype(F32) + inv * (
            dn - n * jnp.mean(dn * n, axis=1, keepdims=True)
        )
        r.DMID[p] = dmid
        r.DA[2 * p + c] = dmid.astype(BF16)
        own = jnp.where(x == p, jnp.sum(dh * n, axis=0, keepdims=True), 0.0)
        r.SGA[1:2] = r.SGA[1:2] + own
        return share(r.DA, 1, p)

    def back_out(p):
        da = r.DA[pl.ds(2 * p, 2)].reshape(HP, D)
        r.QKV[0:HP, 0:HW] = nt(da, W2[:, :, pl.ds(0, D)].reshape(HW, D))

    def back_attend(p, j):
        do = r.QKV[0:HP, HD * j : HD * (j + 1)].astype(BF16)
        dof = do.astype(F32)
        delta = jnp.sum(dof.T * r.OT[j, :, rows_of(p)], axis=0, keepdims=True)
        span = HP * (p + 1)
        pt = r.PT1[j] if p else r.PT0[j]
        dpt = nt(r.VH[j, pl.ds(0, span)], do)
        dst = (pt.astype(F32) * (dpt - delta)).astype(BF16)
        dv = nn(pt, do)
        dk = nn(dst, r.QH[j, rows_of(p)])
        dq = nn(r.KT[j, :, pl.ds(0, span)], dst).T
        raw = r.QRAW[j, rows_of(p)]
        r.SGA[3:4, 0:HD] = r.SGA[3:4, 0:HD] + jnp.sum(dq * raw, axis=0, keepdims=True)
        r.DQ[rows_of(p), off + HD * j : off + HD * (j + 1)] = (dq * factor).astype(BF16)
        ko, vo = off + HW + HD * j, off + 2 * HW + HD * j
        if p == 0:
            r.DKA[j] = dk
            r.DVA[j] = dv
        else:
            r.DQ[0:HP, ko : ko + HD] = (dk[:HP] + r.DKA[j]).astype(BF16)
            r.DQ[HP:L, ko : ko + HD] = dk[HP:].astype(BF16)
            r.DQ[0:HP, vo : vo + HD] = (dv[:HP] + r.DVA[j]).astype(BF16)
            r.DQ[HP:L, vo : vo + HD] = dv[HP:].astype(BF16)

    def down_proj(p):
        to_sibling(2, p, nn(r.ACT[rows_of(p)], W2[:, :, pl.ds(D, D)].reshape(HW, D)))

    wait_da = back_middle(0)
    down_proj(0)
    down_proj(1)
    if nz > 3:
        s_up[1](3)
    wait_da()
    back_out(0)
    for j in range(NH):
        back_attend(0, j)
    if nz > 2:
        s_up[1](2)
    wait_da = back_middle(1)
    r.XS[4] = chip_sum(2, 1 - x).astype(BF16)
    send(lambda: xcopy(2, 0))
    r.PF2[...] = chip_sum(2, x)
    s_up[1](1)
    if nz > 3:
        s_dn[1](3)
    wait_da()
    back_out(1)
    da_all = r.DA[...].reshape(L, D)
    r.G2[:, :, pl.ds(0, D)] = tn(r.OB[...], da_all).astype(BF16).reshape(nz, CB, D)
    if nz > 3:
        s_out[1](3)
    for d in (*far, 0):
        s_out2[0](d)
    for j in range(NH):
        back_attend(1, j)

    def qkv_block(bb):
        t = nn(r.HN1T[bb], r.DQ[...]).reshape(2, CB, D - LO)
        head = t[:, :, 0:128] + r.G1[bb, :, :, pl.ds(LO, 128)].astype(F32)
        r.G1[bb, :, :, pl.ds(LO, 128)] = head.astype(BF16)
        r.G1[bb, :, :, pl.ds(384, D - 384)] = t[:, :, 128:].astype(BF16)

    for d in far:
        pl.when(z + d < nz)(lambda: qkv_block(2 * (z + d) + (1 - y)))
        pl.when(z - d >= 0)(lambda: qkv_block(2 * (z - d) + (1 - y)))
        s_far[0](d)
        if d > 1:
            s_own[0](d)
    qkv_block(2 * z + (1 - y))
    for k in range(nz):
        qkv_block(2 * k + y)

    for p in range(2):
        w = W1[:, :, :, pl.ds(LO, D - LO)].reshape(D, D - LO)
        to_sibling(3, p, nt(r.DQ[rows_of(p)], w))
    s_up[1](0)
    if nz > 2:
        s_dn[1](2)
    arrive(lambda: xcopy(2, 0))
    own_out = r.PF2[...] + r.XR[4].astype(F32)
    mixed_o[...] = (r.MID[x] + own_out + bias_down).astype(BF16)
    r.XS[5] = chip_sum(3, 1 - x).astype(BF16)
    send(lambda: xcopy(3, 0))
    r.PF2[...] = chip_sum(3, x)
    s_dn[1](1)
    if nz > 2:
        s_out[1](2)
    if nz > 3:
        s_out2[1](3)
        s_far[1](3)
        s_own[1](3)
    s_out[1](1)
    if nz > 2:
        s_out2[1](2)
    s_dn[1](0)

    arrive(lambda: xcopy(3, 0))
    dh = r.PF2[...] + r.XR[5].astype(F32)
    xv = r.X[s].astype(F32)
    inv = lax.rsqrt(jnp.mean(xv * xv, axis=1, keepdims=True) + epsilon)
    n = xv * inv
    dn = dh * gain_attn
    gtok_o[...] = r.DMID[x] + inv * (dn - n * jnp.mean(dn * n, axis=1, keepdims=True))
    r.SGA[0:1] = jnp.sum(dh * n, axis=0, keepdims=True)
    r.SGA[2:3] = jnp.sum(r.DY[s].astype(F32), axis=0, keepdims=True)

    def small_copy(k, slot, dev):
        return lambda: copy(
            r.SGA if k == 0 else r.SGS.at[k - 1], r.SGR.at[slot], r.s_sg.at[slot], r.r_sg.at[slot], dev
        )

    total = r.SGA[...]
    for k, dev in enumerate((sib, xp, yp)):
        mk = small_copy(k, k, dev)
        send(mk)
        if k == 0 and nz > 2:
            s_far[1](2)
        if k == 2:
            cut_o = pl.ds(0, D // 2)
            s_out[1](0)
            m_gy = lambda: copy(
                r.G2.at[z, :, cut_o], r.YR2.at[z, :, cut_o], r.s_one.at[15], r.r_one.at[15], yp
            )
            send(m_gy, not_mine)
            s_far[0](0)
            s_own[0](1)
            s_own[0](0)
            if nz > 2:
                s_own[1](2)
            s_far[1](1)
            s_out2[1](1)
        arrive(mk)
        total = total + r.SGR[k]
        r.SGS[k] = total
    mks = []
    for k in range(1, nz):
        mk = small_copy(3, 2 + k, (2 * lax.rem(z + k, nz) + y, s))
        send(mk)
        mks.append(mk)
    s_out2[1](0)
    arrive(m_gy, mine)

    def out_from_y():
        r.G2[z, :, cut_o] = (r.G2[z, :, cut_o].astype(F32) + r.YR2[z, :, cut_o].astype(F32)).astype(BF16)

    when(mine, out_from_y)
    done2 = r.G2[z].astype(F32)
    r.GF2[0] = done2[:RW]
    r.GF2[1] = done2[RW:]
    m_g2 = lambda: copy(r.GF2.at[1 - c], r.GR2, r.s_one.at[12], r.r_one.at[12], sib)
    send(m_g2, mine)
    s_far[1](0)
    m_fx = lambda: copy(r.G1.at[b, 1 - x], r.FX, r.s_one.at[11], r.r_one.at[11], xp)
    send(m_fx)
    for k, mk in enumerate(mks):
        arrive(mk)
        total = total + r.SGR[3 + k]
    sg_o[...] = total
    arrive(m_g2, not_mine)

    def out2_own():
        o2[...] = r.GF2[c]

    def out2_sib():
        o2[...] = r.GR2[...]

    when(mine, out2_own)
    when(not_mine, out2_sib)

    def hand_over(k, xx, block):
        done = block.astype(F32)
        r.GF[0, xx] = done[:RW]
        r.GF[1, xx] = done[RW:]
        mk = lambda i: copy(r.GF.at[1 - c, i], r.GRV.at[i], r.s_gf.at[k], r.r_gf.at[k], sib)
        send(lambda: mk(xx))
        o1[xx, c] = r.GF[c, xx]

        def take():
            arrive(lambda: mk(xx))
            o1[xx, 1 - c] = r.GRV[xx]

        return take

    s_own[1](1)
    arrive(m_fx)
    take_other = hand_over(0, 1 - x, r.FX[...])
    s_own[1](0)
    take_own = hand_over(1, x, r.G1[b, x])
    take_other()
    take_own()

    for make, cond in drains:
        when(cond, lambda make=make: make().wait_send())


def fused_layer(nb, ns, tokens, wqkv, wout, wup, wdown, gattn, gffn, bup, bdown, scale_param, cot):
    nz = nb // 2
    rows, D = wout.shape
    T = tokens.shape[1]
    L = ns * T
    V = pltpu.VMEM
    scratch = dict(
        WQ=V((rows, 3 * D), BF16),
        WU=V((rows, D), BF16),
        WO=V((rows, D), BF16),
        WD=V((rows, D), BF16),
        SM=V((8, 128), F32),
        W1P=V((2, 2, 48, D), BF16),
        W2P=V((48, 2 * D), BF16),
        SIB1=V((2, 48, D), BF16),
        SIB2=V((48, 2 * D), BF16),
        CB1=V((HD, D), BF16),
        W1=V((nb, 2, HD, D), BF16),
        W2=V((nz, HD, 2 * D), BF16),
        S=V((nb, 4, 8, 128), F32),
        X=V((4, T, D), BF16),
        DY=V((4, T, D), BF16),
        ROWS=V((8, D), F32),
        BUP=V((8, 4 * HD), F32),
        HN1=V((L, D), BF16),
        HN1T=V((nb, 2 * HD, L), BF16),
        HN2T=V((nb, 2 * HD, L), BF16),
        QKV=V((L, D - 256), F32),
        QRAW=V((4, L, HD), F32),
        QH=V((4, L, HD), BF16),
        KH=V((4, L, HD), BF16),
        VH=V((4, L, HD), BF16),
        KT=V((4, HD, L), BF16),
        VT=V((4, HD, L), BF16),
        PT0=V((4, L // 2, L // 2), BF16),
        PT1=V((4, L, L // 2), BF16),
        OT=V((4, HD, L), F32),
        OB=V((L, 4 * HD), BF16),
        PF=V((2, 2, T, D), F32),
        PF2=V((T, D), F32),
        ES=V((4, 2, T, D), BF16),
        ER=V((4, 2, T, D), BF16),
        XS=V((6, T, D), BF16),
        XR=V((6, T, D), BF16),
        MID=V((2, T, D), F32),
        HN2=V((4, T, D), BF16),
        ACT=V((L, 4 * HD), BF16),
        DUP=V((L, 384), BF16),
        DA=V((4, T, D), BF16),
        DMID=V((2, T, D), F32),
        DQ=V((L, D - 256), BF16),
        DKA=V((4, L // 2, HD), F32),
        DVA=V((4, L // 2, HD), F32),
        G1=V((nb, 2, HD, D), BF16),
        G2=V((nz, HD, 2 * D), BF16),
        YR1=V((nz, 2, HD, D), BF16),
        ZU1=V((nz - 1, 2, HD, D), BF16),
        ZD1=V((nz - 1, 2, HD, D), BF16),
        YR2=V((nz, HD, 2 * D), BF16),
        ZU2=V((nz - 1, HD, 2 * D), BF16),
        ZD2=V((nz - 1, HD, 2 * D), BF16),
        FX=V((HD, D), BF16),
        GF=V((2, 2, rows, D), F32),
        GRV=V((2, rows, D), F32),
        GF2=V((2, rows, 2 * D), F32),
        GR2=V((rows, 2 * D), F32),
        SGA=V((8, D), F32),
        SGS=V((3, 8, D), F32),
        SGR=V((2 + nz, 8, D), F32),
    )
    dma = pltpu.SemaphoreType.DMA
    scratch.update(
        s_in=dma((6,)),
        s_x1=dma((3,)), r_x1=dma((3,)),
        s_gf=dma((2,)), r_gf=dma((2,)),
        s_one=dma((16,)), r_one=dma((16,)),
        s_up=dma((8, nz)), r_up=dma((8, nz)),
        s_dn=dma((8, nz)), r_dn=dma((8, nz)),
        s_y=dma((8, nz)), r_y=dma((8, nz)),
        s_e=dma((4, 2)), r_e=dma((4, 2)),
        s_x=dma((6,)), r_x=dma((6,)),
        s_h=dma((2, 2)), r_h=dma((2, 2)),
        s_ry=dma((6, nz)), r_ry=dma((6, nz)),
        s_ru=dma((6, nz)), r_ru=dma((6, nz)),
        s_rd=dma((6, nz)), r_rd=dma((6, nz)),
        s_sg=dma((2 + nz,)), r_sg=dma((2 + nz,)),
    )
    vmem = pl.BlockSpec(memory_space=pltpu.VMEM)
    hbm = pl.BlockSpec(memory_space=pl.ANY)
    mixed, gtok, o1, o2, sg = pl.pallas_call(
        functools.partial(layer_kernel, nz, tuple(scratch)),
        out_shape=(
            jax.ShapeDtypeStruct((T, D), BF16),
            jax.ShapeDtypeStruct((T, D), F32),
            jax.ShapeDtypeStruct((2, 2, rows, D), F32),
            jax.ShapeDtypeStruct((rows, 2 * D), F32),
            jax.ShapeDtypeStruct((8, D), F32),
        ),
        in_specs=[hbm] * 6 + [vmem] * 5,
        out_specs=(vmem,) * 5,
        scratch_shapes=list(scratch.values()),
        compiler_params=pltpu.CompilerParams(
            collective_id=0, has_side_effects=True, vmem_limit_bytes=63 << 20
        ),
        name="decoder_layer",
    )(tokens[0], cot[0], wqkv, wout, wup, wdown, gattn, gffn, bup, bdown, scale_param)
    mixed, gtok, gqkv, gout, gup, gdown, g_attn, g_ffn, g_bup, g_bdown, gscale = pl.pallas_call(
        functools.partial(outputs_kernel, ns),
        out_shape=(
            jax.ShapeDtypeStruct((T, D), BF16),
            jax.ShapeDtypeStruct((T, D), F32),
            jax.ShapeDtypeStruct((rows, 3 * D), F32),
            jax.ShapeDtypeStruct((rows, D), F32),
            jax.ShapeDtypeStruct((rows, D), F32),
            jax.ShapeDtypeStruct((rows, D), F32),
            jax.ShapeDtypeStruct((rows,), F32),
            jax.ShapeDtypeStruct((rows,), F32),
            jax.ShapeDtypeStruct((rows,), F32),
            jax.ShapeDtypeStruct((rows,), F32),
            jax.ShapeDtypeStruct((HD,), F32),
        ),
        in_specs=[vmem] * 6,
        out_specs=(vmem,) * 11,
        compiler_params=pltpu.CompilerParams(vmem_limit_bytes=63 << 20),
        name="place_outputs",
    )(mixed, gtok, o1, o2, sg, scale_param)
    return mixed[None], gtok[None], gqkv, gout, gup, gdown, g_attn, g_ffn, g_bup, g_bdown, gscale


def outputs_kernel(ns, mixed, gtok, o1, o2, sg, scl, mixed_o, gtok_o, gqkv, gout, gup, gdown, *small):
    rows, D = gup.shape
    HW = 4 * HD
    mixed_o[...] = mixed[...]
    gtok_o[...] = gtok[...]
    gout[...] = o2[:, 0:D]
    gdown[...] = o2[:, D : 2 * D]
    for xx in range(2):
        for cc in range(2):
            for t in range(4):
                for j in range(4):
                    v = o1[xx, cc, :, HW * t + HD * j : HW * t + HD * (j + 1)]
                    at = HD * (4 * j + 2 * cc + xx)
                    if t == 0:
                        gup[:, at : at + HD] = v
                    else:
                        gqkv[:, D * (t - 1) + at : D * (t - 1) + at + HD] = v
    first = (lax.axis_index("batch") * ns + lax.axis_index("seq")) * rows
    parts = []
    for h in range(H):
        j, cc, xx = h // 4, (h // 2) % 2, h % 2
        row = 4 + 2 * xx + cc
        parts.append(sg[row : row + 1, HD * j : HD * (j + 1)])
    bias_up = jnp.concatenate(parts, axis=1)
    shift = lax.rem(D - first, D)
    for ref, v in zip(small, (sg[0:1], sg[1:2], bias_up, sg[2:3])):
        v = jnp.broadcast_to(v, (8, D))
        ref[...] = pltpu.roll(v, shift, 1)[0, 0:rows]
    scale = scl[...].astype(F32).reshape(1, HD)
    small[4][...] = (sg[3:4, 0:HD] * (soft_unit / math.sqrt(HD)) / (1.0 + jnp.exp(-scale)))[0]


def layer_step(nb, ns, *args):
    if fits_fused(nb, ns, args[0], args[1], args[3]):
        return fused_layer(nb, ns, *args)
    return generic_layer(*args)


def solution(mesh):
    return jax.shard_map(
        functools.partial(layer_step, mesh.shape["batch"], mesh.shape["seq"]),
        mesh=mesh,
        in_specs=(
            P("batch", "seq", None),
            P(("batch", "seq"), None),
            P(("batch", "seq"), None),
            P(("batch", "seq"), None),
            P(("batch", "seq"), None),
            P(("batch", "seq")),
            P(("batch", "seq")),
            P(("batch", "seq")),
            P(("batch", "seq")),
            P(),
            P("batch", "seq", None),
        ),
        out_specs=(
            P("batch", "seq", None),
            P("batch", "seq", None),
            P(("batch", "seq"), None),
            P(("batch", "seq"), None),
            P(("batch", "seq"), None),
            P(("batch", "seq"), None),
            P(("batch", "seq")),
            P(("batch", "seq")),
            P(("batch", "seq")),
            P(("batch", "seq")),
            P(),
        ),
        check_vma=False,
    )
```

```python
import functools
import math
import types

import jax
import jax.numpy as jnp
from jax import lax
from jax.experimental import pallas as pl
from jax.experimental.pallas import tpu as pltpu
from jax.sharding import PartitionSpec as P

H = 16
HD = 80


epsilon = 1e-06
soft_unit = 1.442695041
neg_large = -1e30


def norm_forward(values, gain):
    inverse = lax.rsqrt(jnp.mean(values * values, axis=1, keepdims=True) + epsilon)
    return (inverse, (values * inverse * gain.astype(jnp.float32)).astype(jnp.bfloat16))


def norm_back(grad_out, values, inverse, gain):
    normed = values * inverse
    scaled = grad_out * gain.astype(jnp.float32)
    grad_gain = jnp.sum(grad_out * normed, axis=0)
    grad_in = inverse * (scaled - normed * jnp.mean(scaled * normed, axis=1, keepdims=True))
    return (grad_in, grad_gain)


def generic_layer(
    tokens,
    query_key_value_weight,
    attention_output_weight,
    up_projection_weight,
    down_projection_weight,
    gain_attn,
    gain_ffn,
    up_projection_bias,
    down_projection_bias,
    scale_param,
    cotangent,
):
    seq_local, tok_seq, width = tokens.shape
    row_count = seq_local * tok_seq
    shards = (
        query_key_value_weight,
        attention_output_weight,
        up_projection_weight,
        down_projection_weight,
        gain_attn,
        gain_ffn,
        up_projection_bias,
        down_projection_bias,
    )
    fwd_weights = (
        lax.all_gather(shards[0], ("batch", "seq"), axis=0, tiled=True),
        lax.all_gather(shards[1], ("batch", "seq"), axis=0, tiled=True),
        lax.all_gather(shards[2], ("batch", "seq"), axis=0, tiled=True),
        lax.all_gather(shards[3], ("batch", "seq"), axis=0, tiled=True),
        lax.all_gather(shards[4], ("batch", "seq"), axis=0, tiled=True),
        lax.all_gather(shards[5], ("batch", "seq"), axis=0, tiled=True),
        lax.all_gather(shards[6], ("batch", "seq"), axis=0, tiled=True),
        lax.all_gather(shards[7], ("batch", "seq"), axis=0, tiled=True),
    )
    wqkv_full, wout_full, wup_full, wdown_full, gattn_full, gffn_full, bup_full, bdown_full = (
        fwd_weights
    )
    inputs = tokens.astype(jnp.float32).reshape(row_count, width)
    inv_attn, attention_normed_input = norm_forward(inputs, gattn_full)
    query_key_value = jnp.dot(attention_normed_input, wqkv_full, preferred_element_type=jnp.float32)
    q_raw = query_key_value[:, :width]
    scale_float = scale_param.astype(jnp.float32)
    factor = soft_unit / math.sqrt(HD) * jax.nn.softplus(scale_float)
    factor_row = jnp.tile(factor, H)
    queries = (q_raw * factor_row).astype(jnp.bfloat16)
    keys_own = (
        query_key_value[:, width : 2 * width]
        .astype(jnp.bfloat16)
        .reshape(seq_local, tok_seq, width)
    )
    values_own = (
        query_key_value[:, 2 * width :].astype(jnp.bfloat16).reshape(seq_local, tok_seq, width)
    )
    keys_all, values_all = (
        lax.all_gather(keys_own, "seq", axis=1, tiled=True),
        lax.all_gather(values_own, "seq", axis=1, tiled=True),
    )
    position = lax.axis_index("seq")
    block_total = lax.axis_size("seq")
    query_pos = position * tok_seq + jnp.arange(tok_seq, dtype=jnp.int32)
    key_offsets = jnp.arange(tok_seq, dtype=jnp.int32)
    queries_h = queries.reshape(seq_local, tok_seq, H, HD)

    def key_block(source, block):
        piece = lax.dynamic_slice_in_dim(source, block * tok_seq, tok_seq, 1)
        return piece.reshape(seq_local, tok_seq, H, HD)

    def block_scores(block):
        scores = jnp.einsum(
            "sqhd,skhd->shqk",
            queries_h,
            key_block(keys_all, block),
            preferred_element_type=jnp.float32,
        )
        allowed = (block * tok_seq + key_offsets)[None, :] <= query_pos[:, None]
        return jnp.where(allowed, scores, neg_large)

    def max_step(block, carry):
        top, total = carry
        scores = block_scores(block)
        new_top = jnp.maximum(top, jnp.max(scores, axis=3, keepdims=True))
        total = total * jnp.exp(top - new_top) + jnp.sum(
            jnp.exp(scores - new_top), axis=3, keepdims=True
        )
        return (new_top, total)

    start_top = jnp.full((seq_local, H, tok_seq, 1), neg_large, jnp.float32)
    top, total = lax.fori_loop(0, block_total, max_step, (start_top, jnp.zeros_like(start_top)))
    log_sum = top + jnp.log(total)

    def value_step(block, accum):
        probs = jnp.exp(block_scores(block) - log_sum).astype(jnp.bfloat16)
        return accum + jnp.einsum(
            "shqk,skhd->sqhd",
            probs,
            key_block(values_all, block),
            preferred_element_type=jnp.float32,
        )

    attention_output = lax.fori_loop(
        0, block_total, value_step, jnp.zeros((seq_local, tok_seq, H, HD), jnp.float32)
    )
    attention_output = attention_output.reshape(row_count, width)
    att_low = attention_output.astype(jnp.bfloat16)
    middle = inputs + jnp.dot(att_low, wout_full, preferred_element_type=jnp.float32)
    inv_ffn, feedforward_normed_input = norm_forward(middle, gffn_full)
    up_projected_value = jnp.dot(
        feedforward_normed_input, wup_full, preferred_element_type=jnp.float32
    ) + bup_full.astype(jnp.float32)
    act_low = jax.nn.silu(up_projected_value).astype(jnp.bfloat16)
    result = (
        middle
        + jnp.dot(act_low, wdown_full, preferred_element_type=jnp.float32)
        + bdown_full.astype(jnp.float32)
    )
    mixed = result.astype(jnp.bfloat16).reshape(seq_local, tok_seq, width)
    back_weights = (
        lax.all_gather(shards[0], ("batch", "seq"), axis=0, tiled=True),
        lax.all_gather(shards[1], ("batch", "seq"), axis=0, tiled=True),
        lax.all_gather(shards[2], ("batch", "seq"), axis=0, tiled=True),
        lax.all_gather(shards[3], ("batch", "seq"), axis=0, tiled=True),
        lax.all_gather(shards[4], ("batch", "seq"), axis=0, tiled=True),
        lax.all_gather(shards[5], ("batch", "seq"), axis=0, tiled=True),
        lax.all_gather(shards[6], ("batch", "seq"), axis=0, tiled=True),
        lax.all_gather(shards[7], ("batch", "seq"), axis=0, tiled=True),
    )
    wqkv_back, wout_back, wup_back, wdown_back, gattn_back, gffn_back, bup_back, bdown_back = (
        back_weights
    )
    grad_low = cotangent.reshape(row_count, width)
    grad_float = grad_low.astype(jnp.float32)
    grad_down = jnp.einsum("rf,rd->fd", act_low, grad_low, preferred_element_type=jnp.float32)
    grad_bias_down = jnp.sum(grad_float, axis=0)
    grad_act = jnp.einsum("rd,fd->rf", grad_low, wdown_back, preferred_element_type=jnp.float32)
    sigma = jax.nn.sigmoid(up_projected_value)
    grad_upv = (grad_act * sigma * (1.0 + up_projected_value * (1.0 - sigma))).astype(jnp.bfloat16)
    grad_up = jnp.einsum(
        "rd,rf->df", feedforward_normed_input, grad_upv, preferred_element_type=jnp.float32
    )
    grad_bias_up = jnp.sum(grad_upv.astype(jnp.float32), axis=0)
    grad_hn_ffn = jnp.einsum("rf,df->rd", grad_upv, wup_back, preferred_element_type=jnp.float32)
    grad_norm_ffn, grad_gain_ffn = norm_back(grad_hn_ffn, middle, inv_ffn, gffn_back)
    grad_middle = grad_float + grad_norm_ffn
    grad_attn = grad_middle.astype(jnp.bfloat16)
    grad_out = jnp.einsum("rd,re->de", att_low, grad_attn, preferred_element_type=jnp.float32)
    block_summed = (
        lax.psum_scatter(grad_out, ("batch", "seq"), scatter_dimension=0, tiled=True),
        lax.psum_scatter(grad_up, ("batch", "seq"), scatter_dimension=0, tiled=True),
        lax.psum_scatter(grad_down, ("batch", "seq"), scatter_dimension=0, tiled=True),
        lax.psum_scatter(grad_gain_ffn, ("batch", "seq"), scatter_dimension=0, tiled=True),
        lax.psum_scatter(grad_bias_up, ("batch", "seq"), scatter_dimension=0, tiled=True),
        lax.psum_scatter(grad_bias_down, ("batch", "seq"), scatter_dimension=0, tiled=True),
    )
    grad_att_low = jnp.einsum(
        "re,de->rd", grad_attn, wout_back, preferred_element_type=jnp.float32
    ).astype(jnp.bfloat16)
    grad_heads = grad_att_low.reshape(seq_local, tok_seq, H, HD)
    delta = jnp.sum(
        (grad_att_low.astype(jnp.float32) * attention_output).reshape(seq_local, tok_seq, H, HD),
        axis=3,
    )
    delta = jnp.transpose(delta, (0, 2, 1))[..., None]
    query_init = jnp.zeros((seq_local, tok_seq, H, HD), jnp.float32)

    def grad_step(block, carry):
        grad_query, term = carry
        scores = block_scores(block)
        probs = jnp.exp(scores - log_sum)
        keys_blk = key_block(keys_all, block)
        values_blk = key_block(values_all, block)
        grad_probs = jnp.einsum(
            "sqhd,skhd->shqk", grad_heads, values_blk, preferred_element_type=jnp.float32
        )
        grad_scores = (probs * (grad_probs - delta)).astype(jnp.bfloat16)
        grad_values = jnp.einsum(
            "shqk,sqhd->skhd",
            probs.astype(jnp.bfloat16),
            grad_heads,
            preferred_element_type=jnp.float32,
        )
        grad_keys = jnp.einsum(
            "shqk,sqhd->skhd", grad_scores, queries_h, preferred_element_type=jnp.float32
        )
        grad_query = grad_query + jnp.einsum(
            "shqk,skhd->sqhd", grad_scores, keys_blk, preferred_element_type=jnp.float32
        )
        piece = jnp.concatenate(
            [
                grad_keys.reshape(seq_local, tok_seq, width),
                grad_values.reshape(seq_local, tok_seq, width),
            ],
            axis=2,
        )
        term = lax.dynamic_update_slice_in_dim(term, piece, block * tok_seq, 1)
        return (grad_query, term)

    term_init = jnp.zeros((seq_local, tok_seq * block_total, 2 * width), jnp.float32)
    grad_query, term = lax.fori_loop(0, block_total, grad_step, (query_init, term_init))
    kv_grads = lax.psum_scatter(
        term.astype(jnp.bfloat16), "seq", scatter_dimension=1, tiled=True
    ).astype(jnp.float32)
    grad_scaled = grad_query.reshape(row_count, width)
    scale_local = jnp.sum((grad_scaled * q_raw).reshape(row_count, H, HD), axis=(0, 1))
    scale_total = lax.psum(scale_local, ("batch", "seq"))
    grad_scale = scale_total * (soft_unit / math.sqrt(HD)) * jax.nn.sigmoid(scale_float)
    grad_qkv_low = jnp.concatenate(
        [grad_scaled * factor_row, kv_grads.reshape(row_count, 2 * width)], axis=1
    ).astype(jnp.bfloat16)
    grad_qkv = jnp.einsum(
        "rd,re->de", attention_normed_input, grad_qkv_low, preferred_element_type=jnp.float32
    )
    grad_hn_attn = jnp.einsum(
        "re,de->rd", grad_qkv_low, wqkv_back, preferred_element_type=jnp.float32
    )
    grad_norm_attn, grad_gain_attn = norm_back(grad_hn_attn, inputs, inv_attn, gattn_back)
    grad_tokens = (grad_middle + grad_norm_attn).reshape(seq_local, tok_seq, width)
    qkv_summed = (
        lax.psum_scatter(grad_qkv, ("batch", "seq"), scatter_dimension=0, tiled=True),
        lax.psum_scatter(grad_gain_attn, ("batch", "seq"), scatter_dimension=0, tiled=True),
    )
    return (
        mixed,
        grad_tokens,
        qkv_summed[0],
        block_summed[0],
        block_summed[1],
        block_summed[2],
        qkv_summed[1],
        block_summed[3],
        block_summed[4],
        block_summed[5],
        grad_scale,
    )


MESH = pl.DeviceIdType.MESH
F32 = jnp.float32
BF16 = jnp.bfloat16


def fits_fused(nb, ns, tokens, wqkv, wup):
    rows, width = wup.shape[0], wup.shape[1]
    return (
        ns == 4
        and nb % 2 == 0
        and tokens.shape == (1, 128, H * HD)
        and width == H * HD
        and 2 * rows == HD
        and nb * ns * rows == width
        and wqkv.shape == (rows, 3 * width)
    )


def nt(a, b):
    return lax.dot_general(a, b, (((1,), (1,)), ((), ())), preferred_element_type=F32)


def nn(a, b):
    return lax.dot_general(a, b, (((1,), (0,)), ((), ())), preferred_element_type=F32)


def tn(a, b):
    return lax.dot_general(a, b, (((0,), (0,)), ((), ())), preferred_element_type=F32)


def layer_kernel(nz, scratch_names, tok, cot, wqkv, wout, wup, wdown, ga, gf, bu, bd, scl, *refs):
    mixed_o, gtok_o, o1, o2, sg_o = refs[:5]
    r = types.SimpleNamespace(**dict(zip(scratch_names, refs[5:])))
    D = tok.shape[1]
    T = tok.shape[0]
    L = 4 * T
    HP = 2 * T
    NH = 4
    HW = NH * HD
    CB = HD
    RW = HD // 2
    LO = 256
    b = lax.axis_index("batch")
    s = lax.axis_index("seq")
    z, y = b // 2, b % 2
    x, c = s // 2, s % 2
    sib = (b, 2 * x + (1 - c))
    xp = (b, 2 * (1 - x) + c)
    yp = (2 * z + (1 - y), s)
    zup = (lax.rem(2 * (z + 1), 2 * nz) + y, s)
    zdn = (lax.rem(2 * (z + nz - 1), 2 * nz) + y, s)
    drains = []

    def when(cond, fn):
        if cond is None:
            fn()
        else:
            pl.when(cond)(fn)

    def both(p, q):
        if p is None:
            return q
        if q is None:
            return p
        return jnp.logical_and(p, q)

    def copy(src, dst, ssem, rsem, dev):
        return pltpu.make_async_remote_copy(
            src_ref=src, dst_ref=dst, send_sem=ssem, recv_sem=rsem, device_id=dev, device_id_type=MESH
        )

    def send(make, cond=None):
        when(cond, lambda: make().start())
        drains.append((make, cond))

    def arrive(make, cond=None):
        when(cond, lambda: make().wait_recv())

    bar = pltpu.get_barrier_semaphore()
    peers = [sib, xp, yp]
    for k in range(1, nz):
        peers.append((2 * lax.rem(z + k, nz) + y, s))
    for dev in peers:
        pl.semaphore_signal(bar, inc=1, device_id=dev, device_id_type=MESH)
    fetches = [
        pltpu.make_async_copy(src, dst, r.s_in.at[k])
        for k, (src, dst) in enumerate(
            (
                (wqkv, r.WQ),
                (wup, r.WU),
                (wout, r.WO),
                (wdown, r.WD),
                (tok, r.X.at[s]),
                (cot, r.DY.at[s]),
            )
        )
    ]
    for f in fetches:
        f.start()
    small_rows = [v[...].astype(F32).reshape(1, RW) for v in (ga, gf, bu, bd)]
    r.SM[...] = jnp.zeros_like(r.SM)
    for k, row in enumerate(small_rows):
        r.SM[k : k + 1, 0:RW] = row
    fetches[0].wait()
    fetches[1].wait()

    def pieces(cc):
        for xx in range(2):
            for t in range(4):
                for j in range(NH):
                    src = HD * (4 * j + 2 * cc + xx)
                    v = r.WU[:, src : src + HD] if t == 0 else r.WQ[:, D * (t - 1) + src : D * (t - 1) + src + HD]
                    r.W1P[cc, xx, 0:RW, HW * t + HD * j : HW * t + HD * (j + 1)] = v

    pieces(0)
    pieces(1)
    pl.semaphore_wait(bar, len(peers))

    m_sib1 = lambda: copy(r.W1P.at[1 - c], r.SIB1, r.s_one.at[0], r.r_one.at[0], sib)
    m_ssib = lambda: copy(r.SM, r.S.at[b, s], r.s_one.at[1], r.r_one.at[1], sib)
    m_sib2 = lambda: copy(r.W2P, r.SIB2, r.s_one.at[2], r.r_one.at[2], sib)
    send(m_ssib)
    send(m_sib1)
    fetches[2].wait()
    fetches[3].wait()
    r.W2P[0:RW, 0:D] = r.WO[...]
    r.W2P[0:RW, D : 2 * D] = r.WD[...]
    send(m_sib2)
    r.S[b, s] = r.SM[...]

    def chip_rows(own, other):
        own, other = own[:RW].astype(F32), other[:RW].astype(F32)
        lo = jnp.where(c == 0, own, other)
        hi = jnp.where(c == 0, other, own)
        return jnp.concatenate([lo, hi], axis=0).astype(BF16)

    m_ssib_r = lambda: copy(r.SM, r.S.at[b, 2 * x + (1 - c)], r.s_one.at[1], r.r_one.at[1], sib)
    arrive(m_ssib_r)
    m_xs = lambda: copy(
        r.S.at[b, pl.ds(2 * x, 2)], r.S.at[b, pl.ds(2 * x, 2)], r.s_one.at[4], r.r_one.at[4], xp
    )
    send(m_xs)
    arrive(m_sib1)
    r.CB1[...] = chip_rows(r.W1P[c, 1 - x], r.SIB1[1 - x])
    half = (D - LO) // 2
    cuts = (pl.ds(LO, half), pl.ds(LO + half, half), pl.ds(0, LO))

    def m_x1(k, xx):
        return copy(r.CB1.at[:, cuts[k]], r.W1.at[b, xx, :, cuts[k]], r.s_x1.at[k], r.r_x1.at[k], xp)

    for k in range(3):
        send(lambda k=k: m_x1(k, x))
    r.W1[b, x] = chip_rows(r.W1P[c, x], r.SIB1[x])

    def gather_item(idx, block, zcond, passes_y=True):
        up = lambda zz: copy(block(zz, y), block(zz, y), r.s_up.at[idx, zz], r.r_up.at[idx, zz], zup)
        dn = lambda zz: copy(block(zz, y), block(zz, y), r.s_dn.at[idx, zz], r.r_dn.at[idx, zz], zdn)
        yy = lambda zz: copy(block(zz, y), block(zz, y), r.s_y.at[idx, zz], r.r_y.at[idx, zz], yp)

        def start():
            send(lambda: up(z), both(zcond, z < nz - 1))
            send(lambda: dn(z), both(zcond, z > 0))
            if passes_y:
                send(lambda: yy(z), zcond)

        def step(d):
            lo, hi = z - d, z + d
            below, above = both(zcond, lo >= 0), both(zcond, hi < nz)
            arrive(lambda: up(lo), below)
            send(lambda: up(lo), both(below, z < nz - 1))
            arrive(lambda: dn(hi), above)
            send(lambda: dn(hi), both(above, z > 0))
            if passes_y:
                send(lambda: yy(lo), below)
                send(lambda: yy(hi), above)

        def finish():
            if passes_y:
                for k in range(nz):
                    when(
                        None if zcond is None else jnp.logical_not(zcond),
                        lambda k=k: copy(
                            block(k, 1 - y), block(k, 1 - y), r.s_y.at[idx, k], r.r_y.at[idx, k], yp
                        ).wait_recv(),
                    )

        return start, step, finish

    mine = c == y
    not_mine = c != y
    g_s = gather_item(0, lambda zz, q: r.S.at[2 * zz + q], None)
    g_own = [gather_item(1 + k, lambda zz, q, k=k: r.W1.at[2 * zz + q, x, :, cuts[k]], None) for k in range(2)]
    g_oth = [
        gather_item(3 + k, lambda zz, q, k=k: r.W1.at[2 * zz + q, 1 - x, :, cuts[k]], None) for k in range(2)
    ]
    g_out = gather_item(5, lambda zz, q: r.W2.at[zz, :, pl.ds(0, D)], None, False)
    g_up = gather_item(6, lambda zz, q: r.W1.at[2 * zz + q, :, :, pl.ds(0, LO)], None)
    g_dn = gather_item(7, lambda zz, q: r.W2.at[zz, :, pl.ds(D, D)], mine)

    g_own[0][0]()
    g_own[1][0]()
    m_xs_r = lambda: copy(
        r.S.at[b, pl.ds(2 - 2 * x, 2)],
        r.S.at[b, pl.ds(2 - 2 * x, 2)],
        r.s_one.at[4],
        r.r_one.at[4],
        xp,
    )
    arrive(m_xs_r)
    g_s[0]()
    fetches[4].wait()
    fetches[5].wait()
    own_tok, own_cot = r.X.at[s], r.DY.at[s]
    m_xt = lambda: copy(own_tok, own_tok, r.s_one.at[5], r.r_one.at[5], xp)
    m_st = lambda: copy(own_tok, own_tok, r.s_one.at[6], r.r_one.at[6], sib)
    m_xc = lambda: copy(own_cot, own_cot, r.s_one.at[7], r.r_one.at[7], xp)
    m_sc = lambda: copy(own_cot, own_cot, r.s_one.at[8], r.r_one.at[8], sib)
    send(m_xt)
    send(m_st)
    send(m_xc)
    send(m_sc)
    arrive(m_sib2)

    def fill_w2():
        r.W2[z] = chip_rows(r.W2P[...], r.SIB2[...])

    when(mine, fill_w2)
    m_y2 = lambda: copy(
        r.W2.at[z, :, pl.ds(0, D)], r.W2.at[z, :, pl.ds(0, D)], r.s_one.at[14], r.r_one.at[14], yp
    )
    sx = 2 * (1 - x) + c
    so = 2 * (1 - x) + (1 - c)
    ss = 2 * x + (1 - c)
    fwd = lambda name, k, src_i: copy(
        name.at[src_i], name.at[src_i], r.s_one.at[k], r.r_one.at[k], sib
    )
    arrive(lambda: m_x1(0, 1 - x))
    g_oth[0][0]()
    g_own[0][1](1)
    arrive(lambda: m_x1(1, 1 - x))
    g_oth[1][0]()
    send(m_y2, mine)
    g_own[1][1](1)
    g_s[1](1)
    arrive(lambda: m_x1(2, 1 - x))
    g_oth[0][1](1)
    g_oth[1][1](1)
    g_own[0][1](2)
    g_own[1][1](2)
    g_s[1](2)
    arrive(lambda: copy(own_tok, r.X.at[sx], r.s_one.at[5], r.r_one.at[5], xp))
    send(lambda: fwd(r.X, 9, sx))
    g_oth[0][1](2)
    arrive(m_y2, not_mine)
    g_out[0]()
    g_oth[1][1](2)
    for d in range(3, nz):
        g_own[0][1](d)
        g_own[1][1](d)
        g_s[1](d)
        g_oth[0][1](d)
        g_oth[1][1](d)
    arrive(lambda: copy(own_tok, r.X.at[ss], r.s_one.at[6], r.r_one.at[6], sib))
    arrive(lambda: fwd(r.X, 9, so))
    arrive(lambda: copy(own_cot, r.DY.at[sx], r.s_one.at[7], r.r_one.at[7], xp))
    send(lambda: fwd(r.DY, 10, sx))
    arrive(lambda: copy(own_cot, r.DY.at[ss], r.s_one.at[8], r.r_one.at[8], sib))
    g_out[1](1)
    g_s[2]()
    arrive(lambda: fwd(r.DY, 10, so))

    jf = lax.broadcasted_iota(jnp.int32, (1, D), 1).astype(F32)
    jk = jnp.floor((jf + 0.5) / RW)
    jl = jf - RW * jk
    pick = (lax.broadcasted_iota(jnp.int32, (128, D), 0).astype(F32) == jl).astype(BF16)
    sm_rows = 2 * nz * 4
    spread = nn(r.S[...].reshape(sm_rows * 8, 128).astype(BF16), pick)
    spread = spread.reshape(sm_rows, 8, D)
    owner = lax.broadcasted_iota(jnp.int32, (sm_rows, 8, D), 0).astype(F32)
    r.ROWS[...] = jnp.sum(jnp.where(owner == jk[None], spread, 0.0), axis=0)
    uf = jf[:, :HW]
    uj = jnp.floor((uf + 0.5) / HD)
    uh = jnp.floor((uf - HD * uj + 0.5) / RW)
    base = (2 * c + x).astype(F32)
    uk = 2.0 * (4.0 * uj + base) + uh
    r.BUP[...] = jnp.sum(
        jnp.where(owner[:, :, :HW] == uk[None], spread[:, :, :HW], 0.0), axis=0
    )
    gain_attn = r.ROWS[0:1]
    gain_ffn = r.ROWS[1:2]
    bias_down = r.ROWS[3:4]
    bias_up = r.BUP[2:3]
    scale = scl[...].astype(F32).reshape(1, HD)
    factor = soft_unit / math.sqrt(HD) * (
        jnp.maximum(scale, 0.0) + jnp.log(1.0 + jnp.exp(-jnp.abs(scale)))
    )

    for k in range(4):
        xv = r.X[k].astype(F32)
        inv = lax.rsqrt(jnp.mean(xv * xv, axis=1, keepdims=True) + epsilon)
        hn = xv * inv * gain_attn
        r.HN1[pl.ds(k * T, T)] = hn.astype(BF16)
        r.HN1T[:, :, pl.ds(k * T, T)] = hn.T.astype(BF16).reshape(2 * nz, 2 * CB, T)
    g_out[1](2)
    g_up[0]()
    g_dn[0]()
    for g in (*g_own, *g_oth):
        g[2]()

    W1 = r.W1
    W2 = r.W2
    for h in range(2):
        wq = W1[:, :, :, pl.ds(LO + 512 * h, 512)].reshape(D, 512)
        r.QKV[:, pl.ds(512 * h, 512)] = nn(r.HN1[...], wq)
    off = HW - LO
    for j in range(NH):
        q = r.QKV[:, off + HD * j : off + HD * (j + 1)]
        k = r.QKV[:, off + HW + HD * j : off + HW + HD * (j + 1)]
        v = r.QKV[:, off + 2 * HW + HD * j : off + 2 * HW + HD * (j + 1)]
        r.QRAW[j] = q
        r.QH[j] = (q * factor).astype(BF16)
        r.KH[j] = k.astype(BF16)
        r.VH[j] = v.astype(BF16)
        r.KT[j] = k.T.astype(BF16)
        r.VT[j] = v.T.astype(BF16)
    tri_k = lax.broadcasted_iota(jnp.int32, (HP, HP), 0)
    tri_q = lax.broadcasted_iota(jnp.int32, (HP, HP), 1)
    seen = tri_k <= tri_q

    def rows_of(p):
        return pl.ds(p * HP, HP)

    def attend(p, j):
        q = r.QH[j, rows_of(p)]
        diag = jnp.where(seen, nt(r.KH[j, rows_of(p)], q), neg_large)
        top = jnp.max(diag, axis=0, keepdims=True)
        if p:
            full = nt(r.KH[j, pl.ds(0, HP)], q)
            top = jnp.maximum(top, jnp.max(full, axis=0, keepdims=True))
            full = jnp.exp(full - top)
        diag = jnp.exp(diag - top)
        total = jnp.sum(diag, axis=0, keepdims=True)
        if p:
            total = total + jnp.sum(full, axis=0, keepdims=True)
        inv = 1.0 / total
        diag = (diag * inv).astype(BF16)
        if p:
            r.PT1[j, pl.ds(0, HP)] = (full * inv).astype(BF16)
            r.PT1[j, pl.ds(HP, HP)] = diag
            ot = nn(r.VT[j], r.PT1[j])
        else:
            r.PT0[j] = diag
            ot = nn(r.VT[j, :, pl.ds(0, HP)], diag)
        r.OT[j, :, rows_of(p)] = ot
        r.OB[rows_of(p), HD * j : HD * (j + 1)] = ot.T.astype(BF16)

    def to_sibling(st, p, value):
        r.PF[p] = value.reshape(2, T, D)
        r.ES[st, p] = r.PF[p, 1 - c].astype(BF16)
        send(lambda: copy(r.ES.at[st, p], r.ER.at[st, p], r.s_e.at[st, p], r.r_e.at[st, p], sib))

    def chip_sum(st, p):
        arrive(lambda: copy(r.ES.at[st, p], r.ER.at[st, p], r.s_e.at[st, p], r.r_e.at[st, p], sib))
        return r.PF[p, c] + r.ER[st, p].astype(F32)

    def xslot(st, p):
        return 2 * st + p if st < 2 else st + 2

    def xcopy(st, p):
        i = xslot(st, p)
        return copy(r.XS.at[i], r.XR.at[i], r.s_x.at[i], r.r_x.at[i], xp)

    def to_x(st, p):
        r.XS[xslot(st, p)] = chip_sum(st, p).astype(BF16)
        send(lambda: xcopy(st, p))

    def pair_sum(st, p):
        arrive(lambda: xcopy(st, p))
        return r.XS[xslot(st, p)].astype(F32) + r.XR[xslot(st, p)].astype(F32)

    def share(name, st, p):
        mk = lambda i: copy(name.at[i], name.at[i], r.s_h.at[st, p], r.r_h.at[st, p], sib)
        send(lambda: mk(2 * p + c))
        return lambda: arrive(lambda: mk(2 * p + (1 - c)))

    def out_proj(p):
        to_sibling(0, p, nn(r.OB[rows_of(p)], W2[:, :, pl.ds(0, D)].reshape(HW, D)))

    for j in range(NH):
        attend(0, j)
    for d in range(3, nz):
        g_out[1](d)
    out_proj(0)
    attend(1, 0)
    attend(1, 1)
    to_x(0, 0)
    g_up[1](1)
    g_dn[1](1)
    attend(1, 2)
    attend(1, 3)
    out_proj(1)
    to_x(0, 1)
    for d in range(2, nz):
        g_up[1](d)
        g_dn[1](d)

    r.SGA[...] = jnp.zeros_like(r.SGA)

    def middle(p):
        mid = r.X[2 * p + c].astype(F32) + pair_sum(0, p)
        r.MID[p] = mid
        inv = lax.rsqrt(jnp.mean(mid * mid, axis=1, keepdims=True) + epsilon)
        r.HN2[2 * p + c] = (mid * inv * gain_ffn).astype(BF16)
        return share(r.HN2, 0, p)

    def w_up():
        return W1[:, :, :, pl.ds(0, HW)].reshape(D, HW)

    def feed(p):
        hn = r.HN2[pl.ds(2 * p, 2)].reshape(HP, D)
        u = nn(hn, w_up()) + bias_up
        sig = 1.0 / (1.0 + jnp.exp(-u))
        r.ACT[rows_of(p)] = (u * sig).astype(BF16)
        dy = r.DY[pl.ds(2 * p, 2)].reshape(HP, D)
        dact = nt(dy, W2[:, :, pl.ds(D, D)].reshape(HW, D))
        dup = (dact * sig * (1.0 + u * (1.0 - sig))).astype(BF16)
        r.DUP[rows_of(p), 0:HW] = dup
        to_sibling(1, p, nt(dup, w_up()))
        row = pl.ds(4 + s, 1)
        r.SGA[row, 0:HW] = r.SGA[row, 0:HW] + jnp.sum(dup.astype(F32), axis=0, keepdims=True)

    def transpose_hn2(p):
        for k in range(2):
            t = r.HN2[2 * p + k].astype(F32).T.astype(BF16)
            r.HN2T[:, :, pl.ds((2 * p + k) * T, T)] = t.reshape(2 * nz, 2 * CB, T)

    r.DUP[:, 256:384] = jnp.zeros((L, 128), BF16)
    r.DQ[:, 0:128] = jnp.zeros((L, 128), BF16)
    wait_hn = middle(0)
    g_up[2]()
    g_dn[2]()
    wait_hn()
    feed(0)
    transpose_hn2(0)
    wait_hn = middle(1)
    to_x(1, 0)
    wait_hn()
    feed(1)
    transpose_hn2(1)

    def scatter_item(idx, part, yr, zu, zd, zcond, y_first=True):
        yc = lambda zz: copy(part(zz, 1 - y), yr(zz), r.s_ry.at[idx, zz], r.r_ry.at[idx, zz], yp)
        up = lambda zz: copy(part(zz, y), zu(zz), r.s_ru.at[idx, zz], r.r_ru.at[idx, zz], zup)
        dn = lambda zz: copy(part(zz, y), zd(zz), r.s_rd.at[idx, zz], r.r_rd.at[idx, zz], zdn)

        def add(zz, other):
            part(zz, y)[...] = (part(zz, y)[...].astype(F32) + other(zz)[...].astype(F32)).astype(BF16)

        ycond = None if zcond is None else jnp.logical_not(zcond)

        def start(d):
            if d:
                send(lambda: yc(z + d), both(z + d < nz, ycond))
                send(lambda: yc(z - d), both(z - d >= 0, ycond))
            else:
                send(lambda: yc(z), ycond)

        def step(d):
            if d:
                ok = both(zcond, z + d < nz)
                from_below = both(ok, z > 0)
                if y_first:
                    arrive(lambda: yc(z + d), ok)
                    when(ok, lambda: add(z + d, yr))
                arrive(lambda: up(z + d), from_below)
                when(from_below, lambda: add(z + d, zu))
                send(lambda: up(z + d), ok)
                ok2 = both(zcond, z - d >= 0)
                from_above = both(ok2, z < nz - 1)
                if y_first:
                    arrive(lambda: yc(z - d), ok2)
                    when(ok2, lambda: add(z - d, yr))
                arrive(lambda: dn(z - d), from_above)
                when(from_above, lambda: add(z - d, zd))
                send(lambda: dn(z - d), ok2)
            else:
                below, above = both(zcond, z > 0), both(zcond, z < nz - 1)
                arrive(lambda: up(z), below)
                when(below, lambda: add(z, zu))
                arrive(lambda: dn(z), above)
                when(above, lambda: add(z, zd))
                if y_first:
                    arrive(lambda: yc(z), zcond)
                    when(zcond, lambda: add(z, yr))

        return start, step

    far = range(nz - 1, 0, -1)
    cut_up = pl.ds(0, LO)
    s_up = scatter_item(
        0,
        lambda zz, q: r.G1.at[2 * zz + q, :, :, cut_up],
        lambda zz: r.YR1.at[zz, :, :, cut_up],
        lambda zz: r.ZU1.at[zz - 1, :, :, cut_up],
        lambda zz: r.ZD1.at[zz, :, :, cut_up],
        None,
    )

    def qkv_item(idx, xx, cut):
        return scatter_item(
            idx,
            lambda zz, q: r.G1.at[2 * zz + q, xx, :, cut],
            lambda zz: r.YR1.at[zz, xx, :, cut],
            lambda zz: r.ZU1.at[zz - 1, xx, :, cut],
            lambda zz: r.ZD1.at[zz, xx, :, cut],
            None,
        )

    def together(items):
        def start(d):
            for it in items:
                it[0](d)

        def step(d):
            for it in items:
                it[1](d)

        return start, step

    def w2_item(idx, lo, width, zcond, y_first):
        cut = pl.ds(lo, width)
        return scatter_item(
            idx,
            lambda zz, q: r.G2.at[zz, :, cut],
            lambda zz: r.YR2.at[zz, :, cut],
            lambda zz: r.ZU2.at[zz - 1, :, cut],
            lambda zz: r.ZD2.at[zz, :, cut],
            zcond,
            y_first,
        )

    s_dn = w2_item(1, D, D, mine, True)
    WZ = D // 2
    s_out = w2_item(2, 0, WZ, None, False)
    s_out2 = w2_item(5, WZ, D - WZ, mine, True) if WZ < D else ((lambda d: None), (lambda d: None))
    fars = [qkv_item(3, 1 - x, cuts[0]), qkv_item(6, 1 - x, cuts[1])]
    owns = [qkv_item(4, x, cuts[0]), qkv_item(7, x, cuts[1])]
    s_far, s_own = together(fars), together(owns)

    gu = nn(r.HN2T[...].reshape(D, L), r.DUP[...])
    r.G1[:, :, :, 0:384] = gu.astype(BF16).reshape(2 * nz, 2, CB, 384)
    for d in (*far, 0):
        s_up[0](d)
    to_x(1, 1)
    dy_all = r.DY[...].reshape(L, D)
    r.G2[:, :, pl.ds(D, D)] = tn(r.ACT[...], dy_all).astype(BF16).reshape(nz, CB, D)
    for d in (*far, 0):
        s_dn[0](d)

    def back_middle(p):
        dh = pair_sum(1, p)
        mid = r.MID[p]
        inv = lax.rsqrt(jnp.mean(mid * mid, axis=1, keepdims=True) + epsilon)
        n = mid * inv
        dn = dh * gain_ffn
        dmid = r.DY[2 * p + c].astype(F32) + inv * (
            dn - n * jnp.mean(dn * n, axis=1, keepdims=True)
        )
        r.DMID[p] = dmid
        r.DA[2 * p + c] = dmid.astype(BF16)
        own = jnp.where(x == p, jnp.sum(dh * n, axis=0, keepdims=True), 0.0)
        r.SGA[1:2] = r.SGA[1:2] + own
        return share(r.DA, 1, p)

    def back_out(p):
        da = r.DA[pl.ds(2 * p, 2)].reshape(HP, D)
        r.QKV[0:HP, 0:HW] = nt(da, W2[:, :, pl.ds(0, D)].reshape(HW, D))

    def back_attend(p, j):
        do = r.QKV[0:HP, HD * j : HD * (j + 1)].astype(BF16)
        dof = do.astype(F32)
        delta = jnp.sum(dof.T * r.OT[j, :, rows_of(p)], axis=0, keepdims=True)
        span = HP * (p + 1)
        pt = r.PT1[j] if p else r.PT0[j]
        dpt = nt(r.VH[j, pl.ds(0, span)], do)
        dst = (pt.astype(F32) * (dpt - delta)).astype(BF16)
        dv = nn(pt, do)
        dk = nn(dst, r.QH[j, rows_of(p)])
        dq = nn(r.KT[j, :, pl.ds(0, span)], dst).T
        raw = r.QRAW[j, rows_of(p)]
        r.SGA[3:4, 0:HD] = r.SGA[3:4, 0:HD] + jnp.sum(dq * raw, axis=0, keepdims=True)
        r.DQ[rows_of(p), off + HD * j : off + HD * (j + 1)] = (dq * factor).astype(BF16)
        ko, vo = off + HW + HD * j, off + 2 * HW + HD * j
        if p == 0:
            r.DKA[j] = dk
            r.DVA[j] = dv
        else:
            r.DQ[0:HP, ko : ko + HD] = (dk[:HP] + r.DKA[j]).astype(BF16)
            r.DQ[HP:L, ko : ko + HD] = dk[HP:].astype(BF16)
            r.DQ[0:HP, vo : vo + HD] = (dv[:HP] + r.DVA[j]).astype(BF16)
            r.DQ[HP:L, vo : vo + HD] = dv[HP:].astype(BF16)

    def down_proj(p):
        to_sibling(2, p, nn(r.ACT[rows_of(p)], W2[:, :, pl.ds(D, D)].reshape(HW, D)))

    wait_da = back_middle(0)
    down_proj(0)
    down_proj(1)
    if nz > 3:
        s_up[1](3)
    wait_da()
    back_out(0)
    for j in range(NH):
        back_attend(0, j)
    if nz > 2:
        s_up[1](2)
    wait_da = back_middle(1)
    r.XS[4] = chip_sum(2, 1 - x).astype(BF16)
    send(lambda: xcopy(2, 0))
    r.PF2[...] = chip_sum(2, x)
    s_up[1](1)
    if nz > 3:
        s_dn[1](3)
    wait_da()
    back_out(1)
    da_all = r.DA[...].reshape(L, D)
    r.G2[:, :, pl.ds(0, D)] = tn(r.OB[...], da_all).astype(BF16).reshape(nz, CB, D)
    if nz > 3:
        s_out[1](3)
    for d in (*far, 0):
        s_out2[0](d)
    for j in range(NH):
        back_attend(1, j)

    def qkv_block(bb):
        t = nn(r.HN1T[bb], r.DQ[...]).reshape(2, CB, D - LO)
        head = t[:, :, 0:128] + r.G1[bb, :, :, pl.ds(LO, 128)].astype(F32)
        r.G1[bb, :, :, pl.ds(LO, 128)] = head.astype(BF16)
        r.G1[bb, :, :, pl.ds(384, D - 384)] = t[:, :, 128:].astype(BF16)

    for d in far:
        pl.when(z + d < nz)(lambda: qkv_block(2 * (z + d) + (1 - y)))
        pl.when(z - d >= 0)(lambda: qkv_block(2 * (z - d) + (1 - y)))
        s_far[0](d)
        s_own[0](d)
    qkv_block(2 * z + (1 - y))
    s_far[0](0)
    s_own[0](0)
    for k in range(nz):
        qkv_block(2 * k + y)

    for p in range(2):
        w = W1[:, :, :, pl.ds(LO, D - LO)].reshape(D, D - LO)
        to_sibling(3, p, nt(r.DQ[rows_of(p)], w))
    s_up[1](0)
    if nz > 2:
        s_dn[1](2)
    arrive(lambda: xcopy(2, 0))
    own_out = r.PF2[...] + r.XR[4].astype(F32)
    mixed_o[...] = (r.MID[x] + own_out + bias_down).astype(BF16)
    r.XS[5] = chip_sum(3, 1 - x).astype(BF16)
    send(lambda: xcopy(3, 0))
    r.PF2[...] = chip_sum(3, x)
    s_dn[1](1)
    if nz > 2:
        s_out[1](2)
    if nz > 3:
        s_out2[1](3)
        s_far[1](3)
        s_own[1](3)
    s_dn[1](0)
    if nz > 2:
        s_far[1](2)
    s_out[1](1)
    if nz > 2:
        s_out2[1](2)
        s_own[1](2)

    arrive(lambda: xcopy(3, 0))
    dh = r.PF2[...] + r.XR[5].astype(F32)
    xv = r.X[s].astype(F32)
    inv = lax.rsqrt(jnp.mean(xv * xv, axis=1, keepdims=True) + epsilon)
    n = xv * inv
    dn = dh * gain_attn
    gtok_o[...] = r.DMID[x] + inv * (dn - n * jnp.mean(dn * n, axis=1, keepdims=True))
    r.SGA[0:1] = jnp.sum(dh * n, axis=0, keepdims=True)
    r.SGA[2:3] = jnp.sum(r.DY[s].astype(F32), axis=0, keepdims=True)

    def small_copy(k, slot, dev):
        return lambda: copy(
            r.SGA if k == 0 else r.SGS.at[k - 1], r.SGR.at[slot], r.s_sg.at[slot], r.r_sg.at[slot], dev
        )

    total = r.SGA[...]
    for k, dev in enumerate((sib, xp, yp)):
        mk = small_copy(k, k, dev)
        send(mk)
        if k == 2:
            s_far[1](1)
            s_own[1](1)
            cut_o = pl.ds(0, WZ)
            s_out[1](0)
            m_gy = lambda: copy(
                r.G2.at[z, :, cut_o], r.YR2.at[z, :, cut_o], r.s_one.at[15], r.r_one.at[15], yp
            )
            send(m_gy, not_mine)
            ends = (pl.ds(0, LO + half), pl.ds(LO + half, half))

            def m_fx(k):
                return copy(
                    r.G1.at[b, 1 - x, :, ends[k]], r.FX.at[:, ends[k]], r.s_fx.at[k], r.r_fx.at[k], xp
                )

            for h in range(2):
                fars[h][1](0)
                send(lambda h=h: m_fx(h))
            s_out2[1](1)
        arrive(mk)
        total = total + r.SGR[k]
        r.SGS[k] = total
    mks = []
    for k in range(1, nz):
        mk = small_copy(3, 2 + k, (2 * lax.rem(z + k, nz) + y, s))
        send(mk)
        mks.append(mk)
    s_out2[1](0)

    def hand_over(k, h, xx, block):
        cut = ends[h]
        done = block.astype(F32)
        r.GF[0, xx, :, cut] = done[:RW]
        r.GF[1, xx, :, cut] = done[RW:]
        mk = lambda: copy(
            r.GF.at[1 - c, xx, :, cut], r.GRV.at[xx, :, cut], r.s_gf.at[k, h], r.r_gf.at[k, h], sib
        )
        send(mk)
        o1[xx, c, :, cut] = r.GF[c, xx, :, cut]

        def take():
            arrive(mk)
            o1[xx, 1 - c, :, cut] = r.GRV[xx, :, cut]

        return take

    takes = []
    for h in range(2):
        arrive(lambda h=h: m_fx(h))
        takes.append(hand_over(0, h, 1 - x, r.FX[:, ends[h]]))
    for h in range(2):
        owns[h][1](0)
        takes.append(hand_over(1, h, x, r.G1[b, x, :, ends[h]]))
    arrive(m_gy, mine)

    def out_from_y():
        r.G2[z, :, cut_o] = (r.G2[z, :, cut_o].astype(F32) + r.YR2[z, :, cut_o].astype(F32)).astype(BF16)

    when(mine, out_from_y)
    done2 = r.G2[z].astype(F32)
    r.GF2[0] = done2[:RW]
    r.GF2[1] = done2[RW:]
    m_g2 = lambda: copy(r.GF2.at[1 - c], r.GR2, r.s_one.at[12], r.r_one.at[12], sib)
    send(m_g2, mine)
    for take in takes:
        take()
    for k, mk in enumerate(mks):
        arrive(mk)
        total = total + r.SGR[3 + k]
    sg_o[...] = total
    arrive(m_g2, not_mine)

    def out2_own():
        o2[...] = r.GF2[c]

    def out2_sib():
        o2[...] = r.GR2[...]

    when(mine, out2_own)
    when(not_mine, out2_sib)

    for make, cond in drains:
        when(cond, lambda make=make: make().wait_send())


def fused_layer(nb, ns, tokens, wqkv, wout, wup, wdown, gattn, gffn, bup, bdown, scale_param, cot):
    nz = nb // 2
    rows, D = wout.shape
    T = tokens.shape[1]
    L = ns * T
    V = pltpu.VMEM
    scratch = dict(
        WQ=V((rows, 3 * D), BF16),
        WU=V((rows, D), BF16),
        WO=V((rows, D), BF16),
        WD=V((rows, D), BF16),
        SM=V((8, 128), F32),
        W1P=V((2, 2, 48, D), BF16),
        W2P=V((48, 2 * D), BF16),
        SIB1=V((2, 48, D), BF16),
        SIB2=V((48, 2 * D), BF16),
        CB1=V((HD, D), BF16),
        W1=V((nb, 2, HD, D), BF16),
        W2=V((nz, HD, 2 * D), BF16),
        S=V((nb, 4, 8, 128), F32),
        X=V((4, T, D), BF16),
        DY=V((4, T, D), BF16),
        ROWS=V((8, D), F32),
        BUP=V((8, 4 * HD), F32),
        HN1=V((L, D), BF16),
        HN1T=V((nb, 2 * HD, L), BF16),
        HN2T=V((nb, 2 * HD, L), BF16),
        QKV=V((L, D - 256), F32),
        QRAW=V((4, L, HD), F32),
        QH=V((4, L, HD), BF16),
        KH=V((4, L, HD), BF16),
        VH=V((4, L, HD), BF16),
        KT=V((4, HD, L), BF16),
        VT=V((4, HD, L), BF16),
        PT0=V((4, L // 2, L // 2), BF16),
        PT1=V((4, L, L // 2), BF16),
        OT=V((4, HD, L), F32),
        OB=V((L, 4 * HD), BF16),
        PF=V((2, 2, T, D), F32),
        PF2=V((T, D), F32),
        ES=V((4, 2, T, D), BF16),
        ER=V((4, 2, T, D), BF16),
        XS=V((6, T, D), BF16),
        XR=V((6, T, D), BF16),
        MID=V((2, T, D), F32),
        HN2=V((4, T, D), BF16),
        ACT=V((L, 4 * HD), BF16),
        DUP=V((L, 384), BF16),
        DA=V((4, T, D), BF16),
        DMID=V((2, T, D), F32),
        DQ=V((L, D - 256), BF16),
        DKA=V((4, L // 2, HD), F32),
        DVA=V((4, L // 2, HD), F32),
        G1=V((nb, 2, HD, D), BF16),
        G2=V((nz, HD, 2 * D), BF16),
        YR1=V((nz, 2, HD, D), BF16),
        ZU1=V((nz - 1, 2, HD, D), BF16),
        ZD1=V((nz - 1, 2, HD, D), BF16),
        YR2=V((nz, HD, 2 * D), BF16),
        ZU2=V((nz - 1, HD, 2 * D), BF16),
        ZD2=V((nz - 1, HD, 2 * D), BF16),
        FX=V((HD, D), BF16),
        GF=V((2, 2, rows, D), F32),
        GRV=V((2, rows, D), F32),
        GF2=V((2, rows, 2 * D), F32),
        GR2=V((rows, 2 * D), F32),
        SGA=V((8, D), F32),
        SGS=V((3, 8, D), F32),
        SGR=V((2 + nz, 8, D), F32),
    )
    dma = pltpu.SemaphoreType.DMA
    scratch.update(
        s_in=dma((6,)),
        s_x1=dma((3,)), r_x1=dma((3,)),
        s_gf=dma((2, 2)), r_gf=dma((2, 2)),
        s_fx=dma((2,)), r_fx=dma((2,)),
        s_one=dma((16,)), r_one=dma((16,)),
        s_up=dma((9, nz)), r_up=dma((9, nz)),
        s_dn=dma((9, nz)), r_dn=dma((9, nz)),
        s_y=dma((9, nz)), r_y=dma((9, nz)),
        s_e=dma((4, 2)), r_e=dma((4, 2)),
        s_x=dma((6,)), r_x=dma((6,)),
        s_h=dma((2, 2)), r_h=dma((2, 2)),
        s_ry=dma((8, nz)), r_ry=dma((8, nz)),
        s_ru=dma((8, nz)), r_ru=dma((8, nz)),
        s_rd=dma((8, nz)), r_rd=dma((8, nz)),
        s_sg=dma((2 + nz,)), r_sg=dma((2 + nz,)),
    )
    vmem = pl.BlockSpec(memory_space=pltpu.VMEM)
    hbm = pl.BlockSpec(memory_space=pl.ANY)
    mixed, gtok, o1, o2, sg = pl.pallas_call(
        functools.partial(layer_kernel, nz, tuple(scratch)),
        out_shape=(
            jax.ShapeDtypeStruct((T, D), BF16),
            jax.ShapeDtypeStruct((T, D), F32),
            jax.ShapeDtypeStruct((2, 2, rows, D), F32),
            jax.ShapeDtypeStruct((rows, 2 * D), F32),
            jax.ShapeDtypeStruct((8, D), F32),
        ),
        in_specs=[hbm] * 6 + [vmem] * 5,
        out_specs=(vmem,) * 5,
        scratch_shapes=list(scratch.values()),
        compiler_params=pltpu.CompilerParams(
            collective_id=0, has_side_effects=True, vmem_limit_bytes=63 << 20
        ),
        name="decoder_layer",
    )(tokens[0], cot[0], wqkv, wout, wup, wdown, gattn, gffn, bup, bdown, scale_param)
    mixed, gtok, gqkv, gout, gup, gdown, g_attn, g_ffn, g_bup, g_bdown, gscale = pl.pallas_call(
        functools.partial(outputs_kernel, ns),
        out_shape=(
            jax.ShapeDtypeStruct((T, D), BF16),
            jax.ShapeDtypeStruct((T, D), F32),
            jax.ShapeDtypeStruct((rows, 3 * D), F32),
            jax.ShapeDtypeStruct((rows, D), F32),
            jax.ShapeDtypeStruct((rows, D), F32),
            jax.ShapeDtypeStruct((rows, D), F32),
            jax.ShapeDtypeStruct((rows,), F32),
            jax.ShapeDtypeStruct((rows,), F32),
            jax.ShapeDtypeStruct((rows,), F32),
            jax.ShapeDtypeStruct((rows,), F32),
            jax.ShapeDtypeStruct((HD,), F32),
        ),
        in_specs=[vmem] * 6,
        out_specs=(vmem,) * 11,
        compiler_params=pltpu.CompilerParams(vmem_limit_bytes=63 << 20),
        name="place_outputs",
    )(mixed, gtok, o1, o2, sg, scale_param)
    return mixed[None], gtok[None], gqkv, gout, gup, gdown, g_attn, g_ffn, g_bup, g_bdown, gscale


def outputs_kernel(ns, mixed, gtok, o1, o2, sg, scl, mixed_o, gtok_o, gqkv, gout, gup, gdown, *small):
    rows, D = gup.shape
    HW = 4 * HD
    mixed_o[...] = mixed[...]
    gtok_o[...] = gtok[...]
    gout[...] = o2[:, 0:D]
    gdown[...] = o2[:, D : 2 * D]
    for xx in range(2):
        for cc in range(2):
            for t in range(4):
                for j in range(4):
                    v = o1[xx, cc, :, HW * t + HD * j : HW * t + HD * (j + 1)]
                    at = HD * (4 * j + 2 * cc + xx)
                    if t == 0:
                        gup[:, at : at + HD] = v
                    else:
                        gqkv[:, D * (t - 1) + at : D * (t - 1) + at + HD] = v
    first = (lax.axis_index("batch") * ns + lax.axis_index("seq")) * rows
    parts = []
    for h in range(H):
        j, cc, xx = h // 4, (h // 2) % 2, h % 2
        row = 4 + 2 * xx + cc
        parts.append(sg[row : row + 1, HD * j : HD * (j + 1)])
    bias_up = jnp.concatenate(parts, axis=1)
    shift = lax.rem(D - first, D)
    for ref, v in zip(small, (sg[0:1], sg[1:2], bias_up, sg[2:3])):
        v = jnp.broadcast_to(v, (8, D))
        ref[...] = pltpu.roll(v, shift, 1)[0, 0:rows]
    scale = scl[...].astype(F32).reshape(1, HD)
    small[4][...] = (sg[3:4, 0:HD] * (soft_unit / math.sqrt(HD)) / (1.0 + jnp.exp(-scale)))[0]


def layer_step(nb, ns, *args):
    if fits_fused(nb, ns, args[0], args[1], args[3]):
        return fused_layer(nb, ns, *args)
    return generic_layer(*args)


def solution(mesh):
    return jax.shard_map(
        functools.partial(layer_step, mesh.shape["batch"], mesh.shape["seq"]),
        mesh=mesh,
        in_specs=(
            P("batch", "seq", None),
            P(("batch", "seq"), None),
            P(("batch", "seq"), None),
            P(("batch", "seq"), None),
            P(("batch", "seq"), None),
            P(("batch", "seq")),
            P(("batch", "seq")),
            P(("batch", "seq")),
            P(("batch", "seq")),
            P(),
            P("batch", "seq", None),
        ),
        out_specs=(
            P("batch", "seq", None),
            P("batch", "seq", None),
            P(("batch", "seq"), None),
            P(("batch", "seq"), None),
            P(("batch", "seq"), None),
            P(("batch", "seq"), None),
            P(("batch", "seq")),
            P(("batch", "seq")),
            P(("batch", "seq")),
            P(("batch", "seq")),
            P(),
        ),
        check_vma=False,
    )
```

```python
import functools
import math
import types

import jax
import jax.numpy as jnp
from jax import lax
from jax.experimental import pallas as pl
from jax.experimental.pallas import tpu as pltpu
from jax.sharding import PartitionSpec as P

H = 16
HD = 80


epsilon = 1e-06
soft_unit = 1.442695041
neg_large = -1e30


def norm_forward(values, gain):
    inverse = lax.rsqrt(jnp.mean(values * values, axis=1, keepdims=True) + epsilon)
    return (inverse, (values * inverse * gain.astype(jnp.float32)).astype(jnp.bfloat16))


def norm_back(grad_out, values, inverse, gain):
    normed = values * inverse
    scaled = grad_out * gain.astype(jnp.float32)
    grad_gain = jnp.sum(grad_out * normed, axis=0)
    grad_in = inverse * (scaled - normed * jnp.mean(scaled * normed, axis=1, keepdims=True))
    return (grad_in, grad_gain)


def generic_layer(
    tokens,
    query_key_value_weight,
    attention_output_weight,
    up_projection_weight,
    down_projection_weight,
    gain_attn,
    gain_ffn,
    up_projection_bias,
    down_projection_bias,
    scale_param,
    cotangent,
):
    seq_local, tok_seq, width = tokens.shape
    row_count = seq_local * tok_seq
    shards = (
        query_key_value_weight,
        attention_output_weight,
        up_projection_weight,
        down_projection_weight,
        gain_attn,
        gain_ffn,
        up_projection_bias,
        down_projection_bias,
    )
    fwd_weights = (
        lax.all_gather(shards[0], ("batch", "seq"), axis=0, tiled=True),
        lax.all_gather(shards[1], ("batch", "seq"), axis=0, tiled=True),
        lax.all_gather(shards[2], ("batch", "seq"), axis=0, tiled=True),
        lax.all_gather(shards[3], ("batch", "seq"), axis=0, tiled=True),
        lax.all_gather(shards[4], ("batch", "seq"), axis=0, tiled=True),
        lax.all_gather(shards[5], ("batch", "seq"), axis=0, tiled=True),
        lax.all_gather(shards[6], ("batch", "seq"), axis=0, tiled=True),
        lax.all_gather(shards[7], ("batch", "seq"), axis=0, tiled=True),
    )
    wqkv_full, wout_full, wup_full, wdown_full, gattn_full, gffn_full, bup_full, bdown_full = (
        fwd_weights
    )
    inputs = tokens.astype(jnp.float32).reshape(row_count, width)
    inv_attn, attention_normed_input = norm_forward(inputs, gattn_full)
    query_key_value = jnp.dot(attention_normed_input, wqkv_full, preferred_element_type=jnp.float32)
    q_raw = query_key_value[:, :width]
    scale_float = scale_param.astype(jnp.float32)
    factor = soft_unit / math.sqrt(HD) * jax.nn.softplus(scale_float)
    factor_row = jnp.tile(factor, H)
    queries = (q_raw * factor_row).astype(jnp.bfloat16)
    keys_own = (
        query_key_value[:, width : 2 * width]
        .astype(jnp.bfloat16)
        .reshape(seq_local, tok_seq, width)
    )
    values_own = (
        query_key_value[:, 2 * width :].astype(jnp.bfloat16).reshape(seq_local, tok_seq, width)
    )
    keys_all, values_all = (
        lax.all_gather(keys_own, "seq", axis=1, tiled=True),
        lax.all_gather(values_own, "seq", axis=1, tiled=True),
    )
    position = lax.axis_index("seq")
    block_total = lax.axis_size("seq")
    query_pos = position * tok_seq + jnp.arange(tok_seq, dtype=jnp.int32)
    key_offsets = jnp.arange(tok_seq, dtype=jnp.int32)
    queries_h = queries.reshape(seq_local, tok_seq, H, HD)

    def key_block(source, block):
        piece = lax.dynamic_slice_in_dim(source, block * tok_seq, tok_seq, 1)
        return piece.reshape(seq_local, tok_seq, H, HD)

    def block_scores(block):
        scores = jnp.einsum(
            "sqhd,skhd->shqk",
            queries_h,
            key_block(keys_all, block),
            preferred_element_type=jnp.float32,
        )
        allowed = (block * tok_seq + key_offsets)[None, :] <= query_pos[:, None]
        return jnp.where(allowed, scores, neg_large)

    def max_step(block, carry):
        top, total = carry
        scores = block_scores(block)
        new_top = jnp.maximum(top, jnp.max(scores, axis=3, keepdims=True))
        total = total * jnp.exp(top - new_top) + jnp.sum(
            jnp.exp(scores - new_top), axis=3, keepdims=True
        )
        return (new_top, total)

    start_top = jnp.full((seq_local, H, tok_seq, 1), neg_large, jnp.float32)
    top, total = lax.fori_loop(0, block_total, max_step, (start_top, jnp.zeros_like(start_top)))
    log_sum = top + jnp.log(total)

    def value_step(block, accum):
        probs = jnp.exp(block_scores(block) - log_sum).astype(jnp.bfloat16)
        return accum + jnp.einsum(
            "shqk,skhd->sqhd",
            probs,
            key_block(values_all, block),
            preferred_element_type=jnp.float32,
        )

    attention_output = lax.fori_loop(
        0, block_total, value_step, jnp.zeros((seq_local, tok_seq, H, HD), jnp.float32)
    )
    attention_output = attention_output.reshape(row_count, width)
    att_low = attention_output.astype(jnp.bfloat16)
    middle = inputs + jnp.dot(att_low, wout_full, preferred_element_type=jnp.float32)
    inv_ffn, feedforward_normed_input = norm_forward(middle, gffn_full)
    up_projected_value = jnp.dot(
        feedforward_normed_input, wup_full, preferred_element_type=jnp.float32
    ) + bup_full.astype(jnp.float32)
    act_low = jax.nn.silu(up_projected_value).astype(jnp.bfloat16)
    result = (
        middle
        + jnp.dot(act_low, wdown_full, preferred_element_type=jnp.float32)
        + bdown_full.astype(jnp.float32)
    )
    mixed = result.astype(jnp.bfloat16).reshape(seq_local, tok_seq, width)
    back_weights = (
        lax.all_gather(shards[0], ("batch", "seq"), axis=0, tiled=True),
        lax.all_gather(shards[1], ("batch", "seq"), axis=0, tiled=True),
        lax.all_gather(shards[2], ("batch", "seq"), axis=0, tiled=True),
        lax.all_gather(shards[3], ("batch", "seq"), axis=0, tiled=True),
        lax.all_gather(shards[4], ("batch", "seq"), axis=0, tiled=True),
        lax.all_gather(shards[5], ("batch", "seq"), axis=0, tiled=True),
        lax.all_gather(shards[6], ("batch", "seq"), axis=0, tiled=True),
        lax.all_gather(shards[7], ("batch", "seq"), axis=0, tiled=True),
    )
    wqkv_back, wout_back, wup_back, wdown_back, gattn_back, gffn_back, bup_back, bdown_back = (
        back_weights
    )
    grad_low = cotangent.reshape(row_count, width)
    grad_float = grad_low.astype(jnp.float32)
    grad_down = jnp.einsum("rf,rd->fd", act_low, grad_low, preferred_element_type=jnp.float32)
    grad_bias_down = jnp.sum(grad_float, axis=0)
    grad_act = jnp.einsum("rd,fd->rf", grad_low, wdown_back, preferred_element_type=jnp.float32)
    sigma = jax.nn.sigmoid(up_projected_value)
    grad_upv = (grad_act * sigma * (1.0 + up_projected_value * (1.0 - sigma))).astype(jnp.bfloat16)
    grad_up = jnp.einsum(
        "rd,rf->df", feedforward_normed_input, grad_upv, preferred_element_type=jnp.float32
    )
    grad_bias_up = jnp.sum(grad_upv.astype(jnp.float32), axis=0)
    grad_hn_ffn = jnp.einsum("rf,df->rd", grad_upv, wup_back, preferred_element_type=jnp.float32)
    grad_norm_ffn, grad_gain_ffn = norm_back(grad_hn_ffn, middle, inv_ffn, gffn_back)
    grad_middle = grad_float + grad_norm_ffn
    grad_attn = grad_middle.astype(jnp.bfloat16)
    grad_out = jnp.einsum("rd,re->de", att_low, grad_attn, preferred_element_type=jnp.float32)
    block_summed = (
        lax.psum_scatter(grad_out, ("batch", "seq"), scatter_dimension=0, tiled=True),
        lax.psum_scatter(grad_up, ("batch", "seq"), scatter_dimension=0, tiled=True),
        lax.psum_scatter(grad_down, ("batch", "seq"), scatter_dimension=0, tiled=True),
        lax.psum_scatter(grad_gain_ffn, ("batch", "seq"), scatter_dimension=0, tiled=True),
        lax.psum_scatter(grad_bias_up, ("batch", "seq"), scatter_dimension=0, tiled=True),
        lax.psum_scatter(grad_bias_down, ("batch", "seq"), scatter_dimension=0, tiled=True),
    )
    grad_att_low = jnp.einsum(
        "re,de->rd", grad_attn, wout_back, preferred_element_type=jnp.float32
    ).astype(jnp.bfloat16)
    grad_heads = grad_att_low.reshape(seq_local, tok_seq, H, HD)
    delta = jnp.sum(
        (grad_att_low.astype(jnp.float32) * attention_output).reshape(seq_local, tok_seq, H, HD),
        axis=3,
    )
    delta = jnp.transpose(delta, (0, 2, 1))[..., None]
    query_init = jnp.zeros((seq_local, tok_seq, H, HD), jnp.float32)

    def grad_step(block, carry):
        grad_query, term = carry
        scores = block_scores(block)
        probs = jnp.exp(scores - log_sum)
        keys_blk = key_block(keys_all, block)
        values_blk = key_block(values_all, block)
        grad_probs = jnp.einsum(
            "sqhd,skhd->shqk", grad_heads, values_blk, preferred_element_type=jnp.float32
        )
        grad_scores = (probs * (grad_probs - delta)).astype(jnp.bfloat16)
        grad_values = jnp.einsum(
            "shqk,sqhd->skhd",
            probs.astype(jnp.bfloat16),
            grad_heads,
            preferred_element_type=jnp.float32,
        )
        grad_keys = jnp.einsum(
            "shqk,sqhd->skhd", grad_scores, queries_h, preferred_element_type=jnp.float32
        )
        grad_query = grad_query + jnp.einsum(
            "shqk,skhd->sqhd", grad_scores, keys_blk, preferred_element_type=jnp.float32
        )
        piece = jnp.concatenate(
            [
                grad_keys.reshape(seq_local, tok_seq, width),
                grad_values.reshape(seq_local, tok_seq, width),
            ],
            axis=2,
        )
        term = lax.dynamic_update_slice_in_dim(term, piece, block * tok_seq, 1)
        return (grad_query, term)

    term_init = jnp.zeros((seq_local, tok_seq * block_total, 2 * width), jnp.float32)
    grad_query, term = lax.fori_loop(0, block_total, grad_step, (query_init, term_init))
    kv_grads = lax.psum_scatter(
        term.astype(jnp.bfloat16), "seq", scatter_dimension=1, tiled=True
    ).astype(jnp.float32)
    grad_scaled = grad_query.reshape(row_count, width)
    scale_local = jnp.sum((grad_scaled * q_raw).reshape(row_count, H, HD), axis=(0, 1))
    scale_total = lax.psum(scale_local, ("batch", "seq"))
    grad_scale = scale_total * (soft_unit / math.sqrt(HD)) * jax.nn.sigmoid(scale_float)
    grad_qkv_low = jnp.concatenate(
        [grad_scaled * factor_row, kv_grads.reshape(row_count, 2 * width)], axis=1
    ).astype(jnp.bfloat16)
    grad_qkv = jnp.einsum(
        "rd,re->de", attention_normed_input, grad_qkv_low, preferred_element_type=jnp.float32
    )
    grad_hn_attn = jnp.einsum(
        "re,de->rd", grad_qkv_low, wqkv_back, preferred_element_type=jnp.float32
    )
    grad_norm_attn, grad_gain_attn = norm_back(grad_hn_attn, inputs, inv_attn, gattn_back)
    grad_tokens = (grad_middle + grad_norm_attn).reshape(seq_local, tok_seq, width)
    qkv_summed = (
        lax.psum_scatter(grad_qkv, ("batch", "seq"), scatter_dimension=0, tiled=True),
        lax.psum_scatter(grad_gain_attn, ("batch", "seq"), scatter_dimension=0, tiled=True),
    )
    return (
        mixed,
        grad_tokens,
        qkv_summed[0],
        block_summed[0],
        block_summed[1],
        block_summed[2],
        qkv_summed[1],
        block_summed[3],
        block_summed[4],
        block_summed[5],
        grad_scale,
    )


MESH = pl.DeviceIdType.MESH
F32 = jnp.float32
BF16 = jnp.bfloat16


def fits_fused(nb, ns, tokens, wqkv, wup):
    rows, width = wup.shape[0], wup.shape[1]
    return (
        ns == 4
        and nb % 2 == 0
        and tokens.shape == (1, 128, H * HD)
        and width == H * HD
        and 2 * rows == HD
        and nb * ns * rows == width
        and wqkv.shape == (rows, 3 * width)
    )


def nt(a, b):
    return lax.dot_general(a, b, (((1,), (1,)), ((), ())), preferred_element_type=F32)


def nn(a, b):
    return lax.dot_general(a, b, (((1,), (0,)), ((), ())), preferred_element_type=F32)


def tn(a, b):
    return lax.dot_general(a, b, (((0,), (0,)), ((), ())), preferred_element_type=F32)


def layer_kernel(nz, scratch_names, tok, cot, wqkv, wout, wup, wdown, ga, gf, bu, bd, scl, *refs):
    mixed_o, gtok_o, o1, o2, sg_o = refs[:5]
    r = types.SimpleNamespace(**dict(zip(scratch_names, refs[5:])))
    D = tok.shape[1]
    T = tok.shape[0]
    L = 4 * T
    HP = 2 * T
    NH = 4
    HW = NH * HD
    CB = HD
    RW = HD // 2
    LO = 256
    b = lax.axis_index("batch")
    s = lax.axis_index("seq")
    z, y = b // 2, b % 2
    x, c = s // 2, s % 2
    sib = (b, 2 * x + (1 - c))
    xp = (b, 2 * (1 - x) + c)
    yp = (2 * z + (1 - y), s)
    zup = (lax.rem(2 * (z + 1), 2 * nz) + y, s)
    zdn = (lax.rem(2 * (z + nz - 1), 2 * nz) + y, s)
    drains = []

    def when(cond, fn):
        if cond is None:
            fn()
        else:
            pl.when(cond)(fn)

    def both(p, q):
        if p is None:
            return q
        if q is None:
            return p
        return jnp.logical_and(p, q)

    def copy(src, dst, ssem, rsem, dev):
        return pltpu.make_async_remote_copy(
            src_ref=src, dst_ref=dst, send_sem=ssem, recv_sem=rsem, device_id=dev, device_id_type=MESH
        )

    def send(make, cond=None):
        when(cond, lambda: make().start())
        drains.append((make, cond))

    def arrive(make, cond=None):
        when(cond, lambda: make().wait_recv())

    bar = pltpu.get_barrier_semaphore()
    peers = [sib, xp, yp]
    for k in range(1, nz):
        peers.append((2 * lax.rem(z + k, nz) + y, s))
    for dev in peers:
        pl.semaphore_signal(bar, inc=1, device_id=dev, device_id_type=MESH)
    fetches = [
        pltpu.make_async_copy(src, dst, r.s_in.at[k])
        for k, (src, dst) in enumerate(
            (
                (wqkv, r.WQ),
                (wup, r.WU),
                (wout, r.WO),
                (wdown, r.WD),
                (tok, r.X.at[s]),
                (cot, r.DY.at[s]),
                (ga, r.V0),
                (gf, r.V1),
                (bu, r.V2),
                (bd, r.V3),
                (scl, r.V4),
            )
        )
    ]
    for f in fetches:
        f.start()
    r.SM[...] = jnp.zeros_like(r.SM)
    for k in range(6, 11):
        fetches[k].wait()
    small_rows = [v[...].astype(F32).reshape(1, RW) for v in (r.V0, r.V1, r.V2, r.V3)]
    for k, row in enumerate(small_rows):
        r.SM[k : k + 1, 0:RW] = row
    fetches[0].wait()
    fetches[1].wait()

    def pieces(cc):
        for xx in range(2):
            for t in range(4):
                for j in range(NH):
                    src = HD * (4 * j + 2 * cc + xx)
                    v = r.WU[:, src : src + HD] if t == 0 else r.WQ[:, D * (t - 1) + src : D * (t - 1) + src + HD]
                    r.W1P[cc, xx, 0:RW, HW * t + HD * j : HW * t + HD * (j + 1)] = v

    pieces(0)
    pieces(1)
    pl.semaphore_wait(bar, len(peers))

    m_sib1 = lambda: copy(r.W1P.at[1 - c], r.SIB1, r.s_one.at[0], r.r_one.at[0], sib)
    m_ssib = lambda: copy(r.SM, r.S.at[b, s], r.s_one.at[1], r.r_one.at[1], sib)
    m_sib2 = lambda: copy(r.W2P, r.SIB2, r.s_one.at[2], r.r_one.at[2], sib)
    send(m_ssib)
    send(m_sib1)
    fetches[2].wait()
    fetches[3].wait()
    r.W2P[0:RW, 0:D] = r.WO[...]
    r.W2P[0:RW, D : 2 * D] = r.WD[...]
    send(m_sib2)
    r.S[b, s] = r.SM[...]

    def chip_rows(own, other):
        own, other = own[:RW].astype(F32), other[:RW].astype(F32)
        lo = jnp.where(c == 0, own, other)
        hi = jnp.where(c == 0, other, own)
        return jnp.concatenate([lo, hi], axis=0).astype(BF16)

    m_ssib_r = lambda: copy(r.SM, r.S.at[b, 2 * x + (1 - c)], r.s_one.at[1], r.r_one.at[1], sib)
    arrive(m_ssib_r)
    m_xs = lambda: copy(
        r.S.at[b, pl.ds(2 * x, 2)], r.S.at[b, pl.ds(2 * x, 2)], r.s_one.at[4], r.r_one.at[4], xp
    )
    send(m_xs)
    arrive(m_sib1)
    r.CB1[...] = chip_rows(r.W1P[c, 1 - x], r.SIB1[1 - x])
    half = (D - LO) // 2
    cuts = (pl.ds(LO, half), pl.ds(LO + half, half), pl.ds(0, LO))

    def m_x1(k, xx):
        return copy(r.CB1.at[:, cuts[k]], r.W1.at[b, xx, :, cuts[k]], r.s_x1.at[k], r.r_x1.at[k], xp)

    for k in range(3):
        send(lambda k=k: m_x1(k, x))
    r.W1[b, x] = chip_rows(r.W1P[c, x], r.SIB1[x])

    def gather_item(idx, block, zcond, passes_y=True):
        up = lambda zz: copy(block(zz, y), block(zz, y), r.s_up.at[idx, zz], r.r_up.at[idx, zz], zup)
        dn = lambda zz: copy(block(zz, y), block(zz, y), r.s_dn.at[idx, zz], r.r_dn.at[idx, zz], zdn)
        yy = lambda zz: copy(block(zz, y), block(zz, y), r.s_y.at[idx, zz], r.r_y.at[idx, zz], yp)

        def start():
            send(lambda: up(z), both(zcond, z < nz - 1))
            send(lambda: dn(z), both(zcond, z > 0))
            if passes_y:
                send(lambda: yy(z), zcond)

        def step(d):
            lo, hi = z - d, z + d
            below, above = both(zcond, lo >= 0), both(zcond, hi < nz)
            arrive(lambda: up(lo), below)
            send(lambda: up(lo), both(below, z < nz - 1))
            arrive(lambda: dn(hi), above)
            send(lambda: dn(hi), both(above, z > 0))
            if passes_y:
                send(lambda: yy(lo), below)
                send(lambda: yy(hi), above)

        def finish():
            if passes_y:
                for k in range(nz):
                    when(
                        None if zcond is None else jnp.logical_not(zcond),
                        lambda k=k: copy(
                            block(k, 1 - y), block(k, 1 - y), r.s_y.at[idx, k], r.r_y.at[idx, k], yp
                        ).wait_recv(),
                    )

        return start, step, finish

    mine = c == y
    not_mine = c != y
    g_s = gather_item(0, lambda zz, q: r.S.at[2 * zz + q], None)
    g_own = [gather_item(1 + k, lambda zz, q, k=k: r.W1.at[2 * zz + q, x, :, cuts[k]], None) for k in range(2)]
    g_oth = [
        gather_item(3 + k, lambda zz, q, k=k: r.W1.at[2 * zz + q, 1 - x, :, cuts[k]], None) for k in range(2)
    ]
    g_out = gather_item(5, lambda zz, q: r.W2.at[zz, :, pl.ds(0, D)], None, False)
    g_up = gather_item(6, lambda zz, q: r.W1.at[2 * zz + q, :, :, pl.ds(0, LO)], None)
    g_dn = gather_item(7, lambda zz, q: r.W2.at[zz, :, pl.ds(D, D)], mine)

    g_own[0][0]()
    g_own[1][0]()
    m_xs_r = lambda: copy(
        r.S.at[b, pl.ds(2 - 2 * x, 2)],
        r.S.at[b, pl.ds(2 - 2 * x, 2)],
        r.s_one.at[4],
        r.r_one.at[4],
        xp,
    )
    arrive(m_xs_r)
    g_s[0]()
    fetches[4].wait()
    fetches[5].wait()
    own_tok, own_cot = r.X.at[s], r.DY.at[s]
    m_xt = lambda: copy(own_tok, own_tok, r.s_one.at[5], r.r_one.at[5], xp)
    m_st = lambda: copy(own_tok, own_tok, r.s_one.at[6], r.r_one.at[6], sib)
    m_xc = lambda: copy(own_cot, own_cot, r.s_one.at[7], r.r_one.at[7], xp)
    m_sc = lambda: copy(own_cot, own_cot, r.s_one.at[8], r.r_one.at[8], sib)
    send(m_xt)
    send(m_st)
    send(m_xc)
    send(m_sc)
    arrive(m_sib2)

    def fill_w2():
        r.W2[z] = chip_rows(r.W2P[...], r.SIB2[...])

    when(mine, fill_w2)
    m_y2 = lambda: copy(
        r.W2.at[z, :, pl.ds(0, D)], r.W2.at[z, :, pl.ds(0, D)], r.s_one.at[14], r.r_one.at[14], yp
    )
    sx = 2 * (1 - x) + c
    so = 2 * (1 - x) + (1 - c)
    ss = 2 * x + (1 - c)
    fwd = lambda name, k, src_i: copy(
        name.at[src_i], name.at[src_i], r.s_one.at[k], r.r_one.at[k], sib
    )
    arrive(lambda: m_x1(0, 1 - x))
    g_oth[0][0]()
    g_own[0][1](1)
    arrive(lambda: m_x1(1, 1 - x))
    g_oth[1][0]()
    send(m_y2, mine)
    g_own[1][1](1)
    g_s[1](1)
    arrive(lambda: m_x1(2, 1 - x))
    g_oth[0][1](1)
    g_oth[1][1](1)
    g_own[0][1](2)
    g_own[1][1](2)
    g_s[1](2)
    arrive(lambda: copy(own_tok, r.X.at[sx], r.s_one.at[5], r.r_one.at[5], xp))
    send(lambda: fwd(r.X, 9, sx))
    g_oth[0][1](2)
    arrive(m_y2, not_mine)
    g_out[0]()
    g_oth[1][1](2)
    for d in range(3, nz):
        g_own[0][1](d)
        g_own[1][1](d)
        g_s[1](d)
        g_oth[0][1](d)
        g_oth[1][1](d)
    arrive(lambda: copy(own_tok, r.X.at[ss], r.s_one.at[6], r.r_one.at[6], sib))
    arrive(lambda: fwd(r.X, 9, so))
    arrive(lambda: copy(own_cot, r.DY.at[sx], r.s_one.at[7], r.r_one.at[7], xp))
    send(lambda: fwd(r.DY, 10, sx))
    arrive(lambda: copy(own_cot, r.DY.at[ss], r.s_one.at[8], r.r_one.at[8], sib))
    g_out[1](1)
    g_s[2]()
    arrive(lambda: fwd(r.DY, 10, so))

    jf = lax.broadcasted_iota(jnp.int32, (1, D), 1).astype(F32)
    jk = jnp.floor((jf + 0.5) / RW)
    jl = jf - RW * jk
    pick = (lax.broadcasted_iota(jnp.int32, (128, D), 0).astype(F32) == jl).astype(BF16)
    sm_rows = 2 * nz * 4
    spread = nn(r.S[...].reshape(sm_rows * 8, 128).astype(BF16), pick)
    spread = spread.reshape(sm_rows, 8, D)
    owner = lax.broadcasted_iota(jnp.int32, (sm_rows, 8, D), 0).astype(F32)
    r.ROWS[...] = jnp.sum(jnp.where(owner == jk[None], spread, 0.0), axis=0)
    uf = jf[:, :HW]
    uj = jnp.floor((uf + 0.5) / HD)
    uh = jnp.floor((uf - HD * uj + 0.5) / RW)
    base = (2 * c + x).astype(F32)
    uk = 2.0 * (4.0 * uj + base) + uh
    r.BUP[...] = jnp.sum(
        jnp.where(owner[:, :, :HW] == uk[None], spread[:, :, :HW], 0.0), axis=0
    )
    gain_attn = r.ROWS[0:1]
    gain_ffn = r.ROWS[1:2]
    bias_down = r.ROWS[3:4]
    bias_up = r.BUP[2:3]
    scale = r.V4[...].astype(F32).reshape(1, HD)
    factor = soft_unit / math.sqrt(HD) * (
        jnp.maximum(scale, 0.0) + jnp.log(1.0 + jnp.exp(-jnp.abs(scale)))
    )

    for k in range(4):
        xv = r.X[k].astype(F32)
        inv = lax.rsqrt(jnp.mean(xv * xv, axis=1, keepdims=True) + epsilon)
        hn = xv * inv * gain_attn
        r.HN1[pl.ds(k * T, T)] = hn.astype(BF16)
        r.HN1T[:, :, pl.ds(k * T, T)] = hn.T.astype(BF16).reshape(2 * nz, 2 * CB, T)
    g_out[1](2)
    g_up[0]()
    g_dn[0]()
    for g in (*g_own, *g_oth):
        g[2]()

    W1 = r.W1
    W2 = r.W2
    for h in range(2):
        wq = W1[:, :, :, pl.ds(LO + 512 * h, 512)].reshape(D, 512)
        r.QKV[:, pl.ds(512 * h, 512)] = nn(r.HN1[...], wq)
    off = HW - LO
    for j in range(NH):
        q = r.QKV[:, off + HD * j : off + HD * (j + 1)]
        k = r.QKV[:, off + HW + HD * j : off + HW + HD * (j + 1)]
        v = r.QKV[:, off + 2 * HW + HD * j : off + 2 * HW + HD * (j + 1)]
        r.QRAW[j] = q
        r.QH[j] = (q * factor).astype(BF16)
        r.KH[j] = k.astype(BF16)
        r.VH[j] = v.astype(BF16)
        r.KT[j] = k.T.astype(BF16)
        r.VT[j] = v.T.astype(BF16)
    tri_k = lax.broadcasted_iota(jnp.int32, (HP, HP), 0)
    tri_q = lax.broadcasted_iota(jnp.int32, (HP, HP), 1)
    seen = tri_k <= tri_q

    def rows_of(p):
        return pl.ds(p * HP, HP)

    def attend(p, j):
        q = r.QH[j, rows_of(p)]
        diag = jnp.where(seen, nt(r.KH[j, rows_of(p)], q), neg_large)
        top = jnp.max(diag, axis=0, keepdims=True)
        if p:
            full = nt(r.KH[j, pl.ds(0, HP)], q)
            top = jnp.maximum(top, jnp.max(full, axis=0, keepdims=True))
            full = jnp.exp(full - top)
        diag = jnp.exp(diag - top)
        total = jnp.sum(diag, axis=0, keepdims=True)
        if p:
            total = total + jnp.sum(full, axis=0, keepdims=True)
        inv = 1.0 / total
        diag = (diag * inv).astype(BF16)
        if p:
            r.PT1[j, pl.ds(0, HP)] = (full * inv).astype(BF16)
            r.PT1[j, pl.ds(HP, HP)] = diag
            ot = nn(r.VT[j], r.PT1[j])
        else:
            r.PT0[j] = diag
            ot = nn(r.VT[j, :, pl.ds(0, HP)], diag)
        r.OT[j, :, rows_of(p)] = ot
        r.OB[rows_of(p), HD * j : HD * (j + 1)] = ot.T.astype(BF16)

    def to_sibling(st, p, value):
        r.PF[p] = value.reshape(2, T, D)
        r.ES[st, p] = r.PF[p, 1 - c].astype(BF16)
        send(lambda: copy(r.ES.at[st, p], r.ER.at[st, p], r.s_e.at[st, p], r.r_e.at[st, p], sib))

    def chip_sum(st, p):
        arrive(lambda: copy(r.ES.at[st, p], r.ER.at[st, p], r.s_e.at[st, p], r.r_e.at[st, p], sib))
        return r.PF[p, c] + r.ER[st, p].astype(F32)

    def xslot(st, p):
        return 2 * st + p if st < 2 else st + 2

    def xcopy(st, p):
        i = xslot(st, p)
        return copy(r.XS.at[i], r.XR.at[i], r.s_x.at[i], r.r_x.at[i], xp)

    def to_x(st, p):
        r.XS[xslot(st, p)] = chip_sum(st, p).astype(BF16)
        send(lambda: xcopy(st, p))

    def pair_sum(st, p):
        arrive(lambda: xcopy(st, p))
        return r.XS[xslot(st, p)].astype(F32) + r.XR[xslot(st, p)].astype(F32)

    def share(name, st, p):
        mk = lambda i: copy(name.at[i], name.at[i], r.s_h.at[st, p], r.r_h.at[st, p], sib)
        send(lambda: mk(2 * p + c))
        return lambda: arrive(lambda: mk(2 * p + (1 - c)))

    def out_proj(p):
        to_sibling(0, p, nn(r.OB[rows_of(p)], W2[:, :, pl.ds(0, D)].reshape(HW, D)))

    for j in range(NH):
        attend(0, j)
    for d in range(3, nz):
        g_out[1](d)
    out_proj(0)
    attend(1, 0)
    attend(1, 1)
    to_x(0, 0)
    g_up[1](1)
    g_dn[1](1)
    attend(1, 2)
    attend(1, 3)
    out_proj(1)
    to_x(0, 1)
    for d in range(2, nz):
        g_up[1](d)
        g_dn[1](d)

    r.SGA[...] = jnp.zeros_like(r.SGA)

    def middle(p):
        mid = r.X[2 * p + c].astype(F32) + pair_sum(0, p)
        r.MID[p] = mid
        inv = lax.rsqrt(jnp.mean(mid * mid, axis=1, keepdims=True) + epsilon)
        r.HN2[2 * p + c] = (mid * inv * gain_ffn).astype(BF16)
        return share(r.HN2, 0, p)

    def w_up():
        return W1[:, :, :, pl.ds(0, HW)].reshape(D, HW)

    def feed(p):
        hn = r.HN2[pl.ds(2 * p, 2)].reshape(HP, D)
        u = nn(hn, w_up()) + bias_up
        sig = 1.0 / (1.0 + jnp.exp(-u))
        r.ACT[rows_of(p)] = (u * sig).astype(BF16)
        dy = r.DY[pl.ds(2 * p, 2)].reshape(HP, D)
        dact = nt(dy, W2[:, :, pl.ds(D, D)].reshape(HW, D))
        dup = (dact * sig * (1.0 + u * (1.0 - sig))).astype(BF16)
        r.DUP[rows_of(p), 0:HW] = dup
        to_sibling(1, p, nt(dup, w_up()))
        row = pl.ds(4 + s, 1)
        r.SGA[row, 0:HW] = r.SGA[row, 0:HW] + jnp.sum(dup.astype(F32), axis=0, keepdims=True)

    def transpose_hn2(p):
        for k in range(2):
            t = r.HN2[2 * p + k].astype(F32).T.astype(BF16)
            r.HN2T[:, :, pl.ds((2 * p + k) * T, T)] = t.reshape(2 * nz, 2 * CB, T)

    r.DUP[:, 256:384] = jnp.zeros((L, 128), BF16)
    r.DQ[:, 0:128] = jnp.zeros((L, 128), BF16)
    wait_hn = middle(0)
    g_up[2]()
    g_dn[2]()
    wait_hn()
    feed(0)
    transpose_hn2(0)
    wait_hn = middle(1)
    to_x(1, 0)
    wait_hn()
    feed(1)
    transpose_hn2(1)

    def scatter_item(idx, part, yr, zu, zd, zcond, y_first=True):
        yc = lambda zz: copy(part(zz, 1 - y), yr(zz), r.s_ry.at[idx, zz], r.r_ry.at[idx, zz], yp)
        up = lambda zz: copy(part(zz, y), zu(zz), r.s_ru.at[idx, zz], r.r_ru.at[idx, zz], zup)
        dn = lambda zz: copy(part(zz, y), zd(zz), r.s_rd.at[idx, zz], r.r_rd.at[idx, zz], zdn)

        def add(zz, other):
            part(zz, y)[...] = (part(zz, y)[...].astype(F32) + other(zz)[...].astype(F32)).astype(BF16)

        ycond = None if zcond is None else jnp.logical_not(zcond)

        def start(d):
            if d:
                send(lambda: yc(z + d), both(z + d < nz, ycond))
                send(lambda: yc(z - d), both(z - d >= 0, ycond))
            else:
                send(lambda: yc(z), ycond)

        def step(d):
            if d:
                ok = both(zcond, z + d < nz)
                from_below = both(ok, z > 0)
                if y_first:
                    arrive(lambda: yc(z + d), ok)
                    when(ok, lambda: add(z + d, yr))
                arrive(lambda: up(z + d), from_below)
                when(from_below, lambda: add(z + d, zu))
                send(lambda: up(z + d), ok)
                ok2 = both(zcond, z - d >= 0)
                from_above = both(ok2, z < nz - 1)
                if y_first:
                    arrive(lambda: yc(z - d), ok2)
                    when(ok2, lambda: add(z - d, yr))
                arrive(lambda: dn(z - d), from_above)
                when(from_above, lambda: add(z - d, zd))
                send(lambda: dn(z - d), ok2)
            else:
                below, above = both(zcond, z > 0), both(zcond, z < nz - 1)
                arrive(lambda: up(z), below)
                when(below, lambda: add(z, zu))
                arrive(lambda: dn(z), above)
                when(above, lambda: add(z, zd))
                if y_first:
                    arrive(lambda: yc(z), zcond)
                    when(zcond, lambda: add(z, yr))

        return start, step

    far = range(nz - 1, 0, -1)
    cut_up = pl.ds(0, LO)
    s_up = scatter_item(
        0,
        lambda zz, q: r.G1.at[2 * zz + q, :, :, cut_up],
        lambda zz: r.YR1.at[zz, :, :, cut_up],
        lambda zz: r.ZU1.at[zz - 1, :, :, cut_up],
        lambda zz: r.ZD1.at[zz, :, :, cut_up],
        None,
    )

    def qkv_item(idx, xx, cut):
        return scatter_item(
            idx,
            lambda zz, q: r.G1.at[2 * zz + q, xx, :, cut],
            lambda zz: r.YR1.at[zz, xx, :, cut],
            lambda zz: r.ZU1.at[zz - 1, xx, :, cut],
            lambda zz: r.ZD1.at[zz, xx, :, cut],
            None,
        )

    def together(items):
        def start(d):
            for it in items:
                it[0](d)

        def step(d):
            for it in items:
                it[1](d)

        return start, step

    def w2_item(idx, lo, width, zcond, y_first):
        cut = pl.ds(lo, width)
        return scatter_item(
            idx,
            lambda zz, q: r.G2.at[zz, :, cut],
            lambda zz: r.YR2.at[zz, :, cut],
            lambda zz: r.ZU2.at[zz - 1, :, cut],
            lambda zz: r.ZD2.at[zz, :, cut],
            zcond,
            y_first,
        )

    s_dn = w2_item(1, D, D, None, False)
    WZ = D // 2
    s_out = w2_item(2, 0, WZ, None, False)
    s_out2 = w2_item(5, WZ, D - WZ, mine, True) if WZ < D else ((lambda d: None), (lambda d: None))
    fars = [qkv_item(3, 1 - x, cuts[0]), qkv_item(6, 1 - x, cuts[1])]
    owns = [qkv_item(4, x, cuts[0]), qkv_item(7, x, cuts[1])]
    s_far, s_own = together(fars), together(owns)

    gu = nn(r.HN2T[...].reshape(D, L), r.DUP[...])
    r.G1[:, :, :, 0:384] = gu.astype(BF16).reshape(2 * nz, 2, CB, 384)
    for d in (*far, 0):
        s_up[0](d)
    to_x(1, 1)
    dy_all = r.DY[...].reshape(L, D)
    r.G2[:, :, pl.ds(D, D)] = tn(r.ACT[...], dy_all).astype(BF16).reshape(nz, CB, D)
    if nz > 3:
        s_dn[1](3)

    def back_middle(p):
        dh = pair_sum(1, p)
        mid = r.MID[p]
        inv = lax.rsqrt(jnp.mean(mid * mid, axis=1, keepdims=True) + epsilon)
        n = mid * inv
        dn = dh * gain_ffn
        dmid = r.DY[2 * p + c].astype(F32) + inv * (
            dn - n * jnp.mean(dn * n, axis=1, keepdims=True)
        )
        r.DMID[p] = dmid
        r.DA[2 * p + c] = dmid.astype(BF16)
        own = jnp.where(x == p, jnp.sum(dh * n, axis=0, keepdims=True), 0.0)
        r.SGA[1:2] = r.SGA[1:2] + own
        return share(r.DA, 1, p)

    def back_out(p):
        da = r.DA[pl.ds(2 * p, 2)].reshape(HP, D)
        r.QKV[0:HP, 0:HW] = nt(da, W2[:, :, pl.ds(0, D)].reshape(HW, D))

    def back_attend(p, j):
        do = r.QKV[0:HP, HD * j : HD * (j + 1)].astype(BF16)
        dof = do.astype(F32)
        delta = jnp.sum(dof.T * r.OT[j, :, rows_of(p)], axis=0, keepdims=True)
        span = HP * (p + 1)
        pt = r.PT1[j] if p else r.PT0[j]
        dpt = nt(r.VH[j, pl.ds(0, span)], do)
        dst = (pt.astype(F32) * (dpt - delta)).astype(BF16)
        dv = nn(pt, do)
        dk = nn(dst, r.QH[j, rows_of(p)])
        dq = nn(r.KT[j, :, pl.ds(0, span)], dst).T
        raw = r.QRAW[j, rows_of(p)]
        r.SGA[3:4, 0:HD] = r.SGA[3:4, 0:HD] + jnp.sum(dq * raw, axis=0, keepdims=True)
        r.DQ[rows_of(p), off + HD * j : off + HD * (j + 1)] = (dq * factor).astype(BF16)
        ko, vo = off + HW + HD * j, off + 2 * HW + HD * j
        if p == 0:
            r.DKA[j] = dk
            r.DVA[j] = dv
        else:
            r.DQ[0:HP, ko : ko + HD] = (dk[:HP] + r.DKA[j]).astype(BF16)
            r.DQ[HP:L, ko : ko + HD] = dk[HP:].astype(BF16)
            r.DQ[0:HP, vo : vo + HD] = (dv[:HP] + r.DVA[j]).astype(BF16)
            r.DQ[HP:L, vo : vo + HD] = dv[HP:].astype(BF16)

    def down_proj(p):
        to_sibling(2, p, nn(r.ACT[rows_of(p)], W2[:, :, pl.ds(D, D)].reshape(HW, D)))

    wait_da = back_middle(0)
    down_proj(0)
    down_proj(1)
    if nz > 3:
        s_up[1](3)
    wait_da()
    back_out(0)
    for j in range(NH):
        back_attend(0, j)
    if nz > 2:
        s_up[1](2)
        s_dn[1](2)
    wait_da = back_middle(1)
    r.XS[4] = chip_sum(2, 1 - x).astype(BF16)
    send(lambda: xcopy(2, 0))
    r.PF2[...] = chip_sum(2, x)
    s_up[1](1)
    wait_da()
    back_out(1)
    da_all = r.DA[...].reshape(L, D)
    r.G2[:, :, pl.ds(0, D)] = tn(r.OB[...], da_all).astype(BF16).reshape(nz, CB, D)
    if nz > 3:
        s_out[1](3)
    for d in (*far, 0):
        s_out2[0](d)
    for j in range(NH):
        back_attend(1, j)
    s_dn[1](1)

    def qkv_block(bb):
        t = nn(r.HN1T[bb], r.DQ[...]).reshape(2, CB, D - LO)
        head = t[:, :, 0:128] + r.G1[bb, :, :, pl.ds(LO, 128)].astype(F32)
        r.G1[bb, :, :, pl.ds(LO, 128)] = head.astype(BF16)
        r.G1[bb, :, :, pl.ds(384, D - 384)] = t[:, :, 128:].astype(BF16)

    for d in far:
        pl.when(z + d < nz)(lambda: qkv_block(2 * (z + d) + (1 - y)))
        pl.when(z - d >= 0)(lambda: qkv_block(2 * (z - d) + (1 - y)))
        s_far[0](d)
        s_own[0](d)
    qkv_block(2 * z + (1 - y))
    s_far[0](0)
    for k in range(nz):
        qkv_block(2 * k + y)

    for p in range(2):
        w = W1[:, :, :, pl.ds(LO, D - LO)].reshape(D, D - LO)
        to_sibling(3, p, nt(r.DQ[rows_of(p)], w))
    s_up[1](0)
    arrive(lambda: xcopy(2, 0))
    own_out = r.PF2[...] + r.XR[4].astype(F32)
    mixed_o[...] = (r.MID[x] + own_out + bias_down).astype(BF16)
    r.XS[5] = chip_sum(3, 1 - x).astype(BF16)
    send(lambda: xcopy(3, 0))
    r.PF2[...] = chip_sum(3, x)
    s_dn[1](0)
    cut_d = pl.ds(D, D)
    m_gyd = lambda: copy(
        r.G2.at[z, :, cut_d], r.YR2.at[z, :, cut_d], r.s_one.at[16], r.r_one.at[16], yp
    )
    send(m_gyd, not_mine)
    s_own[0](0)
    if nz > 2:
        s_out[1](2)
    if nz > 3:
        s_out2[1](3)
        s_far[1](3)
        s_own[1](3)
    if nz > 2:
        s_far[1](2)
    s_out[1](1)
    if nz > 2:
        s_out2[1](2)
        s_own[1](2)

    arrive(lambda: xcopy(3, 0))
    dh = r.PF2[...] + r.XR[5].astype(F32)
    xv = r.X[s].astype(F32)
    inv = lax.rsqrt(jnp.mean(xv * xv, axis=1, keepdims=True) + epsilon)
    n = xv * inv
    dn = dh * gain_attn
    gtok_o[...] = r.DMID[x] + inv * (dn - n * jnp.mean(dn * n, axis=1, keepdims=True))
    r.SGA[0:1] = jnp.sum(dh * n, axis=0, keepdims=True)
    r.SGA[2:3] = jnp.sum(r.DY[s].astype(F32), axis=0, keepdims=True)

    def small_copy(k, slot, dev):
        return lambda: copy(
            r.SGA if k == 0 else r.SGS.at[k - 1], r.SGR.at[slot], r.s_sg.at[slot], r.r_sg.at[slot], dev
        )

    total = r.SGA[...]
    for k, dev in enumerate((sib, xp, yp)):
        mk = small_copy(k, k, dev)
        send(mk)
        if k == 2:
            s_far[1](1)
            s_own[1](1)
            cut_o = pl.ds(0, WZ)
            s_out[1](0)
            m_gy = lambda: copy(
                r.G2.at[z, :, cut_o], r.YR2.at[z, :, cut_o], r.s_one.at[15], r.r_one.at[15], yp
            )
            send(m_gy, not_mine)
            ends = (pl.ds(0, LO + half), pl.ds(LO + half, half))

            def m_fx(k):
                return copy(
                    r.G1.at[b, 1 - x, :, ends[k]], r.FX.at[:, ends[k]], r.s_fx.at[k], r.r_fx.at[k], xp
                )

            for h in range(2):
                fars[h][1](0)
                send(lambda h=h: m_fx(h))
            s_out2[1](1)
        arrive(mk)
        total = total + r.SGR[k]
        r.SGS[k] = total
    mks = []
    for k in range(1, nz):
        mk = small_copy(3, 2 + k, (2 * lax.rem(z + k, nz) + y, s))
        send(mk)
        mks.append(mk)
    s_out2[1](0)

    def hand_over(k, h, xx, block):
        cut = ends[h]
        done = block.astype(F32)
        r.GF[0, xx, :, cut] = done[:RW]
        r.GF[1, xx, :, cut] = done[RW:]
        mk = lambda: copy(
            r.GF.at[1 - c, xx, :, cut], r.GRV.at[xx, :, cut], r.s_gf.at[k, h], r.r_gf.at[k, h], sib
        )
        send(mk)
        o1[xx, c, :, cut] = r.GF[c, xx, :, cut]

        def take():
            arrive(mk)
            o1[xx, 1 - c, :, cut] = r.GRV[xx, :, cut]

        return take

    takes = []
    for h in range(2):
        arrive(lambda h=h: m_fx(h))
        takes.append(hand_over(0, h, 1 - x, r.FX[:, ends[h]]))
    for h in range(2):
        owns[h][1](0)
        takes.append(hand_over(1, h, x, r.G1[b, x, :, ends[h]]))
    arrive(m_gy, mine)
    arrive(m_gyd, mine)

    def out_from_y():
        for cut in (cut_o, cut_d):
            r.G2[z, :, cut] = (r.G2[z, :, cut].astype(F32) + r.YR2[z, :, cut].astype(F32)).astype(BF16)

    when(mine, out_from_y)
    done2 = r.G2[z].astype(F32)
    r.GF2[0] = done2[:RW]
    r.GF2[1] = done2[RW:]
    m_g2 = lambda: copy(r.GF2.at[1 - c], r.GR2, r.s_one.at[12], r.r_one.at[12], sib)
    send(m_g2, mine)
    for take in takes:
        take()
    for k, mk in enumerate(mks):
        arrive(mk)
        total = total + r.SGR[3 + k]
    sg_o[...] = total
    arrive(m_g2, not_mine)

    def out2_own():
        o2[...] = r.GF2[c]

    def out2_sib():
        o2[...] = r.GR2[...]

    when(mine, out2_own)
    when(not_mine, out2_sib)

    for make, cond in drains:
        when(cond, lambda make=make: make().wait_send())


def fused_layer(nb, ns, tokens, wqkv, wout, wup, wdown, gattn, gffn, bup, bdown, scale_param, cot):
    nz = nb // 2
    rows, D = wout.shape
    T = tokens.shape[1]
    L = ns * T
    V = pltpu.VMEM
    scratch = dict(
        WQ=V((rows, 3 * D), BF16),
        WU=V((rows, D), BF16),
        WO=V((rows, D), BF16),
        WD=V((rows, D), BF16),
        SM=V((8, 128), F32),
        V0=V((rows,), BF16),
        V1=V((rows,), BF16),
        V2=V((rows,), BF16),
        V3=V((rows,), BF16),
        V4=V((HD,), BF16),
        W1P=V((2, 2, 48, D), BF16),
        W2P=V((48, 2 * D), BF16),
        SIB1=V((2, 48, D), BF16),
        SIB2=V((48, 2 * D), BF16),
        CB1=V((HD, D), BF16),
        W1=V((nb, 2, HD, D), BF16),
        W2=V((nz, HD, 2 * D), BF16),
        S=V((nb, 4, 8, 128), F32),
        X=V((4, T, D), BF16),
        DY=V((4, T, D), BF16),
        ROWS=V((8, D), F32),
        BUP=V((8, 4 * HD), F32),
        HN1=V((L, D), BF16),
        HN1T=V((nb, 2 * HD, L), BF16),
        HN2T=V((nb, 2 * HD, L), BF16),
        QKV=V((L, D - 256), F32),
        QRAW=V((4, L, HD), F32),
        QH=V((4, L, HD), BF16),
        KH=V((4, L, HD), BF16),
        VH=V((4, L, HD), BF16),
        KT=V((4, HD, L), BF16),
        VT=V((4, HD, L), BF16),
        PT0=V((4, L // 2, L // 2), BF16),
        PT1=V((4, L, L // 2), BF16),
        OT=V((4, HD, L), F32),
        OB=V((L, 4 * HD), BF16),
        PF=V((2, 2, T, D), F32),
        PF2=V((T, D), F32),
        ES=V((4, 2, T, D), BF16),
        ER=V((4, 2, T, D), BF16),
        XS=V((6, T, D), BF16),
        XR=V((6, T, D), BF16),
        MID=V((2, T, D), F32),
        HN2=V((4, T, D), BF16),
        ACT=V((L, 4 * HD), BF16),
        DUP=V((L, 384), BF16),
        DA=V((4, T, D), BF16),
        DMID=V((2, T, D), F32),
        DQ=V((L, D - 256), BF16),
        DKA=V((4, L // 2, HD), F32),
        DVA=V((4, L // 2, HD), F32),
        G1=V((nb, 2, HD, D), BF16),
        G2=V((nz, HD, 2 * D), BF16),
        YR1=V((nz, 2, HD, D), BF16),
        ZU1=V((nz - 1, 2, HD, D), BF16),
        ZD1=V((nz - 1, 2, HD, D), BF16),
        YR2=V((nz, HD, 2 * D), BF16),
        ZU2=V((nz - 1, HD, 2 * D), BF16),
        ZD2=V((nz - 1, HD, 2 * D), BF16),
        FX=V((HD, D), BF16),
        GF=V((2, 2, rows, D), F32),
        GRV=V((2, rows, D), F32),
        GF2=V((2, rows, 2 * D), F32),
        GR2=V((rows, 2 * D), F32),
        SGA=V((8, D), F32),
        SGS=V((3, 8, D), F32),
        SGR=V((2 + nz, 8, D), F32),
    )
    dma = pltpu.SemaphoreType.DMA
    scratch.update(
        s_in=dma((11,)),
        s_x1=dma((3,)), r_x1=dma((3,)),
        s_gf=dma((2, 2)), r_gf=dma((2, 2)),
        s_fx=dma((2,)), r_fx=dma((2,)),
        s_one=dma((17,)), r_one=dma((17,)),
        s_up=dma((9, nz)), r_up=dma((9, nz)),
        s_dn=dma((9, nz)), r_dn=dma((9, nz)),
        s_y=dma((9, nz)), r_y=dma((9, nz)),
        s_e=dma((4, 2)), r_e=dma((4, 2)),
        s_x=dma((6,)), r_x=dma((6,)),
        s_h=dma((2, 2)), r_h=dma((2, 2)),
        s_ry=dma((8, nz)), r_ry=dma((8, nz)),
        s_ru=dma((8, nz)), r_ru=dma((8, nz)),
        s_rd=dma((8, nz)), r_rd=dma((8, nz)),
        s_sg=dma((2 + nz,)), r_sg=dma((2 + nz,)),
    )
    vmem = pl.BlockSpec(memory_space=pltpu.VMEM)
    hbm = pl.BlockSpec(memory_space=pl.ANY)
    mixed, gtok, o1, o2, sg = pl.pallas_call(
        functools.partial(layer_kernel, nz, tuple(scratch)),
        out_shape=(
            jax.ShapeDtypeStruct((T, D), BF16),
            jax.ShapeDtypeStruct((T, D), F32),
            jax.ShapeDtypeStruct((2, 2, rows, D), F32),
            jax.ShapeDtypeStruct((rows, 2 * D), F32),
            jax.ShapeDtypeStruct((8, D), F32),
        ),
        in_specs=[hbm] * 11,
        out_specs=(vmem,) * 5,
        scratch_shapes=list(scratch.values()),
        compiler_params=pltpu.CompilerParams(
            collective_id=0, has_side_effects=True, vmem_limit_bytes=63 << 20
        ),
        name="decoder_layer",
    )(tokens[0], cot[0], wqkv, wout, wup, wdown, gattn, gffn, bup, bdown, scale_param)
    mixed, gtok, gqkv, gout, gup, gdown, g_attn, g_ffn, g_bup, g_bdown, gscale = pl.pallas_call(
        functools.partial(outputs_kernel, ns),
        out_shape=(
            jax.ShapeDtypeStruct((T, D), BF16),
            jax.ShapeDtypeStruct((T, D), F32),
            jax.ShapeDtypeStruct((rows, 3 * D), F32),
            jax.ShapeDtypeStruct((rows, D), F32),
            jax.ShapeDtypeStruct((rows, D), F32),
            jax.ShapeDtypeStruct((rows, D), F32),
            jax.ShapeDtypeStruct((rows,), F32),
            jax.ShapeDtypeStruct((rows,), F32),
            jax.ShapeDtypeStruct((rows,), F32),
            jax.ShapeDtypeStruct((rows,), F32),
            jax.ShapeDtypeStruct((HD,), F32),
        ),
        in_specs=[vmem] * 6,
        out_specs=(vmem,) * 11,
        compiler_params=pltpu.CompilerParams(vmem_limit_bytes=63 << 20),
        name="place_outputs",
    )(mixed, gtok, o1, o2, sg, scale_param)
    return mixed[None], gtok[None], gqkv, gout, gup, gdown, g_attn, g_ffn, g_bup, g_bdown, gscale


def outputs_kernel(ns, mixed, gtok, o1, o2, sg, scl, mixed_o, gtok_o, gqkv, gout, gup, gdown, *small):
    rows, D = gup.shape
    HW = 4 * HD
    mixed_o[...] = mixed[...]
    gtok_o[...] = gtok[...]
    gout[...] = o2[:, 0:D]
    gdown[...] = o2[:, D : 2 * D]
    for xx in range(2):
        for cc in range(2):
            for t in range(4):
                for j in range(4):
                    v = o1[xx, cc, :, HW * t + HD * j : HW * t + HD * (j + 1)]
                    at = HD * (4 * j + 2 * cc + xx)
                    if t == 0:
                        gup[:, at : at + HD] = v
                    else:
                        gqkv[:, D * (t - 1) + at : D * (t - 1) + at + HD] = v
    first = (lax.axis_index("batch") * ns + lax.axis_index("seq")) * rows
    parts = []
    for h in range(H):
        j, cc, xx = h // 4, (h // 2) % 2, h % 2
        row = 4 + 2 * xx + cc
        parts.append(sg[row : row + 1, HD * j : HD * (j + 1)])
    bias_up = jnp.concatenate(parts, axis=1)
    shift = lax.rem(D - first, D)
    for ref, v in zip(small, (sg[0:1], sg[1:2], bias_up, sg[2:3])):
        v = jnp.broadcast_to(v, (8, D))
        ref[...] = pltpu.roll(v, shift, 1)[0, 0:rows]
    scale = scl[...].astype(F32).reshape(1, HD)
    small[4][...] = (sg[3:4, 0:HD] * (soft_unit / math.sqrt(HD)) / (1.0 + jnp.exp(-scale)))[0]


def layer_step(nb, ns, *args):
    if fits_fused(nb, ns, args[0], args[1], args[3]):
        return fused_layer(nb, ns, *args)
    return generic_layer(*args)


def solution(mesh):
    return jax.shard_map(
        functools.partial(layer_step, mesh.shape["batch"], mesh.shape["seq"]),
        mesh=mesh,
        in_specs=(
            P("batch", "seq", None),
            P(("batch", "seq"), None),
            P(("batch", "seq"), None),
            P(("batch", "seq"), None),
            P(("batch", "seq"), None),
            P(("batch", "seq")),
            P(("batch", "seq")),
            P(("batch", "seq")),
            P(("batch", "seq")),
            P(),
            P("batch", "seq", None),
        ),
        out_specs=(
            P("batch", "seq", None),
            P("batch", "seq", None),
            P(("batch", "seq"), None),
            P(("batch", "seq"), None),
            P(("batch", "seq"), None),
            P(("batch", "seq"), None),
            P(("batch", "seq")),
            P(("batch", "seq")),
            P(("batch", "seq")),
            P(("batch", "seq")),
            P(),
        ),
        check_vma=False,
    )
```

```python
import functools
import math
import types

import jax
import jax.numpy as jnp
from jax import lax
from jax.experimental import pallas as pl
from jax.experimental.pallas import tpu as pltpu
from jax.sharding import PartitionSpec as P

H = 16
HD = 80


epsilon = 1e-06
soft_unit = 1.442695041
neg_large = -1e30


def norm_forward(values, gain):
    inverse = lax.rsqrt(jnp.mean(values * values, axis=1, keepdims=True) + epsilon)
    return (inverse, (values * inverse * gain.astype(jnp.float32)).astype(jnp.bfloat16))


def norm_back(grad_out, values, inverse, gain):
    normed = values * inverse
    scaled = grad_out * gain.astype(jnp.float32)
    grad_gain = jnp.sum(grad_out * normed, axis=0)
    grad_in = inverse * (scaled - normed * jnp.mean(scaled * normed, axis=1, keepdims=True))
    return (grad_in, grad_gain)


def generic_layer(
    tokens,
    query_key_value_weight,
    attention_output_weight,
    up_projection_weight,
    down_projection_weight,
    gain_attn,
    gain_ffn,
    up_projection_bias,
    down_projection_bias,
    scale_param,
    cotangent,
):
    seq_local, tok_seq, width = tokens.shape
    row_count = seq_local * tok_seq
    shards = (
        query_key_value_weight,
        attention_output_weight,
        up_projection_weight,
        down_projection_weight,
        gain_attn,
        gain_ffn,
        up_projection_bias,
        down_projection_bias,
    )
    fwd_weights = (
        lax.all_gather(shards[0], ("batch", "seq"), axis=0, tiled=True),
        lax.all_gather(shards[1], ("batch", "seq"), axis=0, tiled=True),
        lax.all_gather(shards[2], ("batch", "seq"), axis=0, tiled=True),
        lax.all_gather(shards[3], ("batch", "seq"), axis=0, tiled=True),
        lax.all_gather(shards[4], ("batch", "seq"), axis=0, tiled=True),
        lax.all_gather(shards[5], ("batch", "seq"), axis=0, tiled=True),
        lax.all_gather(shards[6], ("batch", "seq"), axis=0, tiled=True),
        lax.all_gather(shards[7], ("batch", "seq"), axis=0, tiled=True),
    )
    wqkv_full, wout_full, wup_full, wdown_full, gattn_full, gffn_full, bup_full, bdown_full = (
        fwd_weights
    )
    inputs = tokens.astype(jnp.float32).reshape(row_count, width)
    inv_attn, attention_normed_input = norm_forward(inputs, gattn_full)
    query_key_value = jnp.dot(attention_normed_input, wqkv_full, preferred_element_type=jnp.float32)
    q_raw = query_key_value[:, :width]
    scale_float = scale_param.astype(jnp.float32)
    factor = soft_unit / math.sqrt(HD) * jax.nn.softplus(scale_float)
    factor_row = jnp.tile(factor, H)
    queries = (q_raw * factor_row).astype(jnp.bfloat16)
    keys_own = (
        query_key_value[:, width : 2 * width]
        .astype(jnp.bfloat16)
        .reshape(seq_local, tok_seq, width)
    )
    values_own = (
        query_key_value[:, 2 * width :].astype(jnp.bfloat16).reshape(seq_local, tok_seq, width)
    )
    keys_all, values_all = (
        lax.all_gather(keys_own, "seq", axis=1, tiled=True),
        lax.all_gather(values_own, "seq", axis=1, tiled=True),
    )
    position = lax.axis_index("seq")
    block_total = lax.axis_size("seq")
    query_pos = position * tok_seq + jnp.arange(tok_seq, dtype=jnp.int32)
    key_offsets = jnp.arange(tok_seq, dtype=jnp.int32)
    queries_h = queries.reshape(seq_local, tok_seq, H, HD)

    def key_block(source, block):
        piece = lax.dynamic_slice_in_dim(source, block * tok_seq, tok_seq, 1)
        return piece.reshape(seq_local, tok_seq, H, HD)

    def block_scores(block):
        scores = jnp.einsum(
            "sqhd,skhd->shqk",
            queries_h,
            key_block(keys_all, block),
            preferred_element_type=jnp.float32,
        )
        allowed = (block * tok_seq + key_offsets)[None, :] <= query_pos[:, None]
        return jnp.where(allowed, scores, neg_large)

    def max_step(block, carry):
        top, total = carry
        scores = block_scores(block)
        new_top = jnp.maximum(top, jnp.max(scores, axis=3, keepdims=True))
        total = total * jnp.exp(top - new_top) + jnp.sum(
            jnp.exp(scores - new_top), axis=3, keepdims=True
        )
        return (new_top, total)

    start_top = jnp.full((seq_local, H, tok_seq, 1), neg_large, jnp.float32)
    top, total = lax.fori_loop(0, block_total, max_step, (start_top, jnp.zeros_like(start_top)))
    log_sum = top + jnp.log(total)

    def value_step(block, accum):
        probs = jnp.exp(block_scores(block) - log_sum).astype(jnp.bfloat16)
        return accum + jnp.einsum(
            "shqk,skhd->sqhd",
            probs,
            key_block(values_all, block),
            preferred_element_type=jnp.float32,
        )

    attention_output = lax.fori_loop(
        0, block_total, value_step, jnp.zeros((seq_local, tok_seq, H, HD), jnp.float32)
    )
    attention_output = attention_output.reshape(row_count, width)
    att_low = attention_output.astype(jnp.bfloat16)
    middle = inputs + jnp.dot(att_low, wout_full, preferred_element_type=jnp.float32)
    inv_ffn, feedforward_normed_input = norm_forward(middle, gffn_full)
    up_projected_value = jnp.dot(
        feedforward_normed_input, wup_full, preferred_element_type=jnp.float32
    ) + bup_full.astype(jnp.float32)
    act_low = jax.nn.silu(up_projected_value).astype(jnp.bfloat16)
    result = (
        middle
        + jnp.dot(act_low, wdown_full, preferred_element_type=jnp.float32)
        + bdown_full.astype(jnp.float32)
    )
    mixed = result.astype(jnp.bfloat16).reshape(seq_local, tok_seq, width)
    back_weights = (
        lax.all_gather(shards[0], ("batch", "seq"), axis=0, tiled=True),
        lax.all_gather(shards[1], ("batch", "seq"), axis=0, tiled=True),
        lax.all_gather(shards[2], ("batch", "seq"), axis=0, tiled=True),
        lax.all_gather(shards[3], ("batch", "seq"), axis=0, tiled=True),
        lax.all_gather(shards[4], ("batch", "seq"), axis=0, tiled=True),
        lax.all_gather(shards[5], ("batch", "seq"), axis=0, tiled=True),
        lax.all_gather(shards[6], ("batch", "seq"), axis=0, tiled=True),
        lax.all_gather(shards[7], ("batch", "seq"), axis=0, tiled=True),
    )
    wqkv_back, wout_back, wup_back, wdown_back, gattn_back, gffn_back, bup_back, bdown_back = (
        back_weights
    )
    grad_low = cotangent.reshape(row_count, width)
    grad_float = grad_low.astype(jnp.float32)
    grad_down = jnp.einsum("rf,rd->fd", act_low, grad_low, preferred_element_type=jnp.float32)
    grad_bias_down = jnp.sum(grad_float, axis=0)
    grad_act = jnp.einsum("rd,fd->rf", grad_low, wdown_back, preferred_element_type=jnp.float32)
    sigma = jax.nn.sigmoid(up_projected_value)
    grad_upv = (grad_act * sigma * (1.0 + up_projected_value * (1.0 - sigma))).astype(jnp.bfloat16)
    grad_up = jnp.einsum(
        "rd,rf->df", feedforward_normed_input, grad_upv, preferred_element_type=jnp.float32
    )
    grad_bias_up = jnp.sum(grad_upv.astype(jnp.float32), axis=0)
    grad_hn_ffn = jnp.einsum("rf,df->rd", grad_upv, wup_back, preferred_element_type=jnp.float32)
    grad_norm_ffn, grad_gain_ffn = norm_back(grad_hn_ffn, middle, inv_ffn, gffn_back)
    grad_middle = grad_float + grad_norm_ffn
    grad_attn = grad_middle.astype(jnp.bfloat16)
    grad_out = jnp.einsum("rd,re->de", att_low, grad_attn, preferred_element_type=jnp.float32)
    block_summed = (
        lax.psum_scatter(grad_out, ("batch", "seq"), scatter_dimension=0, tiled=True),
        lax.psum_scatter(grad_up, ("batch", "seq"), scatter_dimension=0, tiled=True),
        lax.psum_scatter(grad_down, ("batch", "seq"), scatter_dimension=0, tiled=True),
        lax.psum_scatter(grad_gain_ffn, ("batch", "seq"), scatter_dimension=0, tiled=True),
        lax.psum_scatter(grad_bias_up, ("batch", "seq"), scatter_dimension=0, tiled=True),
        lax.psum_scatter(grad_bias_down, ("batch", "seq"), scatter_dimension=0, tiled=True),
    )
    grad_att_low = jnp.einsum(
        "re,de->rd", grad_attn, wout_back, preferred_element_type=jnp.float32
    ).astype(jnp.bfloat16)
    grad_heads = grad_att_low.reshape(seq_local, tok_seq, H, HD)
    delta = jnp.sum(
        (grad_att_low.astype(jnp.float32) * attention_output).reshape(seq_local, tok_seq, H, HD),
        axis=3,
    )
    delta = jnp.transpose(delta, (0, 2, 1))[..., None]
    query_init = jnp.zeros((seq_local, tok_seq, H, HD), jnp.float32)

    def grad_step(block, carry):
        grad_query, term = carry
        scores = block_scores(block)
        probs = jnp.exp(scores - log_sum)
        keys_blk = key_block(keys_all, block)
        values_blk = key_block(values_all, block)
        grad_probs = jnp.einsum(
            "sqhd,skhd->shqk", grad_heads, values_blk, preferred_element_type=jnp.float32
        )
        grad_scores = (probs * (grad_probs - delta)).astype(jnp.bfloat16)
        grad_values = jnp.einsum(
            "shqk,sqhd->skhd",
            probs.astype(jnp.bfloat16),
            grad_heads,
            preferred_element_type=jnp.float32,
        )
        grad_keys = jnp.einsum(
            "shqk,sqhd->skhd", grad_scores, queries_h, preferred_element_type=jnp.float32
        )
        grad_query = grad_query + jnp.einsum(
            "shqk,skhd->sqhd", grad_scores, keys_blk, preferred_element_type=jnp.float32
        )
        piece = jnp.concatenate(
            [
                grad_keys.reshape(seq_local, tok_seq, width),
                grad_values.reshape(seq_local, tok_seq, width),
            ],
            axis=2,
        )
        term = lax.dynamic_update_slice_in_dim(term, piece, block * tok_seq, 1)
        return (grad_query, term)

    term_init = jnp.zeros((seq_local, tok_seq * block_total, 2 * width), jnp.float32)
    grad_query, term = lax.fori_loop(0, block_total, grad_step, (query_init, term_init))
    kv_grads = lax.psum_scatter(
        term.astype(jnp.bfloat16), "seq", scatter_dimension=1, tiled=True
    ).astype(jnp.float32)
    grad_scaled = grad_query.reshape(row_count, width)
    scale_local = jnp.sum((grad_scaled * q_raw).reshape(row_count, H, HD), axis=(0, 1))
    scale_total = lax.psum(scale_local, ("batch", "seq"))
    grad_scale = scale_total * (soft_unit / math.sqrt(HD)) * jax.nn.sigmoid(scale_float)
    grad_qkv_low = jnp.concatenate(
        [grad_scaled * factor_row, kv_grads.reshape(row_count, 2 * width)], axis=1
    ).astype(jnp.bfloat16)
    grad_qkv = jnp.einsum(
        "rd,re->de", attention_normed_input, grad_qkv_low, preferred_element_type=jnp.float32
    )
    grad_hn_attn = jnp.einsum(
        "re,de->rd", grad_qkv_low, wqkv_back, preferred_element_type=jnp.float32
    )
    grad_norm_attn, grad_gain_attn = norm_back(grad_hn_attn, inputs, inv_attn, gattn_back)
    grad_tokens = (grad_middle + grad_norm_attn).reshape(seq_local, tok_seq, width)
    qkv_summed = (
        lax.psum_scatter(grad_qkv, ("batch", "seq"), scatter_dimension=0, tiled=True),
        lax.psum_scatter(grad_gain_attn, ("batch", "seq"), scatter_dimension=0, tiled=True),
    )
    return (
        mixed,
        grad_tokens,
        qkv_summed[0],
        block_summed[0],
        block_summed[1],
        block_summed[2],
        qkv_summed[1],
        block_summed[3],
        block_summed[4],
        block_summed[5],
        grad_scale,
    )


MESH = pl.DeviceIdType.MESH
F32 = jnp.float32
BF16 = jnp.bfloat16


def fits_fused(nb, ns, tokens, wqkv, wup):
    rows, width = wup.shape[0], wup.shape[1]
    return (
        ns == 4
        and nb % 2 == 0
        and tokens.shape == (1, 128, H * HD)
        and width == H * HD
        and 2 * rows == HD
        and nb * ns * rows == width
        and wqkv.shape == (rows, 3 * width)
    )


def nt(a, b):
    return lax.dot_general(a, b, (((1,), (1,)), ((), ())), preferred_element_type=F32)


def nn(a, b):
    return lax.dot_general(a, b, (((1,), (0,)), ((), ())), preferred_element_type=F32)


def tn(a, b):
    return lax.dot_general(a, b, (((0,), (0,)), ((), ())), preferred_element_type=F32)


def layer_kernel(nz, scratch_names, tok, cot, wqkv, wout, wup, wdown, ga, gf, bu, bd, scl, *refs):
    mixed_o, gtok_o, o1, o2, sg_o = refs[:5]
    r = types.SimpleNamespace(**dict(zip(scratch_names, refs[5:])))
    D = tok.shape[1]
    T = tok.shape[0]
    L = 4 * T
    HP = 2 * T
    NH = 4
    HW = NH * HD
    CB = HD
    RW = HD // 2
    LO = 256
    b = lax.axis_index("batch")
    s = lax.axis_index("seq")
    z, y = b // 2, b % 2
    x, c = s // 2, s % 2
    sib = (b, 2 * x + (1 - c))
    xp = (b, 2 * (1 - x) + c)
    yp = (2 * z + (1 - y), s)
    zup = (lax.rem(2 * (z + 1), 2 * nz) + y, s)
    zdn = (lax.rem(2 * (z + nz - 1), 2 * nz) + y, s)
    drains = []

    def when(cond, fn):
        if cond is None:
            fn()
        else:
            pl.when(cond)(fn)

    def both(p, q):
        if p is None:
            return q
        if q is None:
            return p
        return jnp.logical_and(p, q)

    def copy(src, dst, ssem, rsem, dev):
        return pltpu.make_async_remote_copy(
            src_ref=src, dst_ref=dst, send_sem=ssem, recv_sem=rsem, device_id=dev, device_id_type=MESH
        )

    def send(make, cond=None):
        when(cond, lambda: make().start())
        drains.append((make, cond))

    def arrive(make, cond=None):
        when(cond, lambda: make().wait_recv())

    bar = pltpu.get_barrier_semaphore()
    peers = [sib, xp, yp]
    for k in range(1, nz):
        peers.append((2 * lax.rem(z + k, nz) + y, s))
    for dev in peers:
        pl.semaphore_signal(bar, inc=1, device_id=dev, device_id_type=MESH)
    fetches = [
        pltpu.make_async_copy(src, dst, r.s_in.at[k])
        for k, (src, dst) in enumerate(
            (
                (wqkv, r.WQ),
                (wup, r.WU),
                (wout, r.WO),
                (wdown, r.WD),
                (tok, r.X.at[s]),
                (cot, r.DY.at[s]),
                (ga, r.V0),
                (gf, r.V1),
                (bu, r.V2),
                (bd, r.V3),
                (scl, r.V4),
            )
        )
    ]
    for f in fetches:
        f.start()
    r.SM[...] = jnp.zeros_like(r.SM)
    for k in range(6, 11):
        fetches[k].wait()
    small_rows = [v[...].astype(F32).reshape(1, RW) for v in (r.V0, r.V1, r.V2, r.V3)]
    for k, row in enumerate(small_rows):
        r.SM[k : k + 1, 0:RW] = row
    fetches[0].wait()
    fetches[1].wait()

    def pieces(cc):
        for xx in range(2):
            for t in range(4):
                for j in range(NH):
                    src = HD * (4 * j + 2 * cc + xx)
                    v = r.WU[:, src : src + HD] if t == 0 else r.WQ[:, D * (t - 1) + src : D * (t - 1) + src + HD]
                    r.W1P[cc, xx, 0:RW, HW * t + HD * j : HW * t + HD * (j + 1)] = v

    pieces(0)
    pieces(1)
    pl.semaphore_wait(bar, len(peers))

    m_sib1 = lambda: copy(r.W1P.at[1 - c], r.SIB1, r.s_one.at[0], r.r_one.at[0], sib)
    m_ssib = lambda: copy(r.SM, r.S.at[b, s], r.s_one.at[1], r.r_one.at[1], sib)
    m_sib2 = lambda: copy(r.W2P, r.SIB2, r.s_one.at[2], r.r_one.at[2], sib)
    send(m_ssib)
    send(m_sib1)
    fetches[2].wait()
    fetches[3].wait()
    r.W2P[0:RW, 0:D] = r.WO[...]
    r.W2P[0:RW, D : 2 * D] = r.WD[...]
    send(m_sib2)
    r.S[b, s] = r.SM[...]

    def chip_rows(own, other):
        own, other = own[:RW].astype(F32), other[:RW].astype(F32)
        lo = jnp.where(c == 0, own, other)
        hi = jnp.where(c == 0, other, own)
        return jnp.concatenate([lo, hi], axis=0).astype(BF16)

    m_ssib_r = lambda: copy(r.SM, r.S.at[b, 2 * x + (1 - c)], r.s_one.at[1], r.r_one.at[1], sib)
    arrive(m_ssib_r)
    m_xs = lambda: copy(
        r.S.at[b, pl.ds(2 * x, 2)], r.S.at[b, pl.ds(2 * x, 2)], r.s_one.at[4], r.r_one.at[4], xp
    )
    send(m_xs)
    arrive(m_sib1)
    r.CB1[...] = chip_rows(r.W1P[c, 1 - x], r.SIB1[1 - x])
    half = (D - LO) // 2
    cuts = (pl.ds(LO, half), pl.ds(LO + half, half), pl.ds(0, LO))

    def m_x1(k, xx):
        return copy(r.CB1.at[:, cuts[k]], r.W1.at[b, xx, :, cuts[k]], r.s_x1.at[k], r.r_x1.at[k], xp)

    for k in range(3):
        send(lambda k=k: m_x1(k, x))
    r.W1[b, x] = chip_rows(r.W1P[c, x], r.SIB1[x])

    def gather_item(idx, block, zcond, passes_y=True):
        up = lambda zz: copy(block(zz, y), block(zz, y), r.s_up.at[idx, zz], r.r_up.at[idx, zz], zup)
        dn = lambda zz: copy(block(zz, y), block(zz, y), r.s_dn.at[idx, zz], r.r_dn.at[idx, zz], zdn)
        yy = lambda zz: copy(block(zz, y), block(zz, y), r.s_y.at[idx, zz], r.r_y.at[idx, zz], yp)

        def start():
            send(lambda: up(z), both(zcond, z < nz - 1))
            send(lambda: dn(z), both(zcond, z > 0))
            if passes_y:
                send(lambda: yy(z), zcond)

        def step(d):
            lo, hi = z - d, z + d
            below, above = both(zcond, lo >= 0), both(zcond, hi < nz)
            arrive(lambda: up(lo), below)
            send(lambda: up(lo), both(below, z < nz - 1))
            arrive(lambda: dn(hi), above)
            send(lambda: dn(hi), both(above, z > 0))
            if passes_y:
                send(lambda: yy(lo), below)
                send(lambda: yy(hi), above)

        def finish():
            if passes_y:
                for k in range(nz):
                    when(
                        None if zcond is None else jnp.logical_not(zcond),
                        lambda k=k: copy(
                            block(k, 1 - y), block(k, 1 - y), r.s_y.at[idx, k], r.r_y.at[idx, k], yp
                        ).wait_recv(),
                    )

        return start, step, finish

    mine = c == y
    not_mine = c != y
    g_s = gather_item(0, lambda zz, q: r.S.at[2 * zz + q], None)
    g_own = [gather_item(1 + k, lambda zz, q, k=k: r.W1.at[2 * zz + q, x, :, cuts[k]], None) for k in range(2)]
    g_oth = [
        gather_item(3 + k, lambda zz, q, k=k: r.W1.at[2 * zz + q, 1 - x, :, cuts[k]], None) for k in range(2)
    ]
    g_out = gather_item(5, lambda zz, q: r.W2.at[zz, :, pl.ds(0, D)], None, False)
    g_up = gather_item(6, lambda zz, q: r.W1.at[2 * zz + q, :, :, pl.ds(0, LO)], None)
    g_dn = gather_item(7, lambda zz, q: r.W2.at[zz, :, pl.ds(D, D)], mine)

    g_own[0][0]()
    g_own[1][0]()
    m_xs_r = lambda: copy(
        r.S.at[b, pl.ds(2 - 2 * x, 2)],
        r.S.at[b, pl.ds(2 - 2 * x, 2)],
        r.s_one.at[4],
        r.r_one.at[4],
        xp,
    )
    arrive(m_xs_r)
    g_s[0]()
    fetches[4].wait()
    fetches[5].wait()
    own_tok, own_cot = r.X.at[s], r.DY.at[s]
    m_xt = lambda: copy(own_tok, own_tok, r.s_one.at[5], r.r_one.at[5], xp)
    m_st = lambda: copy(own_tok, own_tok, r.s_one.at[6], r.r_one.at[6], sib)
    m_xc = lambda: copy(own_cot, own_cot, r.s_one.at[7], r.r_one.at[7], xp)
    m_sc = lambda: copy(own_cot, own_cot, r.s_one.at[8], r.r_one.at[8], sib)
    send(m_xt)
    send(m_st)
    send(m_xc)
    send(m_sc)
    arrive(m_sib2)

    def fill_w2():
        r.W2[z] = chip_rows(r.W2P[...], r.SIB2[...])

    when(mine, fill_w2)
    m_y2 = lambda: copy(
        r.W2.at[z, :, pl.ds(0, D)], r.W2.at[z, :, pl.ds(0, D)], r.s_one.at[14], r.r_one.at[14], yp
    )
    sx = 2 * (1 - x) + c
    so = 2 * (1 - x) + (1 - c)
    ss = 2 * x + (1 - c)
    fwd = lambda name, k, src_i: copy(
        name.at[src_i], name.at[src_i], r.s_one.at[k], r.r_one.at[k], sib
    )
    arrive(lambda: m_x1(0, 1 - x))
    g_oth[0][0]()
    g_own[0][1](1)
    arrive(lambda: m_x1(1, 1 - x))
    g_oth[1][0]()
    send(m_y2, mine)
    g_own[1][1](1)
    g_s[1](1)
    arrive(lambda: m_x1(2, 1 - x))
    g_oth[0][1](1)
    g_oth[1][1](1)
    g_own[0][1](2)
    g_own[1][1](2)
    g_s[1](2)
    arrive(lambda: copy(own_tok, r.X.at[sx], r.s_one.at[5], r.r_one.at[5], xp))
    send(lambda: fwd(r.X, 9, sx))
    g_oth[0][1](2)
    arrive(m_y2, not_mine)
    g_out[0]()
    g_oth[1][1](2)
    for d in range(3, nz):
        g_own[0][1](d)
        g_own[1][1](d)
        g_s[1](d)
        g_oth[0][1](d)
        g_oth[1][1](d)
    arrive(lambda: copy(own_tok, r.X.at[ss], r.s_one.at[6], r.r_one.at[6], sib))
    arrive(lambda: fwd(r.X, 9, so))
    arrive(lambda: copy(own_cot, r.DY.at[sx], r.s_one.at[7], r.r_one.at[7], xp))
    send(lambda: fwd(r.DY, 10, sx))
    arrive(lambda: copy(own_cot, r.DY.at[ss], r.s_one.at[8], r.r_one.at[8], sib))
    g_out[1](1)
    g_s[2]()
    arrive(lambda: fwd(r.DY, 10, so))

    jf = lax.broadcasted_iota(jnp.int32, (1, D), 1).astype(F32)
    jk = jnp.floor((jf + 0.5) / RW)
    jl = jf - RW * jk
    pick = (lax.broadcasted_iota(jnp.int32, (128, D), 0).astype(F32) == jl).astype(BF16)
    sm_rows = 2 * nz * 4
    spread = nn(r.S[...].reshape(sm_rows * 8, 128).astype(BF16), pick)
    spread = spread.reshape(sm_rows, 8, D)
    owner = lax.broadcasted_iota(jnp.int32, (sm_rows, 8, D), 0).astype(F32)
    r.ROWS[...] = jnp.sum(jnp.where(owner == jk[None], spread, 0.0), axis=0)
    uf = jf[:, :HW]
    uj = jnp.floor((uf + 0.5) / HD)
    uh = jnp.floor((uf - HD * uj + 0.5) / RW)
    base = (2 * c + x).astype(F32)
    uk = 2.0 * (4.0 * uj + base) + uh
    r.BUP[...] = jnp.sum(
        jnp.where(owner[:, :, :HW] == uk[None], spread[:, :, :HW], 0.0), axis=0
    )
    gain_attn = r.ROWS[0:1]
    gain_ffn = r.ROWS[1:2]
    bias_down = r.ROWS[3:4]
    bias_up = r.BUP[2:3]
    scale = r.V4[...].astype(F32).reshape(1, HD)
    factor = soft_unit / math.sqrt(HD) * (
        jnp.maximum(scale, 0.0) + jnp.log(1.0 + jnp.exp(-jnp.abs(scale)))
    )

    for k in range(4):
        xv = r.X[k].astype(F32)
        inv = lax.rsqrt(jnp.mean(xv * xv, axis=1, keepdims=True) + epsilon)
        hn = xv * inv * gain_attn
        r.HN1[pl.ds(k * T, T)] = hn.astype(BF16)
        r.HN1T[:, :, pl.ds(k * T, T)] = hn.T.astype(BF16).reshape(2 * nz, 2 * CB, T)
    g_out[1](2)
    g_up[0]()
    g_dn[0]()
    for g in (*g_own, *g_oth):
        g[2]()

    W1 = r.W1
    W2 = r.W2
    for h in range(2):
        wq = W1[:, :, :, pl.ds(LO + 512 * h, 512)].reshape(D, 512)
        r.QKV[:, pl.ds(512 * h, 512)] = nn(r.HN1[...], wq)
    off = HW - LO
    for j in range(NH):
        q = r.QKV[:, off + HD * j : off + HD * (j + 1)]
        k = r.QKV[:, off + HW + HD * j : off + HW + HD * (j + 1)]
        v = r.QKV[:, off + 2 * HW + HD * j : off + 2 * HW + HD * (j + 1)]
        r.QRAW[j] = q
        r.QH[j] = (q * factor).astype(BF16)
        r.KH[j] = k.astype(BF16)
        r.VH[j] = v.astype(BF16)
        r.KT[j] = k.T.astype(BF16)
        r.VT[j] = v.T.astype(BF16)
    tri_k = lax.broadcasted_iota(jnp.int32, (HP, HP), 0)
    tri_q = lax.broadcasted_iota(jnp.int32, (HP, HP), 1)
    seen = tri_k <= tri_q

    def rows_of(p):
        return pl.ds(p * HP, HP)

    def attend(p, j):
        q = r.QH[j, rows_of(p)]
        diag = jnp.where(seen, nt(r.KH[j, rows_of(p)], q), neg_large)
        top = jnp.max(diag, axis=0, keepdims=True)
        if p:
            full = nt(r.KH[j, pl.ds(0, HP)], q)
            top = jnp.maximum(top, jnp.max(full, axis=0, keepdims=True))
            full = jnp.exp(full - top)
        diag = jnp.exp(diag - top)
        total = jnp.sum(diag, axis=0, keepdims=True)
        if p:
            total = total + jnp.sum(full, axis=0, keepdims=True)
        inv = 1.0 / total
        diag = (diag * inv).astype(BF16)
        if p:
            r.PT1[j, pl.ds(0, HP)] = (full * inv).astype(BF16)
            r.PT1[j, pl.ds(HP, HP)] = diag
            ot = nn(r.VT[j], r.PT1[j])
        else:
            r.PT0[j] = diag
            ot = nn(r.VT[j, :, pl.ds(0, HP)], diag)
        r.OT[j, :, rows_of(p)] = ot
        r.OB[rows_of(p), HD * j : HD * (j + 1)] = ot.T.astype(BF16)

    def to_sibling(st, p, value):
        r.PF[p] = value.reshape(2, T, D)
        r.ES[st, p] = r.PF[p, 1 - c].astype(BF16)
        send(lambda: copy(r.ES.at[st, p], r.ER.at[st, p], r.s_e.at[st, p], r.r_e.at[st, p], sib))

    def chip_sum(st, p):
        arrive(lambda: copy(r.ES.at[st, p], r.ER.at[st, p], r.s_e.at[st, p], r.r_e.at[st, p], sib))
        return r.PF[p, c] + r.ER[st, p].astype(F32)

    def xslot(st, p):
        return 2 * st + p if st < 2 else st + 2

    def xcopy(st, p):
        i = xslot(st, p)
        return copy(r.XS.at[i], r.XR.at[i], r.s_x.at[i], r.r_x.at[i], xp)

    def to_x(st, p):
        r.XS[xslot(st, p)] = chip_sum(st, p).astype(BF16)
        send(lambda: xcopy(st, p))

    def pair_sum(st, p):
        arrive(lambda: xcopy(st, p))
        return r.XS[xslot(st, p)].astype(F32) + r.XR[xslot(st, p)].astype(F32)

    def share(name, st, p):
        mk = lambda i: copy(name.at[i], name.at[i], r.s_h.at[st, p], r.r_h.at[st, p], sib)
        send(lambda: mk(2 * p + c))
        return lambda: arrive(lambda: mk(2 * p + (1 - c)))

    def out_proj(p):
        to_sibling(0, p, nn(r.OB[rows_of(p)], W2[:, :, pl.ds(0, D)].reshape(HW, D)))

    for j in range(NH):
        attend(0, j)
    for d in range(3, nz):
        g_out[1](d)
    out_proj(0)
    attend(1, 0)
    attend(1, 1)
    to_x(0, 0)
    g_up[1](1)
    g_dn[1](1)
    attend(1, 2)
    attend(1, 3)
    out_proj(1)
    to_x(0, 1)
    for d in range(2, nz):
        g_up[1](d)
        g_dn[1](d)

    r.SGA[...] = jnp.zeros_like(r.SGA)

    def middle(p):
        mid = r.X[2 * p + c].astype(F32) + pair_sum(0, p)
        r.MID[p] = mid
        inv = lax.rsqrt(jnp.mean(mid * mid, axis=1, keepdims=True) + epsilon)
        r.HN2[2 * p + c] = (mid * inv * gain_ffn).astype(BF16)
        return share(r.HN2, 0, p)

    def w_up():
        return W1[:, :, :, pl.ds(0, HW)].reshape(D, HW)

    def feed(p):
        hn = r.HN2[pl.ds(2 * p, 2)].reshape(HP, D)
        u = nn(hn, w_up()) + bias_up
        sig = 1.0 / (1.0 + jnp.exp(-u))
        r.ACT[rows_of(p)] = (u * sig).astype(BF16)
        dy = r.DY[pl.ds(2 * p, 2)].reshape(HP, D)
        dact = nt(dy, W2[:, :, pl.ds(D, D)].reshape(HW, D))
        dup = (dact * sig * (1.0 + u * (1.0 - sig))).astype(BF16)
        r.DUP[rows_of(p), 0:HW] = dup
        to_sibling(1, p, nt(dup, w_up()))
        row = pl.ds(4 + s, 1)
        r.SGA[row, 0:HW] = r.SGA[row, 0:HW] + jnp.sum(dup.astype(F32), axis=0, keepdims=True)

    def transpose_hn2(p):
        for k in range(2):
            t = r.HN2[2 * p + k].astype(F32).T.astype(BF16)
            r.HN2T[:, :, pl.ds((2 * p + k) * T, T)] = t.reshape(2 * nz, 2 * CB, T)

    r.DUP[:, 256:384] = jnp.zeros((L, 128), BF16)
    r.DQ[:, 0:128] = jnp.zeros((L, 128), BF16)
    wait_hn = middle(0)
    g_up[2]()
    g_dn[2]()
    wait_hn()
    feed(0)
    transpose_hn2(0)
    wait_hn = middle(1)
    to_x(1, 0)
    wait_hn()
    feed(1)
    transpose_hn2(1)

    def scatter_item(idx, part, yr, zu, zd, zcond, y_first=True):
        yc = lambda zz: copy(part(zz, 1 - y), yr(zz), r.s_ry.at[idx, zz], r.r_ry.at[idx, zz], yp)
        up = lambda zz: copy(part(zz, y), zu(zz), r.s_ru.at[idx, zz], r.r_ru.at[idx, zz], zup)
        dn = lambda zz: copy(part(zz, y), zd(zz), r.s_rd.at[idx, zz], r.r_rd.at[idx, zz], zdn)

        def add(zz, other):
            part(zz, y)[...] = (part(zz, y)[...].astype(F32) + other(zz)[...].astype(F32)).astype(BF16)

        ycond = None if zcond is None else jnp.logical_not(zcond)

        def start(d):
            if d:
                send(lambda: yc(z + d), both(z + d < nz, ycond))
                send(lambda: yc(z - d), both(z - d >= 0, ycond))
            else:
                send(lambda: yc(z), ycond)

        def step(d):
            if d:
                ok = both(zcond, z + d < nz)
                from_below = both(ok, z > 0)
                if y_first:
                    arrive(lambda: yc(z + d), ok)
                    when(ok, lambda: add(z + d, yr))
                arrive(lambda: up(z + d), from_below)
                when(from_below, lambda: add(z + d, zu))
                send(lambda: up(z + d), ok)
                ok2 = both(zcond, z - d >= 0)
                from_above = both(ok2, z < nz - 1)
                if y_first:
                    arrive(lambda: yc(z - d), ok2)
                    when(ok2, lambda: add(z - d, yr))
                arrive(lambda: dn(z - d), from_above)
                when(from_above, lambda: add(z - d, zd))
                send(lambda: dn(z - d), ok2)
            else:
                below, above = both(zcond, z > 0), both(zcond, z < nz - 1)
                arrive(lambda: up(z), below)
                when(below, lambda: add(z, zu))
                arrive(lambda: dn(z), above)
                when(above, lambda: add(z, zd))
                if y_first:
                    arrive(lambda: yc(z), zcond)
                    when(zcond, lambda: add(z, yr))

        return start, step

    far = range(nz - 1, 0, -1)
    cut_up = pl.ds(0, LO)
    s_up = scatter_item(
        0,
        lambda zz, q: r.G1.at[2 * zz + q, :, :, cut_up],
        lambda zz: r.YR1.at[zz, :, :, cut_up],
        lambda zz: r.ZU1.at[zz - 1, :, :, cut_up],
        lambda zz: r.ZD1.at[zz, :, :, cut_up],
        None,
    )

    def qkv_item(idx, xx, cut):
        return scatter_item(
            idx,
            lambda zz, q: r.G1.at[2 * zz + q, xx, :, cut],
            lambda zz: r.YR1.at[zz, xx, :, cut],
            lambda zz: r.ZU1.at[zz - 1, xx, :, cut],
            lambda zz: r.ZD1.at[zz, xx, :, cut],
            None,
        )

    def together(items):
        def start(d):
            for it in items:
                it[0](d)

        def step(d):
            for it in items:
                it[1](d)

        return start, step

    def w2_item(idx, lo, width, zcond, y_first):
        cut = pl.ds(lo, width)
        return scatter_item(
            idx,
            lambda zz, q: r.G2.at[zz, :, cut],
            lambda zz: r.YR2.at[zz, :, cut],
            lambda zz: r.ZU2.at[zz - 1, :, cut],
            lambda zz: r.ZD2.at[zz, :, cut],
            zcond,
            y_first,
        )

    s_dn = w2_item(1, D, D, None, False)
    WZ = 2 * D // 5
    s_out = w2_item(2, 0, WZ, None, False)
    s_out2 = w2_item(5, WZ, D - WZ, mine, True) if WZ < D else ((lambda d: None), (lambda d: None))
    fars = [qkv_item(3, 1 - x, cuts[0]), qkv_item(6, 1 - x, cuts[1])]
    owns = [qkv_item(4, x, cuts[0]), qkv_item(7, x, cuts[1])]
    s_far, s_own = together(fars), together(owns)

    gu = nn(r.HN2T[...].reshape(D, L), r.DUP[...])
    r.G1[:, :, :, 0:384] = gu.astype(BF16).reshape(2 * nz, 2, CB, 384)
    for d in (*far, 0):
        s_up[0](d)
    to_x(1, 1)
    dy_all = r.DY[...].reshape(L, D)
    r.G2[:, :, pl.ds(D, D)] = tn(r.ACT[...], dy_all).astype(BF16).reshape(nz, CB, D)
    if nz > 3:
        s_dn[1](3)

    def back_middle(p):
        dh = pair_sum(1, p)
        mid = r.MID[p]
        inv = lax.rsqrt(jnp.mean(mid * mid, axis=1, keepdims=True) + epsilon)
        n = mid * inv
        dn = dh * gain_ffn
        dmid = r.DY[2 * p + c].astype(F32) + inv * (
            dn - n * jnp.mean(dn * n, axis=1, keepdims=True)
        )
        r.DMID[p] = dmid
        r.DA[2 * p + c] = dmid.astype(BF16)
        own = jnp.where(x == p, jnp.sum(dh * n, axis=0, keepdims=True), 0.0)
        r.SGA[1:2] = r.SGA[1:2] + own
        return share(r.DA, 1, p)

    def back_out(p):
        da = r.DA[pl.ds(2 * p, 2)].reshape(HP, D)
        r.QKV[0:HP, 0:HW] = nt(da, W2[:, :, pl.ds(0, D)].reshape(HW, D))

    def back_attend(p, j):
        do = r.QKV[0:HP, HD * j : HD * (j + 1)].astype(BF16)
        dof = do.astype(F32)
        delta = jnp.sum(dof.T * r.OT[j, :, rows_of(p)], axis=0, keepdims=True)
        span = HP * (p + 1)
        pt = r.PT1[j] if p else r.PT0[j]
        dpt = nt(r.VH[j, pl.ds(0, span)], do)
        dst = (pt.astype(F32) * (dpt - delta)).astype(BF16)
        dv = nn(pt, do)
        dk = nn(dst, r.QH[j, rows_of(p)])
        dq = nn(r.KT[j, :, pl.ds(0, span)], dst).T
        raw = r.QRAW[j, rows_of(p)]
        r.SGA[3:4, 0:HD] = r.SGA[3:4, 0:HD] + jnp.sum(dq * raw, axis=0, keepdims=True)
        r.DQ[rows_of(p), off + HD * j : off + HD * (j + 1)] = (dq * factor).astype(BF16)
        ko, vo = off + HW + HD * j, off + 2 * HW + HD * j
        if p == 0:
            r.DKA[j] = dk
            r.DVA[j] = dv
        else:
            r.DQ[0:HP, ko : ko + HD] = (dk[:HP] + r.DKA[j]).astype(BF16)
            r.DQ[HP:L, ko : ko + HD] = dk[HP:].astype(BF16)
            r.DQ[0:HP, vo : vo + HD] = (dv[:HP] + r.DVA[j]).astype(BF16)
            r.DQ[HP:L, vo : vo + HD] = dv[HP:].astype(BF16)

    def down_proj(p):
        to_sibling(2, p, nn(r.ACT[rows_of(p)], W2[:, :, pl.ds(D, D)].reshape(HW, D)))

    wait_da = back_middle(0)
    down_proj(0)
    down_proj(1)
    if nz > 3:
        s_up[1](3)
    wait_da()
    back_out(0)
    for j in range(NH):
        back_attend(0, j)
    if nz > 2:
        s_up[1](2)
        s_dn[1](2)
    wait_da = back_middle(1)
    r.XS[4] = chip_sum(2, 1 - x).astype(BF16)
    send(lambda: xcopy(2, 0))
    r.PF2[...] = chip_sum(2, x)
    s_up[1](1)
    wait_da()
    back_out(1)
    da_all = r.DA[...].reshape(L, D)
    r.G2[:, :, pl.ds(0, D)] = tn(r.OB[...], da_all).astype(BF16).reshape(nz, CB, D)
    if nz > 3:
        s_out[1](3)
    for d in (*far, 0):
        s_out2[0](d)
    for j in range(NH):
        back_attend(1, j)
    s_dn[1](1)

    def qkv_block(bb):
        t = nn(r.HN1T[bb], r.DQ[...]).reshape(2, CB, D - LO)
        head = t[:, :, 0:128] + r.G1[bb, :, :, pl.ds(LO, 128)].astype(F32)
        r.G1[bb, :, :, pl.ds(LO, 128)] = head.astype(BF16)
        r.G1[bb, :, :, pl.ds(384, D - 384)] = t[:, :, 128:].astype(BF16)

    for d in far:
        pl.when(z + d < nz)(lambda: qkv_block(2 * (z + d) + (1 - y)))
        pl.when(z - d >= 0)(lambda: qkv_block(2 * (z - d) + (1 - y)))
        s_far[0](d)
        s_own[0](d)
    qkv_block(2 * z + (1 - y))
    s_far[0](0)
    for k in range(nz):
        qkv_block(2 * k + y)

    for p in range(2):
        w = W1[:, :, :, pl.ds(LO, D - LO)].reshape(D, D - LO)
        to_sibling(3, p, nt(r.DQ[rows_of(p)], w))
    s_up[1](0)
    arrive(lambda: xcopy(2, 0))
    own_out = r.PF2[...] + r.XR[4].astype(F32)
    mixed_o[...] = (r.MID[x] + own_out + bias_down).astype(BF16)
    r.XS[5] = chip_sum(3, 1 - x).astype(BF16)
    send(lambda: xcopy(3, 0))
    r.PF2[...] = chip_sum(3, x)
    s_dn[1](0)
    cut_d = pl.ds(D, D)
    m_gyd = lambda: copy(
        r.G2.at[z, :, cut_d], r.YR2.at[z, :, cut_d], r.s_one.at[16], r.r_one.at[16], yp
    )
    send(m_gyd, not_mine)
    s_own[0](0)
    if nz > 2:
        s_out[1](2)
    if nz > 3:
        s_out2[1](3)
        s_far[1](3)
        s_own[1](3)
    if nz > 2:
        s_far[1](2)
    s_out[1](1)
    if nz > 2:
        s_out2[1](2)
        s_own[1](2)

    arrive(lambda: xcopy(3, 0))
    dh = r.PF2[...] + r.XR[5].astype(F32)
    xv = r.X[s].astype(F32)
    inv = lax.rsqrt(jnp.mean(xv * xv, axis=1, keepdims=True) + epsilon)
    n = xv * inv
    dn = dh * gain_attn
    gtok_o[...] = r.DMID[x] + inv * (dn - n * jnp.mean(dn * n, axis=1, keepdims=True))
    r.SGA[0:1] = jnp.sum(dh * n, axis=0, keepdims=True)
    r.SGA[2:3] = jnp.sum(r.DY[s].astype(F32), axis=0, keepdims=True)

    def small_copy(k, slot, dev):
        return lambda: copy(
            r.SGA if k == 0 else r.SGS.at[k - 1], r.SGR.at[slot], r.s_sg.at[slot], r.r_sg.at[slot], dev
        )

    total = r.SGA[...]
    for k, dev in enumerate((sib, xp, yp)):
        mk = small_copy(k, k, dev)
        send(mk)
        if k == 2:
            s_far[1](1)
            s_own[1](1)
            cut_o = pl.ds(0, WZ)
            s_out[1](0)
            m_gy = lambda: copy(
                r.G2.at[z, :, cut_o], r.YR2.at[z, :, cut_o], r.s_one.at[15], r.r_one.at[15], yp
            )
            send(m_gy, not_mine)
            ends = (pl.ds(0, LO + half), pl.ds(LO + half, half))

            def m_fx(k):
                return copy(
                    r.G1.at[b, 1 - x, :, ends[k]], r.FX.at[:, ends[k]], r.s_fx.at[k], r.r_fx.at[k], xp
                )

            for h in range(2):
                fars[h][1](0)
                send(lambda h=h: m_fx(h))
            s_out2[1](1)
        arrive(mk)
        total = total + r.SGR[k]
        r.SGS[k] = total
    mks = []
    for k in range(1, nz):
        mk = small_copy(3, 2 + k, (2 * lax.rem(z + k, nz) + y, s))
        send(mk)
        mks.append(mk)
    s_out2[1](0)

    def hand_over(k, h, xx, block):
        cut = ends[h]
        done = block.astype(F32)
        r.GF[0, xx, :, cut] = done[:RW]
        r.GF[1, xx, :, cut] = done[RW:]
        mk = lambda: copy(
            r.GF.at[1 - c, xx, :, cut], r.GRV.at[xx, :, cut], r.s_gf.at[k, h], r.r_gf.at[k, h], sib
        )
        send(mk)
        o1[xx, c, :, cut] = r.GF[c, xx, :, cut]

        def take():
            arrive(mk)
            o1[xx, 1 - c, :, cut] = r.GRV[xx, :, cut]

        return take

    takes = []
    for h in range(2):
        arrive(lambda h=h: m_fx(h))
        takes.append(hand_over(0, h, 1 - x, r.FX[:, ends[h]]))
    for h in range(2):
        owns[h][1](0)
        takes.append(hand_over(1, h, x, r.G1[b, x, :, ends[h]]))
    arrive(m_gy, mine)
    arrive(m_gyd, mine)

    def out_from_y():
        for cut in (cut_o, cut_d):
            r.G2[z, :, cut] = (r.G2[z, :, cut].astype(F32) + r.YR2[z, :, cut].astype(F32)).astype(BF16)

    when(mine, out_from_y)
    done2 = r.G2[z].astype(F32)
    r.GF2[0] = done2[:RW]
    r.GF2[1] = done2[RW:]
    m_g2 = lambda: copy(r.GF2.at[1 - c], r.GR2, r.s_one.at[12], r.r_one.at[12], sib)
    send(m_g2, mine)
    for take in takes:
        take()
    for k, mk in enumerate(mks):
        arrive(mk)
        total = total + r.SGR[3 + k]
    sg_o[...] = total
    arrive(m_g2, not_mine)

    def out2_own():
        o2[...] = r.GF2[c]

    def out2_sib():
        o2[...] = r.GR2[...]

    when(mine, out2_own)
    when(not_mine, out2_sib)

    for make, cond in drains:
        when(cond, lambda make=make: make().wait_send())


def fused_layer(nb, ns, tokens, wqkv, wout, wup, wdown, gattn, gffn, bup, bdown, scale_param, cot):
    nz = nb // 2
    rows, D = wout.shape
    T = tokens.shape[1]
    L = ns * T
    V = pltpu.VMEM
    scratch = dict(
        WQ=V((rows, 3 * D), BF16),
        WU=V((rows, D), BF16),
        WO=V((rows, D), BF16),
        WD=V((rows, D), BF16),
        SM=V((8, 128), F32),
        V0=V((rows,), BF16),
        V1=V((rows,), BF16),
        V2=V((rows,), BF16),
        V3=V((rows,), BF16),
        V4=V((HD,), BF16),
        W1P=V((2, 2, 48, D), BF16),
        W2P=V((48, 2 * D), BF16),
        SIB1=V((2, 48, D), BF16),
        SIB2=V((48, 2 * D), BF16),
        CB1=V((HD, D), BF16),
        W1=V((nb, 2, HD, D), BF16),
        W2=V((nz, HD, 2 * D), BF16),
        S=V((nb, 4, 8, 128), F32),
        X=V((4, T, D), BF16),
        DY=V((4, T, D), BF16),
        ROWS=V((8, D), F32),
        BUP=V((8, 4 * HD), F32),
        HN1=V((L, D), BF16),
        HN1T=V((nb, 2 * HD, L), BF16),
        HN2T=V((nb, 2 * HD, L), BF16),
        QKV=V((L, D - 256), F32),
        QRAW=V((4, L, HD), F32),
        QH=V((4, L, HD), BF16),
        KH=V((4, L, HD), BF16),
        VH=V((4, L, HD), BF16),
        KT=V((4, HD, L), BF16),
        VT=V((4, HD, L), BF16),
        PT0=V((4, L // 2, L // 2), BF16),
        PT1=V((4, L, L // 2), BF16),
        OT=V((4, HD, L), F32),
        OB=V((L, 4 * HD), BF16),
        PF=V((2, 2, T, D), F32),
        PF2=V((T, D), F32),
        ES=V((4, 2, T, D), BF16),
        ER=V((4, 2, T, D), BF16),
        XS=V((6, T, D), BF16),
        XR=V((6, T, D), BF16),
        MID=V((2, T, D), F32),
        HN2=V((4, T, D), BF16),
        ACT=V((L, 4 * HD), BF16),
        DUP=V((L, 384), BF16),
        DA=V((4, T, D), BF16),
        DMID=V((2, T, D), F32),
        DQ=V((L, D - 256), BF16),
        DKA=V((4, L // 2, HD), F32),
        DVA=V((4, L // 2, HD), F32),
        G1=V((nb, 2, HD, D), BF16),
        G2=V((nz, HD, 2 * D), BF16),
        YR1=V((nz, 2, HD, D), BF16),
        ZU1=V((nz - 1, 2, HD, D), BF16),
        ZD1=V((nz - 1, 2, HD, D), BF16),
        YR2=V((nz, HD, 2 * D), BF16),
        ZU2=V((nz - 1, HD, 2 * D), BF16),
        ZD2=V((nz - 1, HD, 2 * D), BF16),
        FX=V((HD, D), BF16),
        GF=V((2, 2, rows, D), F32),
        GRV=V((2, rows, D), F32),
        GF2=V((2, rows, 2 * D), F32),
        GR2=V((rows, 2 * D), F32),
        SGA=V((8, D), F32),
        SGS=V((3, 8, D), F32),
        SGR=V((2 + nz, 8, D), F32),
    )
    dma = pltpu.SemaphoreType.DMA
    scratch.update(
        s_in=dma((11,)),
        s_x1=dma((3,)), r_x1=dma((3,)),
        s_gf=dma((2, 2)), r_gf=dma((2, 2)),
        s_fx=dma((2,)), r_fx=dma((2,)),
        s_one=dma((17,)), r_one=dma((17,)),
        s_up=dma((9, nz)), r_up=dma((9, nz)),
        s_dn=dma((9, nz)), r_dn=dma((9, nz)),
        s_y=dma((9, nz)), r_y=dma((9, nz)),
        s_e=dma((4, 2)), r_e=dma((4, 2)),
        s_x=dma((6,)), r_x=dma((6,)),
        s_h=dma((2, 2)), r_h=dma((2, 2)),
        s_ry=dma((8, nz)), r_ry=dma((8, nz)),
        s_ru=dma((8, nz)), r_ru=dma((8, nz)),
        s_rd=dma((8, nz)), r_rd=dma((8, nz)),
        s_sg=dma((2 + nz,)), r_sg=dma((2 + nz,)),
    )
    vmem = pl.BlockSpec(memory_space=pltpu.VMEM)
    hbm = pl.BlockSpec(memory_space=pl.ANY)
    mixed, gtok, o1, o2, sg = pl.pallas_call(
        functools.partial(layer_kernel, nz, tuple(scratch)),
        out_shape=(
            jax.ShapeDtypeStruct((T, D), BF16),
            jax.ShapeDtypeStruct((T, D), F32),
            jax.ShapeDtypeStruct((2, 2, rows, D), F32),
            jax.ShapeDtypeStruct((rows, 2 * D), F32),
            jax.ShapeDtypeStruct((8, D), F32),
        ),
        in_specs=[hbm] * 11,
        out_specs=(vmem,) * 5,
        scratch_shapes=list(scratch.values()),
        compiler_params=pltpu.CompilerParams(
            collective_id=0, has_side_effects=True, vmem_limit_bytes=63 << 20
        ),
        name="decoder_layer",
    )(tokens[0], cot[0], wqkv, wout, wup, wdown, gattn, gffn, bup, bdown, scale_param)
    mixed, gtok, gqkv, gout, gup, gdown, g_attn, g_ffn, g_bup, g_bdown, gscale = pl.pallas_call(
        functools.partial(outputs_kernel, ns),
        out_shape=(
            jax.ShapeDtypeStruct((T, D), BF16),
            jax.ShapeDtypeStruct((T, D), F32),
            jax.ShapeDtypeStruct((rows, 3 * D), F32),
            jax.ShapeDtypeStruct((rows, D), F32),
            jax.ShapeDtypeStruct((rows, D), F32),
            jax.ShapeDtypeStruct((rows, D), F32),
            jax.ShapeDtypeStruct((rows,), F32),
            jax.ShapeDtypeStruct((rows,), F32),
            jax.ShapeDtypeStruct((rows,), F32),
            jax.ShapeDtypeStruct((rows,), F32),
            jax.ShapeDtypeStruct((HD,), F32),
        ),
        in_specs=[vmem] * 6,
        out_specs=(vmem,) * 11,
        compiler_params=pltpu.CompilerParams(vmem_limit_bytes=63 << 20),
        name="place_outputs",
    )(mixed, gtok, o1, o2, sg, scale_param)
    return mixed[None], gtok[None], gqkv, gout, gup, gdown, g_attn, g_ffn, g_bup, g_bdown, gscale


def outputs_kernel(ns, mixed, gtok, o1, o2, sg, scl, mixed_o, gtok_o, gqkv, gout, gup, gdown, *small):
    rows, D = gup.shape
    HW = 4 * HD
    mixed_o[...] = mixed[...]
    gtok_o[...] = gtok[...]
    gout[...] = o2[:, 0:D]
    gdown[...] = o2[:, D : 2 * D]
    for xx in range(2):
        for cc in range(2):
            for t in range(4):
                for j in range(4):
                    v = o1[xx, cc, :, HW * t + HD * j : HW * t + HD * (j + 1)]
                    at = HD * (4 * j + 2 * cc + xx)
                    if t == 0:
                        gup[:, at : at + HD] = v
                    else:
                        gqkv[:, D * (t - 1) + at : D * (t - 1) + at + HD] = v
    first = (lax.axis_index("batch") * ns + lax.axis_index("seq")) * rows
    parts = []
    for h in range(H):
        j, cc, xx = h // 4, (h // 2) % 2, h % 2
        row = 4 + 2 * xx + cc
        parts.append(sg[row : row + 1, HD * j : HD * (j + 1)])
    bias_up = jnp.concatenate(parts, axis=1)
    shift = lax.rem(D - first, D)
    for ref, v in zip(small, (sg[0:1], sg[1:2], bias_up, sg[2:3])):
        v = jnp.broadcast_to(v, (8, D))
        ref[...] = pltpu.roll(v, shift, 1)[0, 0:rows]
    scale = scl[...].astype(F32).reshape(1, HD)
    small[4][...] = (sg[3:4, 0:HD] * (soft_unit / math.sqrt(HD)) / (1.0 + jnp.exp(-scale)))[0]


def layer_step(nb, ns, *args):
    if fits_fused(nb, ns, args[0], args[1], args[3]):
        return fused_layer(nb, ns, *args)
    return generic_layer(*args)


def solution(mesh):
    return jax.shard_map(
        functools.partial(layer_step, mesh.shape["batch"], mesh.shape["seq"]),
        mesh=mesh,
        in_specs=(
            P("batch", "seq", None),
            P(("batch", "seq"), None),
            P(("batch", "seq"), None),
            P(("batch", "seq"), None),
            P(("batch", "seq"), None),
            P(("batch", "seq")),
            P(("batch", "seq")),
            P(("batch", "seq")),
            P(("batch", "seq")),
            P(),
            P("batch", "seq", None),
        ),
        out_specs=(
            P("batch", "seq", None),
            P("batch", "seq", None),
            P(("batch", "seq"), None),
            P(("batch", "seq"), None),
            P(("batch", "seq"), None),
            P(("batch", "seq"), None),
            P(("batch", "seq")),
            P(("batch", "seq")),
            P(("batch", "seq")),
            P(("batch", "seq")),
            P(),
        ),
        check_vma=False,
    )
```
